32 devices in a mesh: row: 4 (over y, core), col: 8 (over z, x).
Axes of the slice: x: 2, y: 2, z: 4, core: 2. Of those that a mesh axis runs over, the one named last changes fastest.
Arguments:
- river_lower: float32 [64, 2, 2, 8192], P('row', None, None, 'col'), may hold values from -1.3 to 0.6, as said below
- river_main: float32 [64, 2, 2, 8192], P('row', None, None, 'col'), may hold values from -0.9 to 2.01
- river_upper: float32 [64, 2, 2, 8192], P('row', None, None, 'col'), may hold values from -1.3 to 0.6
- river_rhs: float32 [64, 2, 8192], P('row', None, 'col'), may hold values from -0.08 to 0.08
- weir_crest: float32 [64, 8192], P('row', 'col'), may hold values from -1 to 1
- weir_regime: int32 [64, 8192], P('row', 'col'), may hold values from 0 to 2
- weir_tile: int32 [4, 8, 16, 1024, 1], P('row', 'col'), may hold values from 0 to 31; in each aligned block of 16384 rows (0 to 16383, 16384 to 32767, ..., all dimensions but the last counted through in order) at most 1024 rows name the same one
- weir_row: int32 [64, 8192], P('row', 'col'), may hold values from 0 to 31
- weir_col: int32 [64, 8192], P('row', 'col'), may hold values from 0 to 511
- bed_level: float32 [128, 4096], P('row', 'col'), may hold values from -1 to 0
- water_depth: float32 [128, 4096], P('row', 'col'), may hold values from 0.02 to 1.5
- flux_first: float32 [128, 4096], P('row', 'col'), may hold values from -2.4 to 2.4
- flux_second: float32 [128, 4096], P('row', 'col'), may hold values from -2.4 to 2.4
- wet_mask: int32 [128, 4096], P('row', 'col'), may hold values 0 or 1
Outputs:
- river_state: float32 [64, 2, 8192], P('row', None, 'col')
- depth_out: float32 [128, 4096], P('row', 'col')
- first_out: float32 [128, 4096], P('row', 'col')
- second_out: float32 [128, 4096], P('row', 'col')
The draws below stay inside these ranges and needn't reach their ends.
Inputs may be any that keep to these rules, and one draw needn't show every extreme that they name: `river_lower`: together with river_main and river_upper, the block matrix of each chain has a positive definite symmetric part. Of the weirs in one device's block weir_tile[r, c], at most 1024 feed the same tile, and in some device's block a tile is fed by exactly 1024.
All inputs are finite; a program needn't handle non-finite values. No bound on the sum of `wet_mask` on one device may be relied on, other than what follows from the above.
Results may differ from the reference program's by a relative error of at most 0.0003.
Values sent between devices are 32-bit elements; how exact they have to be, the bound alone decides.
No kernel may reach another device: no remote copies, remote signals or barrier semaphores. Data moves between devices by JAX's collectives and lax.ppermute only.
A program may use at most 64 MiB of HBM per device.

```python
import math
import jax
import jax.numpy as jnp
import numpy as np
from jax import lax

K = 16
CH = 1024
TX = 32
TY = 512
NS = 64
NC = 8192
NX = 128
NY = 4096
CAP = 1024
N_ROW = 4
N_COL = 8
DEVICES = 32


def river_blocks(key):
    subkeys = jax.random.split(jax.random.fold_in(key, 31), 5)
    edge_diag = jax.random.uniform(subkeys[0], (NS + 1, 2, NC), jnp.float32, 0.6, 1.0)
    edge_cross = jax.random.uniform(subkeys[1], (NS + 1, NC), jnp.float32, -0.3, 0.3)
    skew_edge = jax.random.uniform(subkeys[2], (NS + 1, 2, 2, NC), jnp.float32, -0.3, 0.3)
    skew_self = jax.random.uniform(subkeys[3], (NS, NC), jnp.float32, -0.3, 0.3)
    storage = jnp.exp(jax.random.uniform(subkeys[4], (NS, 2, NC), jnp.float32, jnp.log(0.0005), jnp.log(0.002)))
    conduct = jnp.stack([jnp.stack([edge_diag[:, 0], edge_cross], 1), jnp.stack([edge_cross, edge_diag[:, 1]], 1)], 1)
    lower_blocks = -(conduct[:NS] + skew_edge[:NS])
    upper_blocks = -conduct[1:] + jnp.transpose(skew_edge[1:], (0, 2, 1, 3))
    own_part = jnp.stack([jnp.stack([storage[:, 0], skew_self], 1), jnp.stack([-skew_self, storage[:, 1]], 1)], 1)
    main_blocks = conduct[:NS] + conduct[1:] + own_part
    return (lower_blocks, main_blocks, upper_blocks)


def draw_river_lower(key, part):
    return river_blocks(key)[0]


def draw_river_main(key, part):
    return river_blocks(key)[1]


def draw_river_upper(key, part):
    return river_blocks(key)[2]


def set_ends(drawn, own_key, least, largest):
    dims = drawn.shape
    index_at = [jax.random.randint(jax.random.fold_in(own_key, axis), (), 0, dims[axis]) for axis in range(len(dims))]
    drawn = drawn.at[tuple(index_at)].set(least)
    longest = dims.index(max(dims))
    index_at[longest] = (index_at[longest] + 1) % dims[longest]
    return drawn.at[tuple(index_at)].set(largest)


def block_scale(own_key, extent, cuts, low, largest):
    def one(dim, shards_of):
        draws = jax.random.uniform(jax.random.fold_in(jax.random.fold_in(own_key, 6), dim), (shards_of,), jnp.float32, low / len(cuts), largest / len(cuts))
        return jnp.repeat(jnp.exp(draws), extent[dim] // shards_of).reshape((-1,) + (1,) * (len(extent) - dim - 1))

    gain = one(*cuts[0])
    for cut in cuts[1:]:
        gain = gain * one(*cut)
    return gain


def shared_out(key, own, number, rows, count, top, most, skew):
    sequence = jax.random.permutation(key, count)
    heavy_load, common = load_shares(count, rows * top, most, skew, True), load_shares(count, rows * top, most, skew, False)
    places = jnp.arange(count)

    def named(tallies, offset_by):
        used = int((tallies > 0).sum())
        fixed = max(1, used // 4)
        moved = fixed + (places - fixed + offset_by * (used - fixed)) % max(1, count - fixed)
        return jnp.zeros((count,), jnp.int32).at[sequence[jnp.where(places < fixed, places, moved)]].set(jnp.asarray(tallies, jnp.int32))

    tallies = jnp.where(number % 4 == 0, named(heavy_load, number // 4), named(common, number - number // 4 - 1))
    mixed = jax.random.permutation(jax.random.fold_in(own, 3), count)
    source_of, taker = mixed[0:count // 2 * 2:2], mixed[1:count // 2 * 2:2]
    room = jnp.minimum(tallies[source_of] - 1, most - tallies[taker]) // 2
    room = jnp.where((source_of == sequence[0]) | (taker == sequence[0]) | (tallies[taker] == 0), 0, jnp.maximum(room, 0))
    moved = jax.random.randint(jax.random.fold_in(own, 4), (count // 2,), 0, 1 << 20) % (room + 1)
    tallies = tallies.at[source_of].add(-moved).at[taker].add(moved)
    members = jnp.searchsorted(jnp.cumsum(tallies), jnp.arange(rows * top), side="right").astype(jnp.int32)
    grid = members.reshape(top, rows).T
    grid = grid[jax.random.permutation(jax.random.fold_in(own, 1), rows)]
    offset_by = jax.random.randint(jax.random.fold_in(own, 2), (rows, 1), 0, top)
    return jnp.take_along_axis(grid, (jnp.arange(top)[None, :] + offset_by) % top, axis=1)


def load_shares(count, total, most, slope, full):
    portions = [(1 << 20) // math.isqrt(grade ** slope) + 1 for grade in range(1, count + 1)]
    largest = most if full else min(most, max(-(-total // count), total * portions[0] // sum(portions)))
    least = 1 if total - largest >= count - 1 else 0
    given, spare = [largest] + [least] * (count - 1), total - largest - least * (count - 1)
    while spare > 0:
        free = [i for i in range(1, count) if given[i] < largest] or [i for i in range(1, count) if given[i] < most]
        mass, remaining = sum([portions[i] for i in free]), spare
        for i in free:
            addition = min(most - given[i], max(1, remaining * portions[i] // mass), spare)
            given[i] = given[i] + addition
            spare = spare - addition
    return np.array(given)


def scatter_about(key, extent, deviation, limit, cuts=(), kind=jnp.bfloat16):
    array = jax.random.normal(key, extent, jnp.float32) * deviation
    if len(cuts) > 0:
        array = block_scale(key, extent, cuts, -0.22, 0.18) * array
    return jnp.clip(array, min=-limit, max=limit).astype(kind)


def setup_inputs(seed: int = 0) -> dict:
    seeds = jax.random.split(jax.random.key(seed), 15)
    river_lower = draw_river_lower(jax.random.fold_in(seeds[14], 71), 0)
    river_main = draw_river_main(jax.random.fold_in(seeds[14], 71), 0)
    river_upper = draw_river_upper(jax.random.fold_in(seeds[14], 71), 0)
    river_rhs = scatter_about(seeds[3], (NS, 2, NC), 0.01, 0.08, ((0, 4), (2, 8)), jnp.float32)
    weir_crest = jnp.clip(jax.random.uniform(seeds[4], (NS, NC), jnp.float32, -1.0, 1.0) * block_scale(seeds[4], (NS, NC), ((0, 4), (1, 8)), -0.4, 0.0), -1.0, 1.0)
    weir_regime = set_ends(jax.random.randint(seeds[5], (NS, NC), 0, 3), jax.random.fold_in(seeds[5], 1), 0, 2).astype(jnp.int32)
    weir_tile_keys = jax.random.split(jax.random.fold_in(seeds[6], 1), N_ROW * N_COL * K * CH // (K * CH))
    weir_tile_turns = jax.random.permutation(jax.random.fold_in(seeds[6], 3), N_ROW * N_COL * K * CH // (K * CH))
    weir_tile = jax.vmap(lambda own, number: shared_out(jax.random.fold_in(seeds[6], 2), own, number, K * CH, DEVICES, 1, CAP, 2))(weir_tile_keys, weir_tile_turns).reshape((N_ROW, N_COL, K, CH, 1))
    weir_row = set_ends(jax.random.randint(seeds[7], (NS, NC), 0, TX), jax.random.fold_in(seeds[7], 1), 0, TX - 1).astype(jnp.int32)
    weir_col = set_ends(jax.random.randint(seeds[8], (NS, NC), 0, TY), jax.random.fold_in(seeds[8], 1), 0, TY - 1).astype(jnp.int32)
    bed_level = jnp.clip(-1.0 + 1.0 * jax.random.uniform(seeds[9], (NX, NY), jnp.float32) ** block_scale(seeds[9], (NX, NY), ((0, 4), (1, 8)), -0.2, 0.2), -1.0, 0.0)
    water_depth = jnp.clip(jnp.exp(math.log(1.5) - 4.317488 * jax.random.uniform(seeds[10], (NX, NY), jnp.float32) ** block_scale(seeds[10], (NX, NY), ((0, 4), (1, 8)), -0.2, 0.2)), 0.02, 1.5)
    flux_first = scatter_about(seeds[11], (NX, NY), 0.3, 2.4, ((0, 4), (1, 8)), jnp.float32)
    flux_second = scatter_about(seeds[12], (NX, NY), 0.3, 2.4, ((0, 4), (1, 8)), jnp.float32)
    wet_mask = set_ends((jax.random.randint(seeds[13], (NX, NY), 0, 4) < 3).astype(jnp.int32), jax.random.fold_in(seeds[13], 1), 0, 1)
    return {"river_lower": river_lower, "river_main": river_main, "river_upper": river_upper, "river_rhs": river_rhs, "weir_crest": weir_crest, "weir_regime": weir_regime, "weir_tile": weir_tile, "weir_row": weir_row, "weir_col": weir_col, "bed_level": bed_level, "water_depth": water_depth, "flux_first": flux_first, "flux_second": flux_second, "wet_mask": wet_mask}


GRAVITY = 9.81
TIME_STEP = 1.0
CELL_WIDTH = 10.0
MANNING_SQ = 0.0009
DEPTH_FLOOR = 0.05
WEIR_GAIN = 0.5
FREE_COEF = 0.5
SUB_COEF = 0.4
SUB_OFFSET = 0.25
GATE_COEF = 0.2

def times_pair(left_block, right_block):
    return left_block[..., :, 0:1, :] * right_block[..., 0:1, :, :] + left_block[..., :, 1:2, :] * right_block[..., 1:2, :, :]

def invert_pair(matrix):
    determinant = matrix[0, 0] * matrix[1, 1] - matrix[0, 1] * matrix[1, 0]
    upper_row = jnp.stack([matrix[1, 1], -matrix[0, 1]])
    lower_row = jnp.stack([-matrix[1, 0], matrix[0, 0]])
    return jnp.stack([upper_row, lower_row]) / determinant

def chain_solve(lower_blocks, main_blocks, upper_blocks, rhs_cols):
    chain_count = main_blocks.shape[-1]
    column_count = rhs_cols.shape[2]

    def forward(running, blocks):
        coupled, partial_value = running
        lower_k, main_k, upper_k, right_k = blocks
        pivot_inv = invert_pair(main_k - times_pair(lower_k, coupled))
        coupled = times_pair(pivot_inv, upper_k)
        partial_value = times_pair(pivot_inv, right_k - times_pair(lower_k, partial_value))
        return ((coupled, partial_value), (coupled, partial_value))
    zero_state = (jnp.zeros((2, 2, chain_count), jnp.float32), jnp.zeros((2, column_count, chain_count), jnp.float32))
    _, (couples, partials) = lax.scan(forward, zero_state, (lower_blocks, main_blocks, upper_blocks, rhs_cols))

    def backward(after_row, blocks):
        coupled, partial_value = blocks
        solved = partial_value - times_pair(coupled, after_row)
        return (solved, solved)
    _, solutions = lax.scan(backward, jnp.zeros((2, column_count, chain_count), jnp.float32), (couples, partials), reverse=True)
    return solutions

def face_flux(eta_here, eta_next, bed_here, bed_next, old_flux):
    flow_depth = jnp.maximum(jnp.maximum(eta_here, eta_next) - jnp.maximum(bed_here, bed_next), DEPTH_FLOOR)
    gradient = (eta_next - eta_here) / CELL_WIDTH
    pushed = old_flux - GRAVITY * TIME_STEP * flow_depth * gradient
    return pushed / (1.0 + GRAVITY * TIME_STEP * MANNING_SQ * jnp.abs(old_flux) / flow_depth ** (7.0 / 3.0))

def flood_step(padded, depth_now, wet_float, first_closed, last_closed, left_closed, right_closed):
    surface, ground, flux_one, flux_two = (padded[0], padded[1], padded[2], padded[3])
    row_count = depth_now.shape[0]
    col_count = depth_now.shape[1]
    along_one = face_flux(surface[0:row_count + 1, 1:col_count + 1], surface[1:row_count + 2, 1:col_count + 1], ground[0:row_count + 1, 1:col_count + 1], ground[1:row_count + 2, 1:col_count + 1], flux_one[0:row_count + 1, 1:col_count + 1])
    along_one = along_one.at[0].set(jnp.where(first_closed, 0.0, along_one[0]))
    along_one = along_one.at[row_count].set(jnp.where(last_closed, 0.0, along_one[row_count]))
    along_two = face_flux(surface[1:row_count + 1, 0:col_count + 1], surface[1:row_count + 1, 1:col_count + 2], ground[1:row_count + 1, 0:col_count + 1], ground[1:row_count + 1, 1:col_count + 2], flux_two[1:row_count + 1, 0:col_count + 1])
    along_two = along_two.at[:, 0].set(jnp.where(left_closed, 0.0, along_two[:, 0]))
    along_two = along_two.at[:, col_count].set(jnp.where(right_closed, 0.0, along_two[:, col_count]))
    new_depth = depth_now + wet_float * (TIME_STEP / CELL_WIDTH) * (along_one[:-1] - along_one[1:] + (along_two[:, :-1] - along_two[:, 1:]))
    return (new_depth, along_one[1:], along_two[:, 1:])

def reference(river_lower, river_main, river_upper, river_rhs, weir_crest, weir_regime, weir_tile, weir_row, weir_col, bed_level, water_depth, flux_first, flux_second, wet_mask):
    river_state = chain_solve(river_lower, river_main, river_upper, river_rhs[:, :, None, :])[:, :, 0, :]
    river_phase = river_state[:, 0, :]
    head_height = jnp.maximum(river_phase - weir_crest, 0.0)
    free_part = jnp.where(weir_regime == 0, FREE_COEF * head_height * jnp.sqrt(head_height), 0.0)
    sub_part = jnp.where(weir_regime == 1, SUB_COEF * jnp.sqrt(head_height + SUB_OFFSET), jnp.where(weir_regime == 2, GATE_COEF, 0.0))
    tile_ids = weir_tile.reshape(N_ROW, N_COL, K, CH).transpose(0, 2, 1, 3).reshape(NS, NC)
    cell_first = tile_ids // N_COL * TX + weir_row
    cell_second = tile_ids % N_COL * TY + weir_col
    target = (cell_first * NY + cell_second).reshape(-1)
    surface = bed_level + water_depth
    weir_flow = free_part.reshape(-1) + sub_part.reshape(-1) * (river_phase.reshape(-1) - surface.reshape(-1)[target])
    wetted = jnp.maximum(water_depth.reshape(-1).at[target].add(WEIR_GAIN * weir_flow), 0.0).reshape(NX, NY)
    wet_float = wet_mask.astype(jnp.float32)
    depth_now, first_now, second_now = (wetted, flux_first, flux_second)
    for repeat in range(2):
        stacked = jnp.stack([bed_level + depth_now, bed_level, first_now, second_now])
        padded = jnp.pad(stacked, ((0, 0), (1, 1), (1, 1)))
        depth_now, first_now, second_now = flood_step(padded, depth_now, wet_float, True, True, True, True)
    return (river_state, depth_now, first_now, second_now)
```

```python
import functools

import jax
import jax.numpy as jnp
from jax import lax
from jax.experimental import pallas as pl
from jax.experimental.pallas import tpu as pltpu
from jax.sharding import PartitionSpec as P

GRAVITY = 9.81
TIME_STEP = 1.0
CELL_WIDTH = 10.0
MANNING_SQ = 0.0009
DEPTH_FLOOR = 0.05
WEIR_GAIN = 0.5
FREE_COEF = 0.5
SUB_COEF = 0.4
SUB_OFFSET = 0.25
GATE_COEF = 0.2

F32 = jnp.float32
BF16 = jnp.bfloat16
LANES = 128
LOW = 256
VMEM = pl.BlockSpec(memory_space=pltpu.VMEM)
SMEM = pl.BlockSpec(memory_space=pltpu.SMEM)
PARAMS = pltpu.CompilerParams(vmem_limit_bytes=40 * 2**20)


def mat_mat(a, b):
    return [[a[i][0] * b[0][j] + a[i][1] * b[1][j] for j in range(2)] for i in range(2)]


def mat_vec(a, v):
    return [a[i][0] * v[0] + a[i][1] * v[1] for i in range(2)]


def mat_sub(a, b):
    return [[a[i][j] - b[i][j] for j in range(2)] for i in range(2)]


def mat_neg(a):
    return [[-a[i][j] for j in range(2)] for i in range(2)]


def mat_inv(m):
    scale = 1.0 / (m[0][0] * m[1][1] - m[0][1] * m[1][0])
    return [[m[1][1] * scale, -m[0][1] * scale], [-m[1][0] * scale, m[0][0] * scale]]


def solve_kernel(sections, lower_ref, main_ref, upper_ref, rhs_ref, solved_ref, packed_ref):
    def block(ref, k):
        return [[ref[pl.ds(k * 32 + i * 16 + j, 8, stride=2), :] for j in range(2)] for i in range(2)]

    couples = []
    for k in range(sections):
        lower = block(lower_ref, k)
        main = block(main_ref, k)
        upper = block(upper_ref, k)
        right = [rhs_ref[pl.ds(k * 16 + j, 8, stride=2), :] for j in range(2)]
        if k == 0:
            inverse = mat_inv(main)
            left = mat_neg(mat_mat(inverse, lower))
            value = mat_vec(inverse, right)
        else:
            inverse = mat_inv(mat_sub(main, mat_mat(lower, couples[-1])))
            left = mat_neg(mat_mat(inverse, mat_mat(lower, left)))
            moved = mat_vec(lower, value)
            value = mat_vec(inverse, [right[i] - moved[i] for i in range(2)])
        couples.append(mat_mat(inverse, upper))
        for i in range(2):
            solved_ref[k, i] = value[i]
            for j in range(2):
                solved_ref[k, 2 + 2 * i + j] = left[i][j]
    spike = mat_neg(couples[-1])
    tail = (value, left, spike)
    for i in range(2):
        for j in range(2):
            solved_ref[sections - 1, 6 + 2 * i + j] = spike[i][j]
    for k in range(sections - 2, -1, -1):
        couple = couples[k]
        after = mat_vec(couple, value)
        value = [solved_ref[k, i] - after[i] for i in range(2)]
        after = mat_mat(couple, left)
        left = [[solved_ref[k, 2 + 2 * i + j] - after[i][j] for j in range(2)] for i in range(2)]
        spike = mat_neg(mat_mat(couple, spike))
        for i in range(2):
            solved_ref[k, i] = value[i]
            for j in range(2):
                solved_ref[k, 2 + 2 * i + j] = left[i][j]
                solved_ref[k, 6 + 2 * i + j] = spike[i][j]
    for i in range(2):
        packed_ref[i] = value[i]
        packed_ref[2 + i] = tail[0][i]
        for j in range(2):
            packed_ref[4 + 2 * i + j] = left[i][j]
            packed_ref[8 + 2 * i + j] = tail[1][i][j]
            packed_ref[12 + 2 * i + j] = spike[i][j]
            packed_ref[16 + 2 * i + j] = tail[2][i][j]


def rank_kernel(tiles, capacity, groups, tile_ref, slot_ref):
    table = lax.broadcasted_iota(jnp.int32, (tiles, LANES), 0)
    row_at = lax.broadcasted_iota(jnp.int32, (LANES, 2 * LANES), 0)
    col_at = lax.broadcasted_iota(jnp.int32, (LANES, 2 * LANES), 1)
    earlier = jnp.where(row_at < col_at, 1.0, 0.0).astype(BF16)

    def body(g, offset):
        ids = tile_ref[pl.ds((g // 8) * 64 + g % 8, 8, stride=8), :]
        hits = [ids[r : r + 1, :] == table for r in range(8)]
        hot = jnp.concatenate([jnp.where(h, 1.0, 0.0).astype(BF16) for h in hits], 0)
        counts = jnp.dot(hot, earlier, preferred_element_type=F32)
        rows = []
        for r in range(8):
            part = counts[r * tiles : (r + 1) * tiles]
            place = jnp.where(hits[r], part[:, :LANES] + offset, 0.0)
            rows.append(jnp.sum(place, axis=0, keepdims=True))
            offset = offset + part[:, LANES:]
        slot_ref[pl.ds(g * 8, 8), :] = jnp.concatenate(rows, 0).astype(jnp.int32)
        return offset

    lax.fori_loop(0, groups, body, table.astype(F32) * capacity)


def rows16(row):
    return jnp.broadcast_to(row, (16, LANES)).astype(BF16)


def table16(count):
    shape = (count // 16, 16, LANES)
    at = lax.broadcasted_iota(jnp.int32, shape, 0) * 16 + lax.broadcasted_iota(jnp.int32, shape, 1)
    return at.astype(F32).astype(BF16)


def halves(value):
    high = value.astype(BF16).astype(F32)
    return high, value - high


def one_hots(high, low, values, high_table, low_table):
    one = jnp.ones((), BF16)
    zero = jnp.zeros((), BF16)
    left, right = [], []
    for r in range(8):
        hit = high_table == rows16(high[r : r + 1])[None]
        left.append(
            jnp.concatenate(
                [jnp.where(hit, rows16(v[r : r + 1])[None], zero).reshape(-1, LANES) for v in values], 0
            )
        )
        hit = low_table == rows16(low[r : r + 1])[None]
        right.append(jnp.where(hit, one, zero).reshape(-1, LANES))
    return jnp.concatenate(left, 1), jnp.concatenate(right, 1)


def product(left, right):
    return lax.dot_general(left, right, (((1,), (1,)), ((), ())), preferred_element_type=F32)


def weir_kernel(
    sections,
    segments,
    tiles,
    capacity,
    row_count,
    position_ref,
    gathered_ref,
    solved_ref,
    crest_ref,
    regime_ref,
    row_ref,
    col_ref,
    slot_ref,
    state_ref,
    out_ref,
    phase_ref,
    total_ref,
):
    def reduced(d):
        at = lambda n: gathered_ref[d, pl.ds(n * 8, 8), :]
        pair = lambda n: [at(n), at(n + 1)]
        square = lambda n: [[at(n), at(n + 1)], [at(n + 2), at(n + 3)]]
        return pair(0), pair(2), square(4), square(8), square(12), square(16)

    eliminated = []
    for d in range(segments):
        head_y, tail_y, head_left, tail_left, head_right, tail_right = reduced(d)
        if d == 0:
            first = (mat_neg(head_right), head_y)
            last = (mat_neg(tail_right), tail_y)
        else:
            couple, value = last
            inner = mat_mat(head_left, couple)
            inner = [[inner[0][0] + 1.0, inner[0][1]], [inner[1][0], inner[1][1] + 1.0]]
            inverse = mat_inv(inner)
            first_couple = mat_neg(mat_mat(inverse, head_right))
            moved = mat_vec(head_left, value)
            first_value = mat_vec(inverse, [head_y[i] + moved[i] for i in range(2)])
            bridge = mat_mat(tail_left, couple)
            through = mat_mat(bridge, first_couple)
            last_couple = [[-tail_right[i][j] - through[i][j] for j in range(2)] for i in range(2)]
            moved = mat_vec(tail_left, value)
            back = mat_vec(bridge, first_value)
            last_value = [tail_y[i] + moved[i] - back[i] for i in range(2)]
            first = (first_couple, first_value)
            last = (last_couple, last_value)
        eliminated.append((first, last))
    position = position_ref[0]
    nothing = [jnp.zeros((8, LANES), F32)] * 2
    upcoming = nothing
    after = nothing
    before = nothing
    for d in range(segments - 1, -1, -1):
        (first_couple, first_value), (last_couple, last_value) = eliminated[d]
        after = [jnp.where(position == d, upcoming[i], after[i]) for i in range(2)]
        moved = mat_vec(last_couple, upcoming)
        last_state = [last_value[i] - moved[i] for i in range(2)]
        before = [jnp.where(position == d + 1, last_state[i], before[i]) for i in range(2)]
        moved = mat_vec(first_couple, upcoming)
        upcoming = [first_value[i] - moved[i] for i in range(2)]
    for k in range(sections):
        for i in range(2):
            state = solved_ref[k, i]
            for j in range(2):
                state = state + solved_ref[k, 2 + 2 * i + j] * before[j]
                state = state + solved_ref[k, 6 + 2 * i + j] * after[j]
            state_ref[pl.ds(k * 16 + i, 8, stride=2), :] = state
            if i == 0:
                phase_ref[pl.ds((k // 8) * 64 + k % 8, 8, stride=8), :] = state

    high_count = tiles * capacity // LOW
    high_table = table16(high_count)
    low_table = table16(LOW)
    total_ref[...] = jnp.zeros_like(total_ref)

    def body(g, carry):
        over = pl.multiple_of((g // 8) * 8, 8)
        along = pl.multiple_of((g % 8) * LANES, LANES)
        at = (pl.ds(over, 8), pl.ds(along, LANES))
        rows = pl.ds(pl.multiple_of(g * 8, 8), 8)
        phase = phase_ref[rows, :]
        regime = regime_ref[at]
        head = jnp.maximum(phase - crest_ref[at], 0.0)
        free = jnp.where(regime == 0, FREE_COEF * head * jnp.sqrt(head), 0.0)
        sub = jnp.where(
            regime == 1,
            SUB_COEF * jnp.sqrt(head + SUB_OFFSET),
            jnp.where(regime == 2, GATE_COEF, 0.0),
        )
        constant = halves(WEIR_GAIN * (free + sub * phase))
        slope = halves(WEIR_GAIN * sub)
        col = col_ref[at]
        cell_high = (col // LOW) * row_count + row_ref[at]
        cell_low = (col % LOW).astype(F32)
        slot = slot_ref[rows, :]
        left, right = one_hots(
            (slot // LOW).astype(F32),
            (slot % LOW).astype(F32),
            [*constant, *slope, cell_high.astype(F32), cell_low],
            high_table,
            low_table,
        )
        total_ref[...] += product(left, right)
        return carry

    lax.fori_loop(0, sections * 8 // 8, body, 0, unroll=2)
    per_tile = capacity // LOW
    for v in range(3):
        scale = float(LOW) if v == 2 else 1.0
        start = 2 * v * high_count
        value = total_ref[pl.ds(start, high_count), :] * scale + total_ref[pl.ds(start + high_count, high_count), :]
        for t in range(tiles):
            for j in range(LOW // LANES):
                out_ref[t, pl.ds((v * (LOW // LANES) + j) * per_tile, per_tile), :] = value[
                    t * per_tile : (t + 1) * per_tile, j * LANES : (j + 1) * LANES
                ]


def apply_kernel(sources, rows_each, row_count, col_count, in_ref, bed_ref, depth_ref, wetted_ref, total_ref):
    high_count = row_count * col_count // LOW
    high_table = table16(high_count)
    low_table = table16(LOW)
    total_ref[...] = jnp.zeros_like(total_ref)
    step = 8 // rows_each if rows_each < 8 else 1

    def body(g, carry):
        def part(v):
            return jnp.concatenate(
                [in_ref[g * step + n, pl.ds(v * rows_each, rows_each), :] for n in range(step)], 0
            )

        constant = halves(part(0))
        slope = halves(part(1))
        cell = part(2).astype(jnp.int32)
        left, right = one_hots(
            (cell // LOW).astype(F32),
            (cell % LOW).astype(F32),
            [*constant, *slope],
            high_table,
            low_table,
        )
        total_ref[...] += product(left, right)
        return carry

    lax.fori_loop(0, sources // step, body, 0, unroll=2)
    for n in range(col_count // LOW):
        def summed(v):
            start = 2 * v * high_count + n * row_count
            return total_ref[pl.ds(start, row_count), :] + total_ref[pl.ds(start + high_count, row_count), :]

        cols = pl.ds(n * LOW, LOW)
        depth = depth_ref[:, cols]
        surface = bed_ref[:, cols] + depth
        wetted_ref[:, cols] = jnp.maximum(depth + (summed(0) - summed(1) * surface), 0.0)


def face_flux(eta_here, eta_next, bed_here, bed_next, old_flux):
    flow_depth = jnp.maximum(
        jnp.maximum(eta_here, eta_next) - jnp.maximum(bed_here, bed_next), DEPTH_FLOOR
    )
    gradient = (eta_next - eta_here) / CELL_WIDTH
    pushed = old_flux - GRAVITY * TIME_STEP * flow_depth * gradient
    friction = jnp.exp((-7.0 / 3.0) * jnp.log(flow_depth))
    return pushed / (1.0 + GRAVITY * TIME_STEP * MANNING_SQ * jnp.abs(old_flux) * friction)


def flood_kernel(row_count, col_count, closed_ref, in_ref, depth_ref, first_ref, second_ref):
    depth, bed, first, second, wet = (in_ref[n] for n in range(5))
    shape = depth.shape
    row_at = lax.broadcasted_iota(jnp.int32, shape, 0) - 8
    col_at = lax.broadcasted_iota(jnp.int32, shape, 1) - LANES
    first_shut = (row_at == closed_ref[0]) | (row_at == closed_ref[1])
    second_shut = (col_at == closed_ref[2]) | (col_at == closed_ref[3])
    down = lambda x: pltpu.roll(x, shape[0] - 1, 0)
    up = lambda x: pltpu.roll(x, 1, 0)
    onward = lambda x: pltpu.roll(x, shape[1] - 1, 1)
    back = lambda x: pltpu.roll(x, 1, 1)
    bed_down = down(bed)
    bed_onward = onward(bed)
    for _ in range(2):
        eta = bed + depth
        first = jnp.where(first_shut, 0.0, face_flux(eta, down(eta), bed, bed_down, first))
        second = jnp.where(second_shut, 0.0, face_flux(eta, onward(eta), bed, bed_onward, second))
        depth = depth + wet * (TIME_STEP / CELL_WIDTH) * (up(first) - first + (back(second) - second))
    here = (slice(8, 8 + row_count), slice(LANES, LANES + col_count))
    depth_ref[...] = depth[here]
    first_ref[...] = first[here]
    second_ref[...] = second[here]


def shifted(block, axis, step):
    count = lax.axis_size(axis)
    return lax.ppermute(block, axis, [(i, (i + step) % count) for i in range(count)])


def with_sides(block, axis, dim, width):
    size = block.shape[dim]
    low = shifted(lax.slice_in_dim(block, size - width, size, axis=dim), axis, 1)
    high = shifted(lax.slice_in_dim(block, 0, width, axis=dim), axis, -1)
    return jnp.concatenate([low, block, high], axis=dim)


def local(
    river_lower,
    river_main,
    river_upper,
    river_rhs,
    weir_crest,
    weir_regime,
    weir_tile,
    weir_row,
    weir_col,
    bed_level,
    water_depth,
    flux_first,
    flux_second,
    wet_mask,
):
    sections, chains = weir_crest.shape
    row_count, col_count = water_depth.shape
    row_size = lax.axis_size("row")
    col_size = lax.axis_size("col")
    row_at = lax.axis_index("row")
    col_at = lax.axis_index("col")
    tiles = row_size * col_size
    weirs = sections * chains
    capacity = 2 * weirs // tiles
    lane_rows = chains // LANES

    def block_rows(array):
        split = array.reshape(sections, 2, 2, lane_rows, LANES)
        return split.transpose(0, 1, 3, 2, 4).reshape(-1, LANES)

    rhs_rows = river_rhs.reshape(sections, 2, lane_rows, LANES).transpose(0, 2, 1, 3).reshape(-1, LANES)
    solved, packed = pl.pallas_call(
        functools.partial(solve_kernel, sections),
        out_shape=(
            jax.ShapeDtypeStruct((sections, 10, lane_rows, LANES), F32),
            jax.ShapeDtypeStruct((20, lane_rows, LANES), F32),
        ),
        in_specs=[VMEM] * 4,
        out_specs=(VMEM, VMEM),
        compiler_params=PARAMS,
        name="solve",
    )(block_rows(river_lower), block_rows(river_main), block_rows(river_upper), rhs_rows)
    slots = pl.pallas_call(
        functools.partial(rank_kernel, tiles, capacity, sections * lane_rows // 8),
        out_shape=jax.ShapeDtypeStruct((weirs // LANES, LANES), jnp.int32),
        in_specs=[VMEM],
        out_specs=VMEM,
        compiler_params=PARAMS,
        name="rank",
    )(weir_tile.reshape(weirs // LANES, LANES))
    gathered = lax.all_gather(packed.reshape(1, -1, LANES), "row", axis=0, tiled=True)
    high_count = tiles * capacity // LOW
    state_rows, outgoing = pl.pallas_call(
        functools.partial(weir_kernel, sections, row_size, tiles, capacity, row_count),
        out_shape=(
            jax.ShapeDtypeStruct((sections * lane_rows * 2, LANES), F32),
            jax.ShapeDtypeStruct((tiles, 3 * capacity // LANES, LANES), F32),
        ),
        in_specs=[SMEM] + [VMEM] * 7,
        out_specs=(VMEM, VMEM),
        scratch_shapes=[
            pltpu.VMEM((weirs // LANES, LANES), F32),
            pltpu.VMEM((6 * high_count, LOW), F32),
        ],
        compiler_params=PARAMS,
        name="weirs",
    )(row_at.reshape(1), gathered, solved, weir_crest, weir_regime, weir_row, weir_col, slots)
    river_state = (
        state_rows.reshape(sections, lane_rows, 2, LANES).transpose(0, 2, 1, 3).reshape(sections, 2, chains)
    )
    arrived = lax.all_to_all(outgoing, ("row", "col"), split_axis=0, concat_axis=0, tiled=True)
    wetted = pl.pallas_call(
        functools.partial(apply_kernel, tiles, capacity // LANES, row_count, col_count),
        out_shape=jax.ShapeDtypeStruct((row_count, col_count), F32),
        in_specs=[VMEM] * 3,
        out_specs=VMEM,
        scratch_shapes=[pltpu.VMEM((4 * row_count * col_count // LOW, LOW), F32)],
        compiler_params=PARAMS,
        name="apply",
    )(arrived, bed_level, water_depth)
    stacked = jnp.stack([wetted, bed_level, flux_first, flux_second, wet_mask.astype(F32)])
    padded = with_sides(with_sides(stacked, "row", 1, 2), "col", 2, 2)
    padded = jnp.pad(padded, ((0, 0), (6, 6), (LANES - 2, LANES - 2)))
    closed = jnp.stack(
        [
            jnp.where(row_at == 0, -1, -9),
            jnp.where(row_at == row_size - 1, row_count - 1, -9),
            jnp.where(col_at == 0, -1, -LANES - 1),
            jnp.where(col_at == col_size - 1, col_count - 1, -LANES - 1),
        ]
    ).astype(jnp.int32)
    tile_out = jax.ShapeDtypeStruct((row_count, col_count), F32)
    depth_out, first_out, second_out = pl.pallas_call(
        functools.partial(flood_kernel, row_count, col_count),
        out_shape=(tile_out, tile_out, tile_out),
        in_specs=[SMEM, VMEM],
        out_specs=(VMEM, VMEM, VMEM),
        compiler_params=PARAMS,
        name="flood",
    )(closed, padded)
    return (river_state, depth_out, first_out, second_out)


def solution(mesh):
    in_specs = (
        P("row", None, None, "col"),
        P("row", None, None, "col"),
        P("row", None, None, "col"),
        P("row", None, "col"),
        P("row", "col"),
        P("row", "col"),
        P("row", "col", None, None, None),
        P("row", "col"),
        P("row", "col"),
        P("row", "col"),
        P("row", "col"),
        P("row", "col"),
        P("row", "col"),
        P("row", "col"),
    )
    out_specs = (P("row", None, "col"), P("row", "col"), P("row", "col"), P("row", "col"))
    return jax.shard_map(local, mesh=mesh, in_specs=in_specs, out_specs=out_specs, check_vma=False)
```

```python
import functools

import jax
import jax.numpy as jnp
from jax import lax
from jax.experimental import pallas as pl
from jax.experimental.pallas import tpu as pltpu
from jax.sharding import PartitionSpec as P

GRAVITY = 9.81
TIME_STEP = 1.0
CELL_WIDTH = 10.0
MANNING_SQ = 0.0009
DEPTH_FLOOR = 0.05
WEIR_GAIN = 0.5
FREE_COEF = 0.5
SUB_COEF = 0.4
SUB_OFFSET = 0.25
GATE_COEF = 0.2

F32 = jnp.float32
BF16 = jnp.bfloat16
LANES = 128
LOW = 256
VMEM = pl.BlockSpec(memory_space=pltpu.VMEM)
SMEM = pl.BlockSpec(memory_space=pltpu.SMEM)
ANY = pl.BlockSpec(memory_space=pl.ANY)
PARAMS = pltpu.CompilerParams(vmem_limit_bytes=40 * 2**20)
WIDE = pltpu.CompilerParams(vmem_limit_bytes=60 * 2**20)


def start_copies(sources, targets, sems):
    copies = [pltpu.make_async_copy(s, t, sems.at[n]) for n, (s, t) in enumerate(zip(sources, targets))]
    for copy in copies:
        copy.start()
    return copies


def mat_mat(a, b):
    return [[a[i][0] * b[0][j] + a[i][1] * b[1][j] for j in range(2)] for i in range(2)]


def mat_vec(a, v):
    return [a[i][0] * v[0] + a[i][1] * v[1] for i in range(2)]


def mat_sub(a, b):
    return [[a[i][j] - b[i][j] for j in range(2)] for i in range(2)]


def mat_neg(a):
    return [[-a[i][j] for j in range(2)] for i in range(2)]


def mat_inv(m):
    scale = 1.0 / (m[0][0] * m[1][1] - m[0][1] * m[1][0])
    return [[m[1][1] * scale, -m[0][1] * scale], [-m[1][0] * scale, m[0][0] * scale]]


def solve_kernel(sections, *refs):
    solved_ref, packed_ref = refs[4:6]
    lower_ref, main_ref, upper_ref, rhs_ref = refs[6:10]
    for copy in start_copies(refs[:4], refs[6:10], refs[10]):
        copy.wait()

    def block(ref, k):
        return [[ref[pl.ds(k * 32 + i * 16 + j, 8, stride=2), :] for j in range(2)] for i in range(2)]

    couples = []
    for k in range(sections):
        lower = block(lower_ref, k)
        main = block(main_ref, k)
        upper = block(upper_ref, k)
        right = [rhs_ref[pl.ds(k * 16 + j, 8, stride=2), :] for j in range(2)]
        if k == 0:
            inverse = mat_inv(main)
            left = mat_neg(mat_mat(inverse, lower))
            value = mat_vec(inverse, right)
        else:
            inverse = mat_inv(mat_sub(main, mat_mat(lower, couples[-1])))
            left = mat_neg(mat_mat(inverse, mat_mat(lower, left)))
            moved = mat_vec(lower, value)
            value = mat_vec(inverse, [right[i] - moved[i] for i in range(2)])
        couples.append(mat_mat(inverse, upper))
        for i in range(2):
            solved_ref[k, i] = value[i]
            for j in range(2):
                solved_ref[k, 2 + 2 * i + j] = left[i][j]
    spike = mat_neg(couples[-1])
    tail = (value, left, spike)
    for i in range(2):
        for j in range(2):
            solved_ref[sections - 1, 6 + 2 * i + j] = spike[i][j]
    for k in range(sections - 2, -1, -1):
        couple = couples[k]
        after = mat_vec(couple, value)
        value = [solved_ref[k, i] - after[i] for i in range(2)]
        after = mat_mat(couple, left)
        left = [[solved_ref[k, 2 + 2 * i + j] - after[i][j] for j in range(2)] for i in range(2)]
        spike = mat_neg(mat_mat(couple, spike))
        for i in range(2):
            solved_ref[k, i] = value[i]
            for j in range(2):
                solved_ref[k, 2 + 2 * i + j] = left[i][j]
                solved_ref[k, 6 + 2 * i + j] = spike[i][j]
    for i in range(2):
        packed_ref[i] = value[i]
        packed_ref[2 + i] = tail[0][i]
        for j in range(2):
            packed_ref[4 + 2 * i + j] = left[i][j]
            packed_ref[8 + 2 * i + j] = tail[1][i][j]
            packed_ref[12 + 2 * i + j] = spike[i][j]
            packed_ref[16 + 2 * i + j] = tail[2][i][j]


def load_pair(ref, n):
    return [ref[n], ref[n + 1]]


def load_square(ref, n):
    return [load_pair(ref, n), load_pair(ref, n + 2)]


def store_all(ref, values):
    flat = []
    for value in values:
        flat += [*value[0], *value[1]] if isinstance(value[0], list) else value
    for n, item in enumerate(flat):
        ref[n] = item


def pick(flag, one, other):
    if isinstance(one, list):
        return [pick(flag, a, b) for a, b in zip(one, other)]
    return jnp.where(flag, one, other)


def add(a, b):
    if isinstance(a, list):
        return [add(x, y) for x, y in zip(a, b)]
    return a + b


def meet(head_y, head_left, tail_y, tail_right):
    inner = mat_mat(head_left, tail_right)
    inverse = mat_inv([[1.0 - inner[0][0], -inner[0][1]], [-inner[1][0], 1.0 - inner[1][1]]])
    return inverse, mat_vec(inverse, add(head_y, mat_vec(head_left, tail_y)))


def merge_kernel(step, first, position_ref, own_ref, other_ref, *refs):
    known_ref = None if first else refs[0]
    group_ref, map_ref, send_ref = refs[-3:]
    position = position_ref[0]
    late = ((position >> step) & 1) == 1

    def group(ref):
        return [load_pair(ref, 0), load_pair(ref, 2)] + [load_square(ref, n) for n in (4, 8, 12, 16)]

    own, other = group(own_ref), group(other_ref)
    head_y, tail_y, head_left, tail_left, head_right, tail_right = pick(late, other, own)
    next_head_y, next_tail_y, next_head_left, next_tail_left, next_head_right, next_tail_right = pick(
        late, own, other
    )
    inverse, head = meet(next_head_y, next_head_left, tail_y, tail_right)
    head_before = mat_mat(inverse, mat_mat(next_head_left, tail_left))
    head_after = mat_mat(inverse, next_head_right)
    tail = add(tail_y, mat_vec(tail_right, head))
    tail_before = add(tail_left, mat_mat(tail_right, head_before))
    tail_after = mat_mat(tail_right, head_after)
    joined = [
        add(head_y, mat_vec(head_right, head)),
        add(next_tail_y, mat_vec(next_tail_left, tail)),
        add(head_left, mat_mat(head_right, head_before)),
        mat_mat(next_tail_left, tail_before),
        mat_mat(head_right, head_after),
        add(next_tail_right, mat_mat(next_tail_left, tail_after)),
    ]
    zero = jnp.zeros(tail[0].shape, F32)
    one = zero + 1.0
    unit, none, nothing = [[one, zero], [zero, one]], [[zero, zero], [zero, zero]], [zero, zero]
    if first:
        maps = [
            [pick(late, tail_before, unit), pick(late, tail_after, none), pick(late, tail, nothing)],
            [pick(late, none, head_before), pick(late, unit, head_after), pick(late, nothing, head)],
        ]
    else:
        maps = []
        for n in range(2):
            by_before = load_square(known_ref, 10 * n)
            by_after = load_square(known_ref, 10 * n + 4)
            value = load_pair(known_ref, 10 * n + 8)
            maps.append(
                [
                    pick(late, mat_mat(by_before, tail_before), add(by_before, mat_mat(by_after, head_before))),
                    pick(late, add(by_after, mat_mat(by_before, tail_after)), mat_mat(by_after, head_after)),
                    pick(late, add(value, mat_vec(by_before, tail)), add(value, mat_vec(by_after, head))),
                ]
            )
    store_all(group_ref, joined)
    store_all(map_ref, maps[0] + maps[1])
    later = ((position >> (step + 1)) & 1) == 1
    store_all(send_ref, [pick(later, joined[0], joined[1]), pick(later, joined[2], joined[5])])


def rows16(row):
    return jnp.broadcast_to(row, (16, LANES)).astype(BF16)


def table16(count):
    shape = (count // 16, 16, LANES)
    at = lax.broadcasted_iota(jnp.int32, shape, 0) * 16 + lax.broadcasted_iota(jnp.int32, shape, 1)
    return at.astype(F32).astype(BF16)


def halves(value):
    high = value.astype(BF16).astype(F32)
    return high, value - high


def one_hots(high, low, values, high_table, low_table):
    one = jnp.ones((), BF16)
    zero = jnp.zeros((), BF16)
    left, right = [], []
    for r in range(8):
        hit = high_table == rows16(high[r : r + 1])[None]
        left.append(
            jnp.concatenate(
                [jnp.where(hit, rows16(v[r : r + 1])[None], zero).reshape(-1, LANES) for v in values], 0
            )
        )
        hit = low_table == rows16(low[r : r + 1])[None]
        right.append(jnp.where(hit, one, zero).reshape(-1, LANES))
    return jnp.concatenate(left, 1), jnp.concatenate(right, 1)


def product(left, right):
    return lax.dot_general(left, right, (((1,), (1,)), ((), ())), preferred_element_type=F32)


def group_at(g):
    over = pl.multiple_of((g // 8) * 8, 8)
    along = pl.multiple_of((g % 8) * LANES, LANES)
    return (pl.ds(over, 8), pl.ds(along, LANES))


def fill_slots(high_count, groups, slot_ref, values, total_ref):
    high_table = table16(high_count)
    low_table = table16(LOW)
    total_ref[...] = jnp.zeros_like(total_ref)

    def body(g, carry):
        slot = slot_ref[pl.ds(pl.multiple_of(g * 8, 8), 8), :]
        left, right = one_hots(
            (slot // LOW).astype(F32), (slot % LOW).astype(F32), values(g), high_table, low_table
        )
        total_ref[...] += product(left, right)
        return carry

    lax.fori_loop(0, groups, body, 0, unroll=8)


def store_slots(tiles, capacity, total_ref, part, scale, out_ref, row):
    high_count = tiles * capacity // LOW
    per_tile = capacity // LOW
    first = total_ref[pl.ds(part * high_count, high_count), :]
    value = first * scale + total_ref[pl.ds((part + 1) * high_count, high_count), :]
    for t in range(tiles):
        for j in range(LOW // LANES):
            out_ref[t, pl.ds(row + j * per_tile, per_tile), :] = value[
                t * per_tile : (t + 1) * per_tile, j * LANES : (j + 1) * LANES
            ]


def rank_kernel(tiles, capacity, groups, tile_in, slot_ref, tile_ref, sems):
    start_copies((tile_in,), (tile_ref,), sems)[0].wait()
    table = lax.broadcasted_iota(jnp.int32, (tiles, LANES), 0)
    row_at = lax.broadcasted_iota(jnp.int32, (LANES, 2 * LANES), 0)
    col_at = lax.broadcasted_iota(jnp.int32, (LANES, 2 * LANES), 1)
    earlier = jnp.where(row_at < col_at, 1.0, 0.0).astype(BF16)

    def body(g, offset):
        ids = tile_ref[pl.ds((g // 8) * 64 + g % 8, 8, stride=8), :]
        hits = [ids[r : r + 1, :] == table for r in range(8)]
        hot = jnp.concatenate([jnp.where(h, 1.0, 0.0).astype(BF16) for h in hits], 0)
        counts = jnp.dot(hot, earlier, preferred_element_type=F32)
        rows = []
        for r in range(8):
            part = counts[r * tiles : (r + 1) * tiles]
            place = jnp.where(hits[r], part[:, :LANES] + offset, 0.0)
            rows.append(jnp.sum(place, axis=0, keepdims=True))
            offset = offset + part[:, LANES:]
        slot_ref[pl.ds(g * 8, 8), :] = jnp.concatenate(rows, 0).astype(jnp.int32)
        return offset

    lax.fori_loop(0, groups, body, table.astype(F32) * capacity, unroll=4)


def cell_kernel(tiles, capacity, groups, row_count, slot_ref, row_in, col_in, after, cells_ref, *refs):
    row_ref, col_ref, total_ref, sems = refs
    for copy in start_copies((row_in, col_in), (row_ref, col_ref), sems):
        copy.wait()

    def values(g):
        col = col_ref[group_at(g)]
        high = (col // LOW) * row_count + row_ref[group_at(g)]
        return [high.astype(F32), (col % LOW).astype(F32)]

    fill_slots(tiles * capacity // LOW, groups, slot_ref, values, total_ref)
    store_slots(tiles, capacity, total_ref, 0, float(LOW), cells_ref, 0)


def weir_kernel(sections, steps, tiles, capacity, *refs):
    position_ref, own_ref, other_ref, map_ref = refs[:4]
    solved_ref, slot_ref, cells_ref, crest_in, regime_in = refs[4:9]
    state_out, out_ref = refs[9:11]
    crest_ref, regime_ref, state_ref, phase_ref, total_ref, sems = refs[11:]
    copies = start_copies((crest_in, regime_in), (crest_ref, regime_ref), sems)
    late = ((position_ref[0] >> (steps - 1)) & 1) == 1
    own = [load_pair(own_ref, 0), load_square(own_ref, 2)]
    other = [load_pair(other_ref, 0), load_square(other_ref, 2)]
    tail_y, tail_right = pick(late, other, own)
    head_y, head_left = pick(late, own, other)
    head = meet(head_y, head_left, tail_y, tail_right)[1]
    tail = add(tail_y, mat_vec(tail_right, head))
    zero = jnp.zeros(tail[0].shape, F32)
    outer_before = pick(late, tail, [zero, zero])
    outer_after = pick(late, [zero, zero], head)
    before, after = (
        add(
            load_pair(map_ref, n + 8),
            add(
                mat_vec(load_square(map_ref, n), outer_before),
                mat_vec(load_square(map_ref, n + 4), outer_after),
            ),
        )
        for n in (0, 10)
    )
    for k in range(sections):
        for i in range(2):
            state = solved_ref[k, i]
            for j in range(2):
                state = state + solved_ref[k, 2 + 2 * i + j] * before[j]
                state = state + solved_ref[k, 6 + 2 * i + j] * after[j]
            state_ref[pl.ds(k * 16 + i, 8, stride=2), :] = state
            if i == 0:
                phase_ref[pl.ds((k // 8) * 64 + k % 8, 8, stride=8), :] = state

    state_copy = pltpu.make_async_copy(state_ref, state_out, sems.at[2])
    state_copy.start()
    for copy in copies:
        copy.wait()

    def values(g):
        phase = phase_ref[pl.ds(pl.multiple_of(g * 8, 8), 8), :]
        regime = regime_ref[group_at(g)]
        head = jnp.maximum(phase - crest_ref[group_at(g)], 0.0)
        free = jnp.where(regime == 0, FREE_COEF * head * jnp.sqrt(head), 0.0)
        sub = jnp.where(
            regime == 1,
            SUB_COEF * jnp.sqrt(head + SUB_OFFSET),
            jnp.where(regime == 2, GATE_COEF, 0.0),
        )
        return [*halves(WEIR_GAIN * (free + sub * phase)), *halves(WEIR_GAIN * sub)]

    fill_slots(tiles * capacity // LOW, sections, slot_ref, values, total_ref)
    rows_each = capacity // LANES
    for v in range(2):
        store_slots(tiles, capacity, total_ref, 2 * v, 1.0, out_ref, v * rows_each)
    out_ref[:, pl.ds(2 * rows_each, rows_each), :] = cells_ref[...]
    state_copy.wait()


def apply_kernel(sources, rows_each, row_count, col_count, *refs):
    in_ref, bed_in, depth_in, first_in, second_in, wet_in = refs[:6]
    tile_ref, top_ref, bottom_ref = refs[6:9]
    depth_ref, wet_ref, total_ref, sems = refs[9:]
    copies = start_copies(
        (bed_in, depth_in, first_in, second_in, wet_in),
        (tile_ref.at[1], depth_ref, tile_ref.at[2], tile_ref.at[3], wet_ref),
        sems,
    )
    high_count = row_count * col_count // LOW
    high_table = table16(high_count)
    low_table = table16(LOW)
    total_ref[...] = jnp.zeros_like(total_ref)
    step = 8 // rows_each if rows_each < 8 else 1

    def body(g, carry):
        def part(v):
            return jnp.concatenate(
                [in_ref[g * step + n, pl.ds(v * rows_each, rows_each), :] for n in range(step)], 0
            )

        cell = part(2).astype(jnp.int32)
        left, right = one_hots(
            (cell // LOW).astype(F32),
            (cell % LOW).astype(F32),
            [*halves(part(0)), *halves(part(1))],
            high_table,
            low_table,
        )
        total_ref[...] += product(left, right)
        return carry

    lax.fori_loop(0, sources // step, body, 0, unroll=8)
    for copy in copies:
        copy.wait()
    tile_ref[4] = wet_ref[...].astype(F32) * (TIME_STEP / CELL_WIDTH)
    for n in range(col_count // LOW):
        def summed(v):
            start = 2 * v * high_count + n * row_count
            return total_ref[pl.ds(start, row_count), :] + total_ref[pl.ds(start + high_count, row_count), :]

        cols = pl.ds(n * LOW, LOW)
        depth = depth_ref[:, cols]
        surface = tile_ref[1, :, cols] + depth
        tile_ref[0, :, cols] = jnp.maximum(depth + (summed(0) - summed(1) * surface), 0.0)
    for out, near, rows in ((top_ref, 0, (0, 1)), (bottom_ref, row_count - 1, (row_count - 2, row_count - 1))):
        for n in range(3):
            for i in range(2):
                out[pl.ds(2 * n + i, 1), :] = tile_ref[n, pl.ds(rows[i], 1), :]
        for n in (3, 4):
            out[pl.ds(3 + n, 1), :] = tile_ref[n, pl.ds(near, 1), :]


def face_flux(eta_here, eta_next, bed_here, bed_next, old_flux):
    flow_depth = jnp.maximum(
        jnp.maximum(eta_here, eta_next) - jnp.maximum(bed_here, bed_next), DEPTH_FLOOR
    )
    gradient = (eta_next - eta_here) / CELL_WIDTH
    pushed = old_flux - GRAVITY * TIME_STEP * flow_depth * gradient
    friction = jnp.exp((-7.0 / 3.0) * jnp.log(flow_depth))
    return pushed / (1.0 + GRAVITY * TIME_STEP * MANNING_SQ * jnp.abs(old_flux) * friction)


def pad_rows(n, tile_ref, above_ref, below_ref, cols):
    at = lax.broadcasted_iota(jnp.int32, (8, 1), 0)
    row = 2 * n if n < 3 else 3 + n
    low = above_ref[pl.ds(row, 1), cols]
    high = below_ref[pl.ds(row, 1), cols]
    if n < 3:
        low_last = above_ref[pl.ds(row + 1, 1), cols]
        high_last = below_ref[pl.ds(row + 1, 1), cols]
    else:
        low_last, high_last = low, high
    low = jnp.where(at == 6, low, jnp.where(at == 7, low_last, 0.0))
    high = jnp.where(at == 0, high, jnp.where(at == 1, high_last, 0.0))
    return jnp.concatenate([low, tile_ref[n, :, cols], high], 0)


def side_lanes(n):
    at = lax.broadcasted_iota(jnp.int32, (8, LANES), 1)
    return (at == 2 * n) | (at == 2 * n + 1)


def sides_kernel(col_count, tile_ref, above_ref, below_ref, left_ref, right_ref):
    left = jnp.zeros(left_ref.shape, F32)
    right = left
    for n in range(5):
        first = pad_rows(n, tile_ref, above_ref, below_ref, pl.ds(0, LANES))
        last = pad_rows(n, tile_ref, above_ref, below_ref, pl.ds(col_count - LANES, LANES))
        for t in range(first.shape[0] // 8):
            at = 5 * t + n
            rows = slice(8 * t, 8 * t + 8)
            left = jnp.where(side_lanes(at), pltpu.roll(first[rows], 2 * at, 1), left)
            right = jnp.where(side_lanes(at), pltpu.roll(last[rows], 2 * at + 2, 1), right)
    left_ref[...] = left
    right_ref[...] = right


def flood_kernel(row_count, col_count, closed_ref, tile_ref, above_ref, below_ref, before_ref, after_ref, *outs):
    arrays = []
    for n in range(5):
        at = [5 * t + n for t in range(row_count // 8 + 2)]
        before = jnp.concatenate([pltpu.roll(before_ref[...], LANES - 2 - 2 * m, 1) for m in at], 0)
        after = jnp.concatenate([pltpu.roll(after_ref[...], (LANES - 2 * m) % LANES, 1) for m in at], 0)
        inner = pad_rows(n, tile_ref, above_ref, below_ref, slice(None))
        arrays.append(jnp.concatenate([before, inner, after], 1))
    depth, bed, first, second, wet = arrays
    shape = depth.shape
    row_at = lax.broadcasted_iota(jnp.int32, shape, 0) - 8
    col_at = lax.broadcasted_iota(jnp.int32, shape, 1) - LANES
    first_shut = (row_at == closed_ref[0]) | (row_at == closed_ref[1])
    second_shut = (col_at == closed_ref[2]) | (col_at == closed_ref[3])
    down = lambda x: pltpu.roll(x, shape[0] - 1, 0)
    up = lambda x: pltpu.roll(x, 1, 0)
    onward = lambda x: pltpu.roll(x, shape[1] - 1, 1)
    back = lambda x: pltpu.roll(x, 1, 1)
    bed_down = down(bed)
    bed_onward = onward(bed)
    for _ in range(2):
        eta = bed + depth
        first = jnp.where(first_shut, 0.0, face_flux(eta, down(eta), bed, bed_down, first))
        second = jnp.where(second_shut, 0.0, face_flux(eta, onward(eta), bed, bed_onward, second))
        depth = depth + wet * (up(first) - first + (back(second) - second))
    here = (slice(8, 8 + row_count), slice(LANES, LANES + col_count))
    for out, value in zip(outs, (depth, first, second)):
        out[...] = value[here]


def shifted(block, axis, step):
    count = lax.axis_size(axis)
    return lax.ppermute(block, axis, [(i, (i + step) % count) for i in range(count)])


def exchanged(block, axis, step):
    return lax.ppermute(block, axis, [(i, i ^ (1 << step)) for i in range(lax.axis_size(axis))])


def swapped(left, right, position, count):
    odd = position % 2 == 1
    inner = [(i, i ^ 1) for i in range(count)]
    outer = [(0, 0), (count - 1, count - 1)]
    for i in range(1, count - 1, 2):
        outer += [(i, i + 1), (i + 1, i)]
    one = lax.ppermute(jnp.where(odd, left, right), "col", inner)
    two = lax.ppermute(jnp.where(odd, right, left), "col", outer)
    return jnp.where(odd, one, two), jnp.where(odd, two, one)


def local(
    river_lower,
    river_main,
    river_upper,
    river_rhs,
    weir_crest,
    weir_regime,
    weir_tile,
    weir_row,
    weir_col,
    bed_level,
    water_depth,
    flux_first,
    flux_second,
    wet_mask,
):
    sections, chains = weir_crest.shape
    row_count, col_count = water_depth.shape
    row_size = lax.axis_size("row")
    col_size = lax.axis_size("col")
    row_at = lax.axis_index("row")
    col_at = lax.axis_index("col")
    tiles = row_size * col_size
    weirs = sections * chains
    capacity = 2 * weirs // tiles
    lane_rows = chains // LANES

    def block_rows(array):
        split = array.reshape(sections, 2, 2, lane_rows, LANES)
        return split.transpose(0, 1, 3, 2, 4).reshape(-1, LANES)

    rhs_rows = river_rhs.reshape(sections, 2, lane_rows, LANES).transpose(0, 2, 1, 3).reshape(-1, LANES)
    rows = weirs // LANES
    high_count = tiles * capacity // LOW
    rows_each = capacity // LANES
    river_block = pltpu.VMEM((sections * 4 * lane_rows, LANES), F32)
    solved, packed = pl.pallas_call(
        functools.partial(solve_kernel, sections),
        out_shape=(
            jax.ShapeDtypeStruct((sections, 10, lane_rows, LANES), F32),
            jax.ShapeDtypeStruct((20, lane_rows, LANES), F32),
        ),
        in_specs=[ANY] * 4,
        out_specs=(VMEM, VMEM),
        scratch_shapes=[
            river_block,
            river_block,
            river_block,
            pltpu.VMEM((sections * 2 * lane_rows, LANES), F32),
            pltpu.SemaphoreType.DMA((4,)),
        ],
        compiler_params=WIDE,
        name="solve",
    )(block_rows(river_lower), block_rows(river_main), block_rows(river_upper), rhs_rows)
    steps = row_size.bit_length() - 1
    slots = pl.pallas_call(
        functools.partial(rank_kernel, tiles, capacity, sections * lane_rows // 8),
        out_shape=jax.ShapeDtypeStruct((rows, LANES), jnp.int32),
        in_specs=[ANY],
        out_specs=VMEM,
        scratch_shapes=[pltpu.VMEM((rows, LANES), jnp.int32), pltpu.SemaphoreType.DMA((1,))],
        compiler_params=PARAMS,
        cost_estimate=pl.CostEstimate(flops=2 * tiles * weirs * LOW, bytes_accessed=2**17, transcendentals=0),
        name="rank",
    )(weir_tile.reshape(rows, LANES))
    group, known = packed, ()
    for step in range(steps - 1):
        other = exchanged(group, "row", step)
        twenty = jax.ShapeDtypeStruct((20, lane_rows, LANES), F32)
        group, own_map, sent = pl.pallas_call(
            functools.partial(merge_kernel, step, step == 0),
            out_shape=(twenty, twenty, jax.ShapeDtypeStruct((6, lane_rows, LANES), F32)),
            in_specs=[SMEM] + [VMEM] * (2 + len(known)),
            out_specs=(VMEM, VMEM, VMEM),
            compiler_params=PARAMS,
            name="merge",
        )(row_at.reshape(1), group, other, *known)
        known = (own_map,)
    met = exchanged(sent, "row", steps - 1)
    cells = pl.pallas_call(
        functools.partial(cell_kernel, tiles, capacity, sections * lane_rows // 8, row_count),
        out_shape=jax.ShapeDtypeStruct((tiles, rows_each, LANES), F32),
        in_specs=[VMEM] + [ANY] * 3,
        out_specs=VMEM,
        scratch_shapes=[
            pltpu.VMEM((sections, chains), jnp.int32),
            pltpu.VMEM((sections, chains), jnp.int32),
            pltpu.VMEM((2 * high_count, LOW), F32),
            pltpu.SemaphoreType.DMA((2,)),
        ],
        compiler_params=PARAMS,
        cost_estimate=pl.CostEstimate(flops=4 * high_count * LOW * weirs, bytes_accessed=2**18, transcendentals=0),
        name="cells",
    )(slots, weir_row, weir_col, sent)
    state_shape = jax.ShapeDtypeStruct((sections * lane_rows * 2, LANES), F32)
    state_rows, outgoing = pl.pallas_call(
        functools.partial(weir_kernel, sections, steps, tiles, capacity),
        out_shape=(state_shape, jax.ShapeDtypeStruct((tiles, 3 * rows_each, LANES), F32)),
        in_specs=[SMEM] + [VMEM] * 6 + [ANY] * 2,
        out_specs=(ANY, VMEM),
        scratch_shapes=[
            pltpu.VMEM((sections, chains), F32),
            pltpu.VMEM((sections, chains), jnp.int32),
            pltpu.VMEM(state_shape.shape, F32),
            pltpu.VMEM((rows, LANES), F32),
            pltpu.VMEM((4 * high_count, LOW), F32),
            pltpu.SemaphoreType.DMA((3,)),
        ],
        compiler_params=PARAMS,
        name="weirs",
    )(row_at.reshape(1), sent, met, own_map, solved, slots, cells, weir_crest, weir_regime)
    river_state = (
        state_rows.reshape(sections, lane_rows, 2, LANES).transpose(0, 2, 1, 3).reshape(sections, 2, chains)
    )
    arrived = lax.all_to_all(outgoing, ("row", "col"), split_axis=0, concat_axis=0, tiled=True)
    strip = jax.ShapeDtypeStruct((8, col_count), F32)
    tile, top, bottom = pl.pallas_call(
        functools.partial(apply_kernel, tiles, rows_each, row_count, col_count),
        out_shape=(jax.ShapeDtypeStruct((5, row_count, col_count), F32), strip, strip),
        in_specs=[VMEM] + [ANY] * 5,
        out_specs=(VMEM, VMEM, VMEM),
        scratch_shapes=[
            pltpu.VMEM((row_count, col_count), F32),
            pltpu.VMEM((row_count, col_count), jnp.int32),
            pltpu.VMEM((4 * row_count * col_count // LOW, LOW), F32),
            pltpu.SemaphoreType.DMA((5,)),
        ],
        compiler_params=PARAMS,
        name="apply",
    )(arrived, bed_level, water_depth, flux_first, flux_second, wet_mask)
    above = shifted(bottom, "row", 1)
    below = shifted(top, "row", -1)
    side = jax.ShapeDtypeStruct((8, LANES), F32)
    left, right = pl.pallas_call(
        functools.partial(sides_kernel, col_count),
        out_shape=(side, side),
        in_specs=[VMEM] * 3,
        out_specs=(VMEM, VMEM),
        compiler_params=PARAMS,
        name="sides",
    )(tile, above, below)
    before, after = swapped(left, right, col_at, col_size)
    closed = jnp.stack(
        [
            jnp.where(row_at == 0, -1, -9),
            jnp.where(row_at == row_size - 1, row_count - 1, -9),
            jnp.where(col_at == 0, -1, -LANES - 1),
            jnp.where(col_at == col_size - 1, col_count - 1, -LANES - 1),
        ]
    ).astype(jnp.int32)
    tile_out = jax.ShapeDtypeStruct((row_count, col_count), F32)
    depth_out, first_out, second_out = pl.pallas_call(
        functools.partial(flood_kernel, row_count, col_count),
        out_shape=(tile_out, tile_out, tile_out),
        in_specs=[SMEM] + [VMEM] * 5,
        out_specs=(VMEM, VMEM, VMEM),
        compiler_params=PARAMS,
        name="flood",
    )(closed, tile, above, below, before, after)
    return (river_state, depth_out, first_out, second_out)


def solution(mesh):
    in_specs = (
        P("row", None, None, "col"),
        P("row", None, None, "col"),
        P("row", None, None, "col"),
        P("row", None, "col"),
        P("row", "col"),
        P("row", "col"),
        P("row", "col", None, None, None),
        P("row", "col"),
        P("row", "col"),
        P("row", "col"),
        P("row", "col"),
        P("row", "col"),
        P("row", "col"),
        P("row", "col"),
    )
    out_specs = (P("row", None, "col"), P("row", "col"), P("row", "col"), P("row", "col"))
    return jax.shard_map(local, mesh=mesh, in_specs=in_specs, out_specs=out_specs, check_vma=False)
```

```python
import functools

import jax
import jax.numpy as jnp
from jax import lax
from jax.experimental import pallas as pl
from jax.experimental.pallas import tpu as pltpu
from jax.sharding import PartitionSpec as P

GRAVITY = 9.81
TIME_STEP = 1.0
CELL_WIDTH = 10.0
MANNING_SQ = 0.0009
DEPTH_FLOOR = 0.05
WEIR_GAIN = 0.5
FREE_COEF = 0.5
SUB_COEF = 0.4
SUB_OFFSET = 0.25
GATE_COEF = 0.2

F32 = jnp.float32
BF16 = jnp.bfloat16
LANES = 128
LOW = 256
VMEM = pl.BlockSpec(memory_space=pltpu.VMEM)
SMEM = pl.BlockSpec(memory_space=pltpu.SMEM)
ANY = pl.BlockSpec(memory_space=pl.ANY)
PARAMS = pltpu.CompilerParams(vmem_limit_bytes=40 * 2**20)
WIDE = pltpu.CompilerParams(vmem_limit_bytes=60 * 2**20)


def start_copies(sources, targets, sems):
    copies = [pltpu.make_async_copy(s, t, sems.at[n]) for n, (s, t) in enumerate(zip(sources, targets))]
    for copy in copies:
        copy.start()
    return copies


def mat_mat(a, b):
    return [[a[i][0] * b[0][j] + a[i][1] * b[1][j] for j in range(2)] for i in range(2)]


def mat_vec(a, v):
    return [a[i][0] * v[0] + a[i][1] * v[1] for i in range(2)]


def mat_sub(a, b):
    return [[a[i][j] - b[i][j] for j in range(2)] for i in range(2)]


def mat_neg(a):
    return [[-a[i][j] for j in range(2)] for i in range(2)]


def mat_inv(m):
    scale = 1.0 / (m[0][0] * m[1][1] - m[0][1] * m[1][0])
    return [[m[1][1] * scale, -m[0][1] * scale], [-m[1][0] * scale, m[0][0] * scale]]


def solve_kernel(sections, *refs):
    solved_ref, packed_ref = refs[4:6]
    lower_ref, main_ref, upper_ref, rhs_ref = refs[6:10]
    pieces = []
    for n in range(4):
        parts = [[r.at[pl.ds(n * r.shape[0] // 4, r.shape[0] // 4)] for r in group] for group in (refs[:4], refs[6:10])]
        pieces.append(start_copies(*parts, refs[10].at[n]))

    def block(ref, k):
        return [[ref[pl.ds(k * 32 + i * 16 + j, 8, stride=2), :] for j in range(2)] for i in range(2)]

    couples = []
    for k in range(sections):
        if k % (sections // 4) == 0:
            for copy in pieces[k // (sections // 4)]:
                copy.wait()
        lower = block(lower_ref, k)
        main = block(main_ref, k)
        upper = block(upper_ref, k)
        right = [rhs_ref[pl.ds(k * 16 + j, 8, stride=2), :] for j in range(2)]
        if k == 0:
            inverse = mat_inv(main)
            left = mat_neg(mat_mat(inverse, lower))
            value = mat_vec(inverse, right)
        else:
            inverse = mat_inv(mat_sub(main, mat_mat(lower, couples[-1])))
            left = mat_neg(mat_mat(inverse, mat_mat(lower, left)))
            moved = mat_vec(lower, value)
            value = mat_vec(inverse, [right[i] - moved[i] for i in range(2)])
        couples.append(mat_mat(inverse, upper))
        for i in range(2):
            solved_ref[k, i] = value[i]
            for j in range(2):
                solved_ref[k, 2 + 2 * i + j] = left[i][j]
    spike = mat_neg(couples[-1])
    tail = (value, left, spike)
    for i in range(2):
        for j in range(2):
            solved_ref[sections - 1, 6 + 2 * i + j] = spike[i][j]
    for k in range(sections - 2, -1, -1):
        couple = couples[k]
        after = mat_vec(couple, value)
        value = [solved_ref[k, i] - after[i] for i in range(2)]
        after = mat_mat(couple, left)
        left = [[solved_ref[k, 2 + 2 * i + j] - after[i][j] for j in range(2)] for i in range(2)]
        spike = mat_neg(mat_mat(couple, spike))
        for i in range(2):
            solved_ref[k, i] = value[i]
            for j in range(2):
                solved_ref[k, 2 + 2 * i + j] = left[i][j]
                solved_ref[k, 6 + 2 * i + j] = spike[i][j]
    for i in range(2):
        packed_ref[i] = value[i]
        packed_ref[2 + i] = tail[0][i]
        for j in range(2):
            packed_ref[4 + 2 * i + j] = left[i][j]
            packed_ref[8 + 2 * i + j] = tail[1][i][j]
            packed_ref[12 + 2 * i + j] = spike[i][j]
            packed_ref[16 + 2 * i + j] = tail[2][i][j]


def load_pair(ref, n):
    return [ref[n], ref[n + 1]]


def load_square(ref, n):
    return [load_pair(ref, n), load_pair(ref, n + 2)]


def store_all(ref, values):
    flat = []
    for value in values:
        flat += [*value[0], *value[1]] if isinstance(value[0], list) else value
    for n, item in enumerate(flat):
        ref[n] = item


def pick(flag, one, other):
    if isinstance(one, list):
        return [pick(flag, a, b) for a, b in zip(one, other)]
    return jnp.where(flag, one, other)


def add(a, b):
    if isinstance(a, list):
        return [add(x, y) for x, y in zip(a, b)]
    return a + b


def meet(head_y, head_left, tail_y, tail_right):
    inner = mat_mat(head_left, tail_right)
    inverse = mat_inv([[1.0 - inner[0][0], -inner[0][1]], [-inner[1][0], 1.0 - inner[1][1]]])
    return inverse, mat_vec(inverse, add(head_y, mat_vec(head_left, tail_y)))


def merge_kernel(step, first, position_ref, own_ref, other_ref, *refs):
    known_ref = None if first else refs[0]
    group_ref, map_ref, send_ref = refs[-3:]
    position = position_ref[0]
    late = ((position >> step) & 1) == 1

    def group(ref):
        return [load_pair(ref, 0), load_pair(ref, 2)] + [load_square(ref, n) for n in (4, 8, 12, 16)]

    own, other = group(own_ref), group(other_ref)
    head_y, tail_y, head_left, tail_left, head_right, tail_right = pick(late, other, own)
    next_head_y, next_tail_y, next_head_left, next_tail_left, next_head_right, next_tail_right = pick(
        late, own, other
    )
    inverse, head = meet(next_head_y, next_head_left, tail_y, tail_right)
    head_before = mat_mat(inverse, mat_mat(next_head_left, tail_left))
    head_after = mat_mat(inverse, next_head_right)
    tail = add(tail_y, mat_vec(tail_right, head))
    tail_before = add(tail_left, mat_mat(tail_right, head_before))
    tail_after = mat_mat(tail_right, head_after)
    joined = [
        add(head_y, mat_vec(head_right, head)),
        add(next_tail_y, mat_vec(next_tail_left, tail)),
        add(head_left, mat_mat(head_right, head_before)),
        mat_mat(next_tail_left, tail_before),
        mat_mat(head_right, head_after),
        add(next_tail_right, mat_mat(next_tail_left, tail_after)),
    ]
    zero = jnp.zeros(tail[0].shape, F32)
    one = zero + 1.0
    unit, none, nothing = [[one, zero], [zero, one]], [[zero, zero], [zero, zero]], [zero, zero]
    if first:
        maps = [
            [pick(late, tail_before, unit), pick(late, tail_after, none), pick(late, tail, nothing)],
            [pick(late, none, head_before), pick(late, unit, head_after), pick(late, nothing, head)],
        ]
    else:
        maps = []
        for n in range(2):
            by_before = load_square(known_ref, 10 * n)
            by_after = load_square(known_ref, 10 * n + 4)
            value = load_pair(known_ref, 10 * n + 8)
            maps.append(
                [
                    pick(late, mat_mat(by_before, tail_before), add(by_before, mat_mat(by_after, head_before))),
                    pick(late, add(by_after, mat_mat(by_before, tail_after)), mat_mat(by_after, head_after)),
                    pick(late, add(value, mat_vec(by_before, tail)), add(value, mat_vec(by_after, head))),
                ]
            )
    store_all(group_ref, joined)
    store_all(map_ref, maps[0] + maps[1])
    later = ((position >> (step + 1)) & 1) == 1
    store_all(send_ref, [pick(later, joined[0], joined[1]), pick(later, joined[2], joined[5])])


def rows16(row):
    return jnp.broadcast_to(row, (16, LANES)).astype(BF16)


def table16(count):
    shape = (count // 16, 16, LANES)
    at = lax.broadcasted_iota(jnp.int32, shape, 0) * 16 + lax.broadcasted_iota(jnp.int32, shape, 1)
    return at.astype(F32).astype(BF16)


def halves(value):
    high = value.astype(BF16).astype(F32)
    return high, value - high


def one_hots(high, low, values, high_table, low_table):
    one = jnp.ones((), BF16)
    zero = jnp.zeros((), BF16)
    left, right = [], []
    for r in range(8):
        hit = high_table == rows16(high[r : r + 1])[None]
        left.append(
            jnp.concatenate(
                [jnp.where(hit, rows16(v[r : r + 1])[None], zero).reshape(-1, LANES) for v in values], 0
            )
        )
        hit = low_table == rows16(low[r : r + 1])[None]
        right.append(jnp.where(hit, one, zero).reshape(-1, LANES))
    return jnp.concatenate(left, 1), jnp.concatenate(right, 1)


def product(left, right):
    return lax.dot_general(left, right, (((1,), (1,)), ((), ())), preferred_element_type=F32)


def group_at(g):
    over = pl.multiple_of((g // 8) * 8, 8)
    along = pl.multiple_of((g % 8) * LANES, LANES)
    return (pl.ds(over, 8), pl.ds(along, LANES))


def fill_slots(high_count, groups, slot_ref, values, total_ref, side=None):
    if side is not None:
        capacity, side_code, side_ref = side
        tile_table = table16(high_count * LOW // capacity)
        side_table = table16(LANES)
        side_ref[...] = jnp.zeros_like(side_ref)
    high_table = table16(high_count)
    low_table = table16(LOW)
    total_ref[...] = jnp.zeros_like(total_ref)

    def body(g, carry):
        slot = slot_ref[pl.ds(pl.multiple_of(g * 8, 8), 8), :]
        value = values(g)
        left, right = one_hots(
            (slot // LOW).astype(F32), (slot % LOW).astype(F32), value, high_table, low_table
        )
        total_ref[...] += product(left, right)
        if side is not None:
            left, right = one_hots(
                (slot // capacity).astype(F32), side_code(g).astype(F32), value, tile_table, side_table
            )
            side_ref[...] += product(left, right)
        return carry

    lax.fori_loop(0, groups, body, 0, unroll=8)


def store_slots(tiles, capacity, total_ref, part, scale, out_ref, pitch, row):
    high_count = tiles * capacity // LOW
    per_tile = capacity // LOW
    first = total_ref[pl.ds(part * high_count, high_count), :]
    value = first * scale + total_ref[pl.ds((part + 1) * high_count, high_count), :]
    for t in range(tiles):
        for j in range(LOW // LANES):
            out_ref[pl.ds(t * pitch + row + j * per_tile, per_tile), :] = value[
                t * per_tile : (t + 1) * per_tile, j * LANES : (j + 1) * LANES
            ]


def rank_kernel(tiles, capacity, groups, tile_in, slot_ref, tile_ref, sems):
    start_copies((tile_in,), (tile_ref,), sems)[0].wait()
    table = lax.broadcasted_iota(jnp.int32, (tiles, LANES), 0)
    row_at = lax.broadcasted_iota(jnp.int32, (LANES, 2 * LANES), 0)
    col_at = lax.broadcasted_iota(jnp.int32, (LANES, 2 * LANES), 1)
    earlier = jnp.where(row_at < col_at, 1.0, 0.0).astype(BF16)

    def body(g, offset):
        ids = tile_ref[pl.ds((g // 8) * 64 + g % 8, 8, stride=8), :]
        hits = [ids[r : r + 1, :] == table for r in range(8)]
        hot = jnp.concatenate([jnp.where(h, 1.0, 0.0).astype(BF16) for h in hits], 0)
        counts = jnp.dot(hot, earlier, preferred_element_type=F32)
        rows = []
        for r in range(8):
            part = counts[r * tiles : (r + 1) * tiles]
            place = jnp.where(hits[r], part[:, :LANES] + offset, 0.0)
            rows.append(jnp.sum(place, axis=0, keepdims=True))
            offset = offset + part[:, LANES:]
        slot_ref[pl.ds(g * 8, 8), :] = jnp.concatenate(rows, 0).astype(jnp.int32)
        return offset

    lax.fori_loop(0, groups, body, table.astype(F32) * capacity, unroll=4)


def cell_kernel(tiles, capacity, groups, row_count, slot_ref, row_in, col_in, after, cells_ref, *refs):
    row_ref, col_ref, total_ref, sems = refs
    for copy in start_copies((row_in, col_in), (row_ref, col_ref), sems):
        copy.wait()

    def values(g):
        col = col_ref[group_at(g)]
        high = (col // LOW) * row_count + row_ref[group_at(g)]
        return [high.astype(F32), (col % LOW).astype(F32)]

    fill_slots(tiles * capacity // LOW, groups, slot_ref, values, total_ref)
    store_slots(tiles, capacity, total_ref, 0, float(LOW), cells_ref, capacity // LANES, 0)


def weir_kernel(sections, steps, tiles, capacity, row_count, col_count, *refs):
    position_ref, own_ref, other_ref, map_ref = refs[:4]
    solved_ref, slot_ref, cells_ref = refs[4:7]
    state_out, out_ref = refs[11:13]
    crest_ref, regime_ref, row_ref, col_ref, state_ref, phase_ref, total_ref, side_ref, sems = refs[13:]
    copies = start_copies(refs[7:11], (crest_ref, regime_ref, row_ref, col_ref), sems)
    late = ((position_ref[0] >> (steps - 1)) & 1) == 1
    own = [load_pair(own_ref, 0), load_square(own_ref, 2)]
    other = [load_pair(other_ref, 0), load_square(other_ref, 2)]
    tail_y, tail_right = pick(late, other, own)
    head_y, head_left = pick(late, own, other)
    head = meet(head_y, head_left, tail_y, tail_right)[1]
    tail = add(tail_y, mat_vec(tail_right, head))
    zero = jnp.zeros(tail[0].shape, F32)
    outer_before = pick(late, tail, [zero, zero])
    outer_after = pick(late, [zero, zero], head)
    before, after = (
        add(
            load_pair(map_ref, n + 8),
            add(
                mat_vec(load_square(map_ref, n), outer_before),
                mat_vec(load_square(map_ref, n + 4), outer_after),
            ),
        )
        for n in (0, 10)
    )
    for k in range(sections):
        for i in range(2):
            state = solved_ref[k, i]
            for j in range(2):
                state = state + solved_ref[k, 2 + 2 * i + j] * before[j]
                state = state + solved_ref[k, 6 + 2 * i + j] * after[j]
            state_ref[pl.ds(k * 16 + i, 8, stride=2), :] = state
            if i == 0:
                phase_ref[pl.ds((k // 8) * 64 + k % 8, 8, stride=8), :] = state

    state_copy = pltpu.make_async_copy(state_ref, state_out, sems.at[4])
    state_copy.start()
    for copy in copies:
        copy.wait()

    def values(g):
        phase = phase_ref[pl.ds(pl.multiple_of(g * 8, 8), 8), :]
        regime = regime_ref[group_at(g)]
        head = jnp.maximum(phase - crest_ref[group_at(g)], 0.0)
        free = jnp.where(regime == 0, FREE_COEF * head * jnp.sqrt(head), 0.0)
        sub = jnp.where(
            regime == 1,
            SUB_COEF * jnp.sqrt(head + SUB_OFFSET),
            jnp.where(regime == 2, GATE_COEF, 0.0),
        )
        return [*halves(WEIR_GAIN * (free + sub * phase)), *halves(WEIR_GAIN * sub)]

    def side_code(g):
        col = col_ref[group_at(g)]
        place = jnp.where(col < 2, col, jnp.where(col >= col_count - 2, col - (col_count - 4), -1))
        return jnp.where(place >= 0, place * row_count + row_ref[group_at(g)], -1)

    side = (capacity, side_code, side_ref)
    fill_slots(tiles * capacity // LOW, sections, slot_ref, values, total_ref, side)
    rows_each = capacity // LANES
    pitch = 3 * rows_each + 2
    at = lax.broadcasted_iota(jnp.int32, (tiles, LANES), 1)
    first_cols = at < 2 * row_count
    for v in range(2):
        store_slots(tiles, capacity, total_ref, 2 * v, 1.0, out_ref, pitch, v * rows_each)
        sums = side_ref[pl.ds(2 * v * tiles, tiles), :] + side_ref[pl.ds((2 * v + 1) * tiles, tiles), :]
        beside = jnp.where(first_cols, pltpu.roll(sums, tiles - 1, 0), pltpu.roll(sums, 1, 0))
        out_ref[pl.ds(3 * rows_each + v, tiles, stride=pitch), :] = beside
    for t in range(tiles):
        out_ref[pl.ds(t * pitch + 2 * rows_each, rows_each), :] = cells_ref[pl.ds(t * rows_each, rows_each), :]
    state_copy.wait()


def side_lanes(n):
    at = lax.broadcasted_iota(jnp.int32, (8, LANES), 1)
    return (at == 2 * n) | (at == 2 * n + 1)


def stage_kernel(row_count, col_count, *refs):
    tile_ref, left_ref, right_ref, wet_ref, sems = refs[6:]
    for copy in start_copies(refs[:5], [tile_ref.at[n] for n in range(4)] + [wet_ref], sems):
        copy.wait()
    tile_ref[4] = wet_ref[...].astype(F32) * (TIME_STEP / CELL_WIDTH)
    left = jnp.zeros(left_ref.shape, F32)
    right = left
    for t in range(row_count // 8):
        for n in range(5):
            at = 5 * t + n
            first = tile_ref[n, pl.ds(8 * t, 8), pl.ds(0, LANES)]
            last = tile_ref[n, pl.ds(8 * t, 8), pl.ds(col_count - LANES, LANES)]
            left = jnp.where(side_lanes(at), pltpu.roll(first, 2 * at, 1), left)
            right = jnp.where(side_lanes(at), pltpu.roll(last, 2 * at + 2, 1), right)
    left_ref[...] = left
    right_ref[...] = right


def unpacked(strip, n, rows, lane):
    parts = [pltpu.roll(strip, (lane - 2 * (5 * t + n)) % LANES, 1) for t in range(rows // 8)]
    return jnp.concatenate(parts, 0)


def apply_kernel(sources, rows_each, row_count, col_count, *refs):
    in_ref, tile_ref, before_ref, after_ref = refs[:4]
    depth_ref, top_ref, bottom_ref, left_ref, right_ref, total_ref = refs[4:]
    pitch = 3 * rows_each + 2
    high_count = row_count * col_count // LOW
    high_table = table16(high_count)
    low_table = table16(LOW)
    total_ref[...] = jnp.zeros_like(total_ref)
    step = 8 // rows_each if rows_each < 8 else 1

    def body(g, carry):
        def part(v):
            return jnp.concatenate(
                [in_ref[pl.ds((g * step + n) * pitch + v * rows_each, rows_each), :] for n in range(step)], 0
            )

        cell = part(2).astype(jnp.int32)
        left, right = one_hots(
            (cell // LOW).astype(F32),
            (cell % LOW).astype(F32),
            [*halves(part(0)), *halves(part(1))],
            high_table,
            low_table,
        )
        total_ref[...] += product(left, right)
        return carry

    lax.fori_loop(0, sources // step, body, 0, unroll=8)
    for n in range(col_count // LOW):
        def summed(v):
            start = 2 * v * high_count + n * row_count
            return total_ref[pl.ds(start, row_count), :] + total_ref[pl.ds(start + high_count, row_count), :]

        cols = pl.ds(n * LOW, LOW)
        depth = tile_ref[0, :, cols]
        surface = tile_ref[1, :, cols] + depth
        depth_ref[:, cols] = jnp.maximum(depth + (summed(0) - summed(1) * surface), 0.0)
    row_at = lax.broadcasted_iota(jnp.int32, (row_count, LANES), 0)
    col_at = lax.broadcasted_iota(jnp.int32, (row_count, LANES), 1)

    def columns(v, lane, place):
        sums = jnp.sum(in_ref[pl.ds(3 * rows_each + v, sources, stride=pitch), :], axis=0, keepdims=True)
        result = jnp.zeros((row_count, LANES), F32)
        for i in range(2):
            wanted = col_at == (place + i) * row_count + row_at
            column = jnp.sum(jnp.where(wanted, sums, 0.0), axis=1, keepdims=True)
            result = jnp.where(col_at == lane + i, column, result)
        return result

    edges = ((top_ref, 0, (0, 1)), (bottom_ref, row_count - 1, (row_count - 2, row_count - 1)))
    lane_at = lax.broadcasted_iota(jnp.int32, (1, LANES), 1)
    corners = {(i, j): jnp.zeros((1, LANES), F32) for i in range(2) for j in range(2)}
    for out, strip_ref, lane, place in ((left_ref, before_ref, LANES - 2, 2), (right_ref, after_ref, 0, 0)):
        strip = strip_ref[...]
        arrays = [unpacked(strip, n, row_count, lane) for n in range(5)]
        surface = arrays[1] + arrays[0]
        constant, slope = columns(0, lane, place), columns(1, lane, place)
        arrays[0] = jnp.maximum(arrays[0] + (constant - slope * surface), 0.0)
        for n in range(5):
            out[n] = arrays[n]
            start = 2 * n + (LANES // 2 if place == 0 else 0)
            mine = (lane_at == start) | (lane_at == start + 1)
            for i, (_, _, rows) in enumerate(edges):
                for j in range(2):
                    moved = pltpu.roll(arrays[n][rows[j] : rows[j] + 1], (start - lane) % LANES, 1)
                    corners[i, j] = jnp.where(mine, moved, corners[i, j])
    cols = pl.ds(0, col_count)
    for i, (out, near, rows) in enumerate(edges):
        for j in range(2):
            out[pl.ds(j, 1), cols] = depth_ref[pl.ds(rows[j], 1), :]
            for n in (1, 2):
                out[pl.ds(2 * n + j, 1), cols] = tile_ref[n, pl.ds(rows[j], 1), :]
            out[pl.ds(j, 1), pl.ds(col_count, LANES)] = corners[i, j]
        for n in (3, 4):
            out[pl.ds(3 + n, 1), cols] = tile_ref[n, pl.ds(near, 1), :]
        out[pl.ds(2, 6), pl.ds(col_count, LANES)] = jnp.zeros((6, LANES), F32)


def face_flux(eta_here, eta_next, bed_here, bed_next, old_flux):
    flow_depth = jnp.maximum(
        jnp.maximum(eta_here, eta_next) - jnp.maximum(bed_here, bed_next), DEPTH_FLOOR
    )
    gradient = (eta_next - eta_here) / CELL_WIDTH
    pushed = old_flux - GRAVITY * TIME_STEP * flow_depth * gradient
    friction = jnp.exp((-7.0 / 3.0) * jnp.log(flow_depth))
    return pushed / (1.0 + GRAVITY * TIME_STEP * MANNING_SQ * jnp.abs(old_flux) * friction)


def halo_rows(n, ref, start, cols):
    at = lax.broadcasted_iota(jnp.int32, (8, 1), 0)
    row = 2 * n if n < 3 else 3 + n
    one = ref[pl.ds(row, 1), cols]
    two = ref[pl.ds(row + 1, 1), cols] if n < 3 else one
    return jnp.where(at == start, one, jnp.where(at == start + 1, two, 0.0))


def corner_rows(n, ref, start, cols, lane, place):
    at = lax.broadcasted_iota(jnp.int32, (8, 1), 0)
    shift = (lane - 2 * n - place) % LANES
    one, two = (pltpu.roll(ref[pl.ds(j, 1), cols], shift, 1) for j in range(2))
    return jnp.where(at == start, one, jnp.where(at == start + 1, two, 0.0))


def flood_kernel(row_count, col_count, *refs):
    closed_ref, tile_ref, depth_ref, left_ref, right_ref, above_ref, below_ref = refs[:7]
    outs = refs[7:]
    inner = pl.ds(0, col_count)
    outer = pl.ds(col_count, LANES)
    arrays = []
    for n in range(5):
        columns = []
        for ref, lane, place in ((left_ref, LANES - 2, 0), (None, 0, 0), (right_ref, 0, LANES // 2)):
            if ref is None:
                low = halo_rows(n, above_ref, 6, inner)
                own = depth_ref[...] if n == 0 else tile_ref[n]
                high = halo_rows(n, below_ref, 0, inner)
            else:
                low = corner_rows(n, above_ref, 6, outer, lane, place)
                own = ref[n]
                high = corner_rows(n, below_ref, 0, outer, lane, place)
            columns.append(jnp.concatenate([low, own, high], 0))
        arrays.append(jnp.concatenate(columns, 1))
    depth, bed, first, second, wet = arrays
    shape = depth.shape
    row_at = lax.broadcasted_iota(jnp.int32, shape, 0) - 8
    col_at = lax.broadcasted_iota(jnp.int32, shape, 1) - LANES
    first_shut = (row_at == closed_ref[0]) | (row_at == closed_ref[1])
    second_shut = (col_at == closed_ref[2]) | (col_at == closed_ref[3])
    down = lambda x: pltpu.roll(x, shape[0] - 1, 0)
    up = lambda x: pltpu.roll(x, 1, 0)
    onward = lambda x: pltpu.roll(x, shape[1] - 1, 1)
    back = lambda x: pltpu.roll(x, 1, 1)
    bed_down = down(bed)
    bed_onward = onward(bed)
    for _ in range(2):
        eta = bed + depth
        first = jnp.where(first_shut, 0.0, face_flux(eta, down(eta), bed, bed_down, first))
        second = jnp.where(second_shut, 0.0, face_flux(eta, onward(eta), bed, bed_onward, second))
        depth = depth + wet * (up(first) - first + (back(second) - second))
    here = (slice(8, 8 + row_count), slice(LANES, LANES + col_count))
    for out, value in zip(outs, (depth, first, second)):
        out[...] = value[here]


def shifted(block, axis, step):
    count = lax.axis_size(axis)
    return lax.ppermute(block, axis, [(i, (i + step) % count) for i in range(count)])


def exchanged(block, axis, step):
    return lax.ppermute(block, axis, [(i, i ^ (1 << step)) for i in range(lax.axis_size(axis))])


def swapped(left, right, position, count):
    odd = position % 2 == 1
    inner = [(i, i ^ 1) for i in range(count)]
    outer = [(0, 0), (count - 1, count - 1)]
    for i in range(1, count - 1, 2):
        outer += [(i, i + 1), (i + 1, i)]
    one = lax.ppermute(jnp.where(odd, left, right), "col", inner)
    two = lax.ppermute(jnp.where(odd, right, left), "col", outer)
    return jnp.where(odd, one, two), jnp.where(odd, two, one)


def local(
    river_lower,
    river_main,
    river_upper,
    river_rhs,
    weir_crest,
    weir_regime,
    weir_tile,
    weir_row,
    weir_col,
    bed_level,
    water_depth,
    flux_first,
    flux_second,
    wet_mask,
):
    sections, chains = weir_crest.shape
    row_count, col_count = water_depth.shape
    row_size = lax.axis_size("row")
    col_size = lax.axis_size("col")
    row_at = lax.axis_index("row")
    col_at = lax.axis_index("col")
    tiles = row_size * col_size
    weirs = sections * chains
    capacity = 2 * weirs // tiles
    lane_rows = chains // LANES

    def block_rows(array):
        split = array.reshape(sections, 2, 2, lane_rows, LANES)
        return split.transpose(0, 1, 3, 2, 4).reshape(-1, LANES)

    rhs_rows = river_rhs.reshape(sections, 2, lane_rows, LANES).transpose(0, 2, 1, 3).reshape(-1, LANES)
    rows = weirs // LANES
    high_count = tiles * capacity // LOW
    rows_each = capacity // LANES
    pitch = 3 * rows_each + 2
    river_block = pltpu.VMEM((sections * 4 * lane_rows, LANES), F32)
    solved, packed = pl.pallas_call(
        functools.partial(solve_kernel, sections),
        out_shape=(
            jax.ShapeDtypeStruct((sections, 10, lane_rows, LANES), F32),
            jax.ShapeDtypeStruct((20, lane_rows, LANES), F32),
        ),
        in_specs=[ANY] * 4,
        out_specs=(VMEM, VMEM),
        scratch_shapes=[
            river_block,
            river_block,
            river_block,
            pltpu.VMEM((sections * 2 * lane_rows, LANES), F32),
            pltpu.SemaphoreType.DMA((4, 4)),
        ],
        compiler_params=WIDE,
        name="solve",
    )(block_rows(river_lower), block_rows(river_main), block_rows(river_upper), rhs_rows)
    steps = row_size.bit_length() - 1
    slots = pl.pallas_call(
        functools.partial(rank_kernel, tiles, capacity, sections * lane_rows // 8),
        out_shape=jax.ShapeDtypeStruct((rows, LANES), jnp.int32),
        in_specs=[ANY],
        out_specs=VMEM,
        scratch_shapes=[pltpu.VMEM((rows, LANES), jnp.int32), pltpu.SemaphoreType.DMA((1,))],
        compiler_params=PARAMS,
        cost_estimate=pl.CostEstimate(flops=2 * tiles * weirs * LOW, bytes_accessed=2**17, transcendentals=0),
        name="rank",
    )(weir_tile.reshape(rows, LANES))
    group, known = packed, ()
    for step in range(steps - 1):
        other = exchanged(group, "row", step)
        twenty = jax.ShapeDtypeStruct((20, lane_rows, LANES), F32)
        group, own_map, sent = pl.pallas_call(
            functools.partial(merge_kernel, step, step == 0),
            out_shape=(twenty, twenty, jax.ShapeDtypeStruct((6, lane_rows, LANES), F32)),
            in_specs=[SMEM] + [VMEM] * (2 + len(known)),
            out_specs=(VMEM, VMEM, VMEM),
            compiler_params=PARAMS,
            name="merge",
        )(row_at.reshape(1), group, other, *known)
        known = (own_map,)
    met = exchanged(sent, "row", steps - 1)
    cells = pl.pallas_call(
        functools.partial(cell_kernel, tiles, capacity, sections * lane_rows // 8, row_count),
        out_shape=jax.ShapeDtypeStruct((tiles * rows_each, LANES), F32),
        in_specs=[VMEM] + [ANY] * 3,
        out_specs=VMEM,
        scratch_shapes=[
            pltpu.VMEM((sections, chains), jnp.int32),
            pltpu.VMEM((sections, chains), jnp.int32),
            pltpu.VMEM((2 * high_count, LOW), F32),
            pltpu.SemaphoreType.DMA((2,)),
        ],
        compiler_params=PARAMS,
        cost_estimate=pl.CostEstimate(flops=4 * high_count * LOW * weirs, bytes_accessed=2**18, transcendentals=0),
        name="cells",
    )(slots, weir_row, weir_col, sent)
    state_shape = jax.ShapeDtypeStruct((sections * lane_rows * 2, LANES), F32)
    state_rows, outgoing = pl.pallas_call(
        functools.partial(weir_kernel, sections, steps, tiles, capacity, row_count, col_count),
        out_shape=(state_shape, jax.ShapeDtypeStruct((tiles * pitch, LANES), F32)),
        in_specs=[SMEM] + [VMEM] * 6 + [ANY] * 4,
        out_specs=(ANY, VMEM),
        scratch_shapes=[
            pltpu.VMEM((sections, chains), F32),
            pltpu.VMEM((sections, chains), jnp.int32),
            pltpu.VMEM((sections, chains), jnp.int32),
            pltpu.VMEM((sections, chains), jnp.int32),
            pltpu.VMEM(state_shape.shape, F32),
            pltpu.VMEM((rows, LANES), F32),
            pltpu.VMEM((4 * high_count, LOW), F32),
            pltpu.VMEM((4 * tiles, LANES), F32),
            pltpu.SemaphoreType.DMA((5,)),
        ],
        compiler_params=PARAMS,
        name="weirs",
    )(row_at.reshape(1), sent, met, own_map, solved, slots, cells, weir_crest, weir_regime, weir_row, weir_col)
    river_state = (
        state_rows.reshape(sections, lane_rows, 2, LANES).transpose(0, 2, 1, 3).reshape(sections, 2, chains)
    )
    messages = outgoing.reshape(tiles, pitch, 1, LANES)
    arrived = lax.all_to_all(messages, ("row", "col"), split_axis=0, concat_axis=0, tiled=True)
    tile_stack = jax.ShapeDtypeStruct((5, row_count, col_count), F32)
    side = jax.ShapeDtypeStruct((8, LANES), F32)
    tile, left, right = pl.pallas_call(
        functools.partial(stage_kernel, row_count, col_count),
        out_shape=(tile_stack, side, side),
        in_specs=[ANY] * 6,
        out_specs=(VMEM, VMEM, VMEM),
        scratch_shapes=[pltpu.VMEM((row_count, col_count), jnp.int32), pltpu.SemaphoreType.DMA((5,))],
        compiler_params=PARAMS,
        name="stage",
    )(water_depth, bed_level, flux_first, flux_second, wet_mask, outgoing)
    before, after = swapped(left, right, col_at, col_size)
    tile_out = jax.ShapeDtypeStruct((row_count, col_count), F32)
    edge = jax.ShapeDtypeStruct((8, col_count + LANES), F32)
    flank = jax.ShapeDtypeStruct((5, row_count, LANES), F32)
    wetted, top, bottom, left, right = pl.pallas_call(
        functools.partial(apply_kernel, tiles, rows_each, row_count, col_count),
        out_shape=(tile_out, edge, edge, flank, flank),
        in_specs=[VMEM] * 4,
        out_specs=(VMEM,) * 5,
        scratch_shapes=[pltpu.VMEM((4 * row_count * col_count // LOW, LOW), F32)],
        compiler_params=PARAMS,
        name="apply",
    )(arrived.reshape(tiles * pitch, LANES), tile, before, after)
    above = shifted(bottom, "row", 1)
    below = shifted(top, "row", -1)
    closed = jnp.stack(
        [
            jnp.where(row_at == 0, -1, -9),
            jnp.where(row_at == row_size - 1, row_count - 1, -9),
            jnp.where(col_at == 0, -1, -LANES - 1),
            jnp.where(col_at == col_size - 1, col_count - 1, -LANES - 1),
        ]
    ).astype(jnp.int32)
    depth_out, first_out, second_out = pl.pallas_call(
        functools.partial(flood_kernel, row_count, col_count),
        out_shape=(tile_out, tile_out, tile_out),
        in_specs=[SMEM] + [VMEM] * 6,
        out_specs=(VMEM, VMEM, VMEM),
        compiler_params=PARAMS,
        name="flood",
    )(closed, tile, wetted, left, right, above, below)
    return (river_state, depth_out, first_out, second_out)


def solution(mesh):
    in_specs = (
        P("row", None, None, "col"),
        P("row", None, None, "col"),
        P("row", None, None, "col"),
        P("row", None, "col"),
        P("row", "col"),
        P("row", "col"),
        P("row", "col", None, None, None),
        P("row", "col"),
        P("row", "col"),
        P("row", "col"),
        P("row", "col"),
        P("row", "col"),
        P("row", "col"),
        P("row", "col"),
    )
    out_specs = (P("row", None, "col"), P("row", "col"), P("row", "col"), P("row", "col"))
    return jax.shard_map(local, mesh=mesh, in_specs=in_specs, out_specs=out_specs, check_vma=False)
```

```python
import functools

import jax
import jax.numpy as jnp
from jax import lax
from jax.experimental import pallas as pl
from jax.experimental.pallas import tpu as pltpu
from jax.sharding import PartitionSpec as P

GRAVITY = 9.81
TIME_STEP = 1.0
CELL_WIDTH = 10.0
MANNING_SQ = 0.0009
DEPTH_FLOOR = 0.05
WEIR_GAIN = 0.5
FREE_COEF = 0.5
SUB_COEF = 0.4
SUB_OFFSET = 0.25
GATE_COEF = 0.2

F32 = jnp.float32
BF16 = jnp.bfloat16
LANES = 128
LOW = 256
BLOCK = 2
VMEM = pl.BlockSpec(memory_space=pltpu.VMEM)
SMEM = pl.BlockSpec(memory_space=pltpu.SMEM)
ANY = pl.BlockSpec(memory_space=pl.ANY)
PARAMS = pltpu.CompilerParams(vmem_limit_bytes=40 * 2**20)
WIDE = pltpu.CompilerParams(vmem_limit_bytes=60 * 2**20)


def start_copies(sources, targets, sems):
    copies = [pltpu.make_async_copy(s, t, sems.at[n]) for n, (s, t) in enumerate(zip(sources, targets))]
    for copy in copies:
        copy.start()
    return copies


def mat_mat(a, b):
    return [[a[i][0] * b[0][j] + a[i][1] * b[1][j] for j in range(2)] for i in range(2)]


def mat_vec(a, v):
    return [a[i][0] * v[0] + a[i][1] * v[1] for i in range(2)]


def mat_sub(a, b):
    return [[a[i][j] - b[i][j] for j in range(2)] for i in range(2)]


def mat_neg(a):
    return [[-a[i][j] for j in range(2)] for i in range(2)]


def mat_inv(m):
    scale = 1.0 / (m[0][0] * m[1][1] - m[0][1] * m[1][0])
    return [[m[1][1] * scale, -m[0][1] * scale], [-m[1][0] * scale, m[0][0] * scale]]


def rank_kernel(tiles, capacity, blocks, tile_ref, slot_ref, base_ref, flag_ref, whole_ref):
    table = lax.broadcasted_iota(jnp.int32, (tiles, LANES), 0)
    first_slot = table.astype(F32) * capacity
    row_at = lax.broadcasted_iota(jnp.int32, (LANES, 2 * LANES), 0)
    col_at = lax.broadcasted_iota(jnp.int32, (LANES, 2 * LANES), 1)
    earlier = jnp.where(row_at < col_at, 1.0, 0.0).astype(BF16)

    def body(b, carry):
        rank, most = carry
        base = jnp.floor(rank * (1.0 / LOW))
        base_ref[b] = base
        offset = first_slot + (rank - base * LOW)
        start = offset
        for n in range(BLOCK):
            g = b * BLOCK + n
            ids = tile_ref[pl.ds((g // 8) * 64 + g % 8, 8, stride=8), :]
            hits = [ids[r : r + 1, :] == table for r in range(8)]
            hot = jnp.concatenate([jnp.where(h, 1.0, 0.0).astype(BF16) for h in hits], 0)
            counts = jnp.dot(hot, earlier, preferred_element_type=F32)
            rows, bases = [], []
            for r in range(8):
                part = counts[r * tiles : (r + 1) * tiles]
                place = jnp.where(hits[r], part[:, :LANES] + offset, 0.0)
                rows.append(jnp.sum(place, axis=0, keepdims=True))
                bases.append(jnp.sum(jnp.where(hits[r], base * LOW, 0.0), axis=0, keepdims=True))
                offset = offset + part[:, LANES:]
            slots = jnp.concatenate(rows, 0)
            at = pl.ds(pl.multiple_of(g * 8, 8), 8)
            slot_ref[at, :] = slots.astype(jnp.int32)
            whole_ref[at, :] = (slots + jnp.concatenate(bases, 0)).astype(jnp.int32)
        last = jnp.floor((offset - first_slot - 1.0) * (1.0 / LOW))
        return rank + (offset - start), jnp.maximum(most, last)

    nothing = jnp.zeros((tiles, LANES), F32)
    most = lax.fori_loop(0, blocks, body, (nothing, nothing), unroll=8)[1]
    flag_ref[0] = jnp.max(most).astype(jnp.int32)


def solve_kernel(sections, *refs):
    inputs, later = refs[:4], refs[4:8]
    solved_ref, packed_ref = refs[8:10]
    fetched = refs[10:14]
    lower_ref, main_ref, upper_ref, rhs_ref, sems, later_sems = refs[14:]
    pieces = []
    for n in range(4):
        parts = [[r.at[pl.ds(n * r.shape[0] // 4, r.shape[0] // 4)] for r in group] for group in (inputs, refs[14:18])]
        pieces.append(start_copies(*parts, sems.at[n]))
    copies = start_copies(later, fetched, later_sems)

    def block(ref, k):
        return [[ref[pl.ds(k * 32 + i * 16 + j, 8, stride=2), :] for j in range(2)] for i in range(2)]

    couples = []
    for k in range(sections):
        if k % (sections // 4) == 0:
            for copy in pieces[k // (sections // 4)]:
                copy.wait()
        lower = block(lower_ref, k)
        main = block(main_ref, k)
        upper = block(upper_ref, k)
        right = [rhs_ref[pl.ds(k * 16 + j, 8, stride=2), :] for j in range(2)]
        if k == 0:
            inverse = mat_inv(main)
            left = mat_neg(mat_mat(inverse, lower))
            value = mat_vec(inverse, right)
        else:
            inverse = mat_inv(mat_sub(main, mat_mat(lower, couples[-1])))
            left = mat_neg(mat_mat(inverse, mat_mat(lower, left)))
            moved = mat_vec(lower, value)
            value = mat_vec(inverse, [right[i] - moved[i] for i in range(2)])
        couples.append(mat_mat(inverse, upper))
        for i in range(2):
            solved_ref[k, i] = value[i]
            for j in range(2):
                solved_ref[k, 2 + 2 * i + j] = left[i][j]
    spike = mat_neg(couples[-1])
    tail = (value, left, spike)
    for i in range(2):
        for j in range(2):
            solved_ref[sections - 1, 6 + 2 * i + j] = spike[i][j]
    for k in range(sections - 2, -1, -1):
        couple = couples[k]
        after = mat_vec(couple, value)
        value = [solved_ref[k, i] - after[i] for i in range(2)]
        after = mat_mat(couple, left)
        left = [[solved_ref[k, 2 + 2 * i + j] - after[i][j] for j in range(2)] for i in range(2)]
        spike = mat_neg(mat_mat(couple, spike))
        for i in range(2):
            solved_ref[k, i] = value[i]
            for j in range(2):
                solved_ref[k, 2 + 2 * i + j] = left[i][j]
                solved_ref[k, 6 + 2 * i + j] = spike[i][j]
    for i in range(2):
        packed_ref[i] = value[i]
        packed_ref[2 + i] = tail[0][i]
        for j in range(2):
            packed_ref[4 + 2 * i + j] = left[i][j]
            packed_ref[8 + 2 * i + j] = tail[1][i][j]
            packed_ref[12 + 2 * i + j] = spike[i][j]
            packed_ref[16 + 2 * i + j] = tail[2][i][j]
    for copy in copies:
        copy.wait()


def load_pair(ref, n):
    return [ref[n], ref[n + 1]]


def load_square(ref, n):
    return [load_pair(ref, n), load_pair(ref, n + 2)]


def store_all(ref, values):
    flat = []
    for value in values:
        flat += [*value[0], *value[1]] if isinstance(value[0], list) else value
    for n, item in enumerate(flat):
        ref[n] = item


def pick(flag, one, other):
    if isinstance(one, list):
        return [pick(flag, a, b) for a, b in zip(one, other)]
    return jnp.where(flag, one, other)


def add(a, b):
    if isinstance(a, list):
        return [add(x, y) for x, y in zip(a, b)]
    return a + b


def meet(head_y, head_left, tail_y, tail_right):
    inner = mat_mat(head_left, tail_right)
    inverse = mat_inv([[1.0 - inner[0][0], -inner[0][1]], [-inner[1][0], 1.0 - inner[1][1]]])
    return inverse, mat_vec(inverse, add(head_y, mat_vec(head_left, tail_y)))


def merge_kernel(step, first, position_ref, own_ref, other_ref, *refs):
    known_ref = None if first else refs[0]
    group_ref, map_ref, send_ref = refs[-3:]
    position = position_ref[0]
    late = ((position >> step) & 1) == 1

    def group(ref):
        return [load_pair(ref, 0), load_pair(ref, 2)] + [load_square(ref, n) for n in (4, 8, 12, 16)]

    own, other = group(own_ref), group(other_ref)
    head_y, tail_y, head_left, tail_left, head_right, tail_right = pick(late, other, own)
    next_head_y, next_tail_y, next_head_left, next_tail_left, next_head_right, next_tail_right = pick(
        late, own, other
    )
    inverse, head = meet(next_head_y, next_head_left, tail_y, tail_right)
    head_before = mat_mat(inverse, mat_mat(next_head_left, tail_left))
    head_after = mat_mat(inverse, next_head_right)
    tail = add(tail_y, mat_vec(tail_right, head))
    tail_before = add(tail_left, mat_mat(tail_right, head_before))
    tail_after = mat_mat(tail_right, head_after)
    joined = [
        add(head_y, mat_vec(head_right, head)),
        add(next_tail_y, mat_vec(next_tail_left, tail)),
        add(head_left, mat_mat(head_right, head_before)),
        mat_mat(next_tail_left, tail_before),
        mat_mat(head_right, head_after),
        add(next_tail_right, mat_mat(next_tail_left, tail_after)),
    ]
    zero = jnp.zeros(tail[0].shape, F32)
    one = zero + 1.0
    unit, none, nothing = [[one, zero], [zero, one]], [[zero, zero], [zero, zero]], [zero, zero]
    if first:
        maps = [
            [pick(late, tail_before, unit), pick(late, tail_after, none), pick(late, tail, nothing)],
            [pick(late, none, head_before), pick(late, unit, head_after), pick(late, nothing, head)],
        ]
    else:
        maps = []
        for n in range(2):
            by_before = load_square(known_ref, 10 * n)
            by_after = load_square(known_ref, 10 * n + 4)
            value = load_pair(known_ref, 10 * n + 8)
            maps.append(
                [
                    pick(late, mat_mat(by_before, tail_before), add(by_before, mat_mat(by_after, head_before))),
                    pick(late, add(by_after, mat_mat(by_before, tail_after)), mat_mat(by_after, head_after)),
                    pick(late, add(value, mat_vec(by_before, tail)), add(value, mat_vec(by_after, head))),
                ]
            )
    store_all(group_ref, joined)
    store_all(map_ref, maps[0] + maps[1])
    later = ((position >> (step + 1)) & 1) == 1
    store_all(send_ref, [pick(later, joined[0], joined[1]), pick(later, joined[2], joined[5])])


def rows16(row):
    return jnp.broadcast_to(row, (16, LANES)).astype(BF16)


def table16(count):
    shape = (count // 16, 16, LANES)
    at = lax.broadcasted_iota(jnp.int32, shape, 0) * 16 + lax.broadcasted_iota(jnp.int32, shape, 1)
    return at.astype(F32).astype(BF16)


def halves(value):
    high = value.astype(BF16).astype(F32)
    return high, value - high


def one_hots(high, low, values, high_table, low_table):
    one = jnp.ones((), BF16)
    zero = jnp.zeros((), BF16)
    left, right = [], []
    for r in range(high.shape[0]):
        hit = high_table == rows16(high[r : r + 1])[None]
        left.append(
            jnp.concatenate(
                [jnp.where(hit, rows16(v[r : r + 1])[None], zero).reshape(-1, LANES) for v in values], 0
            )
        )
        hit = low_table == rows16(low[r : r + 1])[None]
        right.append(jnp.where(hit, one, zero).reshape(-1, LANES))
    return jnp.concatenate(left, 1), jnp.concatenate(right, 1)


def product(left, right):
    return lax.dot_general(left, right, (((1,), (1,)), ((), ())), preferred_element_type=F32)


def group_at(g):
    over = pl.multiple_of((g // 8) * 8, 8)
    along = pl.multiple_of((g % 8) * LANES, LANES)
    return (pl.ds(over, 8), pl.ds(along, LANES))


def fill_slots(tiles, capacity, start, stop, most, slot_ref, base_ref, flag_ref, values, total_ref, side=None):
    windows = capacity // LOW
    taken = min(most, windows)
    window_table = table16(taken * tiles)
    low_table = table16(LOW)
    if side is not None:
        side_code, side_ref = side
        tile_table = table16(tiles)
        side_table = table16(LANES)
        side_ref[...] = jnp.zeros_like(side_ref)

    def block_values(b):
        groups = [values(b * BLOCK + n) for n in range(BLOCK)]
        return [jnp.concatenate([g[v] for g in groups], 0) for v in range(len(groups[0]))]

    def add_block(b, first, with_side):
        rows = pl.ds(pl.multiple_of(b * (8 * BLOCK), 8 * BLOCK), 8 * BLOCK)
        slot = slot_ref[rows, :]
        value = block_values(b)
        tile = slot // capacity
        window = slot % capacity // LOW - first
        code = jnp.where((window >= 0) & (window < taken), window * tiles + tile, -1)
        left, right = one_hots(code.astype(F32), (slot % LOW).astype(F32), value, window_table, low_table)
        found = product(left, right)
        base = base_ref[b] + first
        base = jnp.concatenate([base, base], 1)
        for v in range(len(value)):
            parts = [found[(v * taken + i) * tiles : (v * taken + i + 1) * tiles] for i in range(taken)]
            for q in range(windows):
                put = jnp.where(base == q, parts[0], 0.0)
                for i in range(1, taken):
                    put = jnp.where(base == q - i, parts[i], put)
                total_ref[pl.ds((v * windows + q) * tiles, tiles), :] += put
        if with_side:
            code = jnp.concatenate([side_code(b * BLOCK + n) for n in range(BLOCK)], 0)
            left, right = one_hots(tile.astype(F32), code.astype(F32), value, tile_table, side_table)
            side_ref[...] += product(left, right)

    def body(b, carry):
        add_block(b, 0, side is not None)
        return carry

    lax.fori_loop(start, stop, body, 0, unroll=4)
    for first in range(taken, windows, taken):

        @pl.when(flag_ref[0] >= first)
        def _(first=first):
            def rest(b, carry):
                add_block(b, first, False)
                return carry

            lax.fori_loop(start, stop, rest, 0)


def store_slots(tiles, capacity, total_ref, part, scale, out_ref, pitch, row):
    windows = capacity // LOW
    for q in range(windows):
        first = total_ref[pl.ds((part * windows + q) * tiles, tiles), :]
        value = first * scale + total_ref[pl.ds(((part + 1) * windows + q) * tiles, tiles), :]
        for j in range(LOW // LANES):
            at = pl.ds(row + j * windows + q, tiles, stride=pitch)
            out_ref[at, :] = value[:, j * LANES : (j + 1) * LANES]


def cell_kernel(tiles, capacity, groups, row_count, *refs):
    slot_ref, row_ref, col_ref, _, out_ref = refs
    high_table = table16(tiles * capacity // LOW)
    low_table = table16(LOW)
    out_ref[...] = jnp.zeros_like(out_ref)

    def body(g, carry):
        slot = slot_ref[pl.ds(pl.multiple_of(g * 8, 8), 8), :]
        col = col_ref[group_at(g)]
        high = (col // LOW) * row_count + row_ref[group_at(g)]
        left, right = one_hots(
            (slot % capacity // LOW * tiles + slot // capacity).astype(F32),
            (slot % LOW).astype(F32),
            [high.astype(F32), (col % LOW).astype(F32)],
            high_table,
            low_table,
        )
        out_ref[...] += product(left, right)
        return carry

    lax.fori_loop(0, groups, body, 0, unroll=8)


def weir_kernel(sections, steps, tiles, capacity, row_count, col_count, *refs):
    position_ref, own_ref, other_ref, map_ref = refs[:4]
    solved_ref, slot_ref, base_ref, flag_ref, cells_ref = refs[4:9]
    crest_ref, regime_ref, row_ref, col_ref = refs[9:13]
    state_out, out_ref, state_ref, phase_ref, total_ref, side_ref, sems = refs[13:]
    late = ((position_ref[0] >> (steps - 1)) & 1) == 1
    own = [load_pair(own_ref, 0), load_square(own_ref, 2)]
    other = [load_pair(other_ref, 0), load_square(other_ref, 2)]
    tail_y, tail_right = pick(late, other, own)
    head_y, head_left = pick(late, own, other)
    head = meet(head_y, head_left, tail_y, tail_right)[1]
    tail = add(tail_y, mat_vec(tail_right, head))
    zero = jnp.zeros(tail[0].shape, F32)
    outer_before = pick(late, tail, [zero, zero])
    outer_after = pick(late, [zero, zero], head)
    before, after = (
        add(
            load_pair(map_ref, n + 8),
            add(
                mat_vec(load_square(map_ref, n), outer_before),
                mat_vec(load_square(map_ref, n + 4), outer_after),
            ),
        )
        for n in (0, 10)
    )
    for k in range(sections):
        for i in range(2):
            state = solved_ref[k, i]
            for j in range(2):
                state = state + solved_ref[k, 2 + 2 * i + j] * before[j]
                state = state + solved_ref[k, 6 + 2 * i + j] * after[j]
            state_ref[pl.ds(k * 16 + i, 8, stride=2), :] = state
            if i == 0:
                phase_ref[pl.ds((k // 8) * 64 + k % 8, 8, stride=8), :] = state

    state_copy = pltpu.make_async_copy(state_ref, state_out, sems.at[0])
    state_copy.start()

    def values(g):
        phase = phase_ref[pl.ds(pl.multiple_of(g * 8, 8), 8), :]
        regime = regime_ref[group_at(g)]
        head = jnp.maximum(phase - crest_ref[group_at(g)], 0.0)
        free = jnp.where(regime == 0, FREE_COEF * head * jnp.sqrt(head), 0.0)
        sub = jnp.where(
            regime == 1,
            SUB_COEF * jnp.sqrt(head + SUB_OFFSET),
            jnp.where(regime == 2, GATE_COEF, 0.0),
        )
        return [*halves(WEIR_GAIN * (free + sub * phase)), *halves(WEIR_GAIN * sub)]

    def side_code(g):
        col = col_ref[group_at(g)]
        place = jnp.where(col < 2, col, jnp.where(col >= col_count - 2, col - (col_count - 4), -1))
        return jnp.where(place >= 0, place * row_count + row_ref[group_at(g)], -1)

    total_ref[...] = jnp.zeros_like(total_ref)
    side = (side_code, side_ref)
    fill_slots(tiles, capacity, 0, sections // BLOCK, 2, slot_ref, base_ref, flag_ref, values, total_ref, side)
    rows_each = capacity // LANES
    pitch = 3 * rows_each + 2
    at = lax.broadcasted_iota(jnp.int32, (tiles, LANES), 1)
    first_cols = at < 2 * row_count
    for v in range(2):
        store_slots(tiles, capacity, total_ref, 2 * v, 1.0, out_ref, pitch, v * rows_each)
        sums = side_ref[pl.ds(2 * v * tiles, tiles), :] + side_ref[pl.ds((2 * v + 1) * tiles, tiles), :]
        beside = jnp.where(first_cols, pltpu.roll(sums, tiles - 1, 0), pltpu.roll(sums, 1, 0))
        out_ref[pl.ds(3 * rows_each + v, tiles, stride=pitch), :] = beside
    store_slots(tiles, capacity, cells_ref, 0, float(LOW), out_ref, pitch, 2 * rows_each)
    state_copy.wait()


def side_lanes(n):
    at = lax.broadcasted_iota(jnp.int32, (8, LANES), 1)
    return (at == 2 * n) | (at == 2 * n + 1)


def stage_kernel(row_count, col_count, *refs):
    tile_ref, left_ref, right_ref, wet_ref, sems = refs[6:]
    for copy in start_copies(refs[:5], [tile_ref.at[n] for n in range(4)] + [wet_ref], sems):
        copy.wait()
    tile_ref[4] = wet_ref[...].astype(F32) * (TIME_STEP / CELL_WIDTH)
    left = jnp.zeros(left_ref.shape, F32)
    right = left
    for t in range(row_count // 8):
        for n in range(5):
            at = 5 * t + n
            first = tile_ref[n, pl.ds(8 * t, 8), pl.ds(0, LANES)]
            last = tile_ref[n, pl.ds(8 * t, 8), pl.ds(col_count - LANES, LANES)]
            left = jnp.where(side_lanes(at), pltpu.roll(first, 2 * at, 1), left)
            right = jnp.where(side_lanes(at), pltpu.roll(last, 2 * at + 2, 1), right)
    left_ref[...] = left
    right_ref[...] = right


def unpacked(strip, n, rows, lane):
    parts = [pltpu.roll(strip, (lane - 2 * (5 * t + n)) % LANES, 1) for t in range(rows // 8)]
    return jnp.concatenate(parts, 0)


def apply_kernel(sources, rows_each, row_count, col_count, *refs):
    in_ref, tile_ref, before_ref, after_ref = refs[:4]
    depth_ref, top_ref, bottom_ref, side_ref, total_ref = refs[4:]
    pitch = 3 * rows_each + 2
    high_count = row_count * col_count // LOW
    high_table = table16(high_count)
    low_table = table16(LOW)
    total_ref[...] = jnp.zeros_like(total_ref)
    step = 8 // rows_each if rows_each < 8 else 1

    def body(g, carry):
        def part(v):
            return jnp.concatenate(
                [in_ref[pl.ds((g * step + n) * pitch + v * rows_each, rows_each), :] for n in range(step)], 0
            )

        cell = part(2).astype(jnp.int32)
        left, right = one_hots(
            (cell // LOW).astype(F32),
            (cell % LOW).astype(F32),
            [*halves(part(0)), *halves(part(1))],
            high_table,
            low_table,
        )
        total_ref[...] += product(left, right)
        return carry

    lax.fori_loop(0, sources // step, body, 0, unroll=16)
    for n in range(col_count // LOW):
        def summed(v):
            start = 2 * v * high_count + n * row_count
            return total_ref[pl.ds(start, row_count), :] + total_ref[pl.ds(start + high_count, row_count), :]

        cols = pl.ds(n * LOW, LOW)
        depth = tile_ref[0, :, cols]
        surface = tile_ref[1, :, cols] + depth
        depth_ref[:, cols] = jnp.maximum(depth + (summed(0) - summed(1) * surface), 0.0)
    row_at = lax.broadcasted_iota(jnp.int32, (row_count, LANES), 0)
    col_at = lax.broadcasted_iota(jnp.int32, (row_count, LANES), 1)

    def columns(v):
        sums = jnp.sum(in_ref[pl.ds(3 * rows_each + v, sources, stride=pitch), :], axis=0, keepdims=True)
        result = jnp.zeros((row_count, LANES), F32)
        for place, lane in enumerate((0, 1, LANES - 2, LANES - 1)):
            wanted = col_at == place * row_count + row_at
            column = jnp.sum(jnp.where(wanted, sums, 0.0), axis=1, keepdims=True)
            result = jnp.where(col_at == lane, column, result)
        return result

    before, after = before_ref[...], after_ref[...]
    for n in range(5):
        right = unpacked(after, n, row_count, 0)
        left = unpacked(before, n, row_count, LANES - 2)
        side_ref[n] = jnp.where(col_at < LANES // 2, right, left)
    depth = side_ref[0]
    surface = side_ref[1] + depth
    side_ref[0] = jnp.maximum(depth + (columns(0) - columns(1) * surface), 0.0)
    inner, outer = pl.ds(0, col_count), pl.ds(col_count, LANES)
    for out, near, rows in ((top_ref, 0, (0, 1)), (bottom_ref, row_count - 1, (row_count - 2, row_count - 1))):
        for n in range(5):
            for j in range(2 if n < 3 else 1):
                row = pl.ds(rows[j] if n < 3 else near, 1)
                at = pl.ds(2 * n + j if n < 3 else 3 + n, 1)
                out[at, inner] = depth_ref[row, :] if n == 0 else tile_ref[n, row, :]
                out[at, outer] = side_ref[n, row, :]


def face_flux(eta_here, eta_next, bed_here, bed_next, old_flux):
    flow_depth = jnp.maximum(
        jnp.maximum(eta_here, eta_next) - jnp.maximum(bed_here, bed_next), DEPTH_FLOOR
    )
    gradient = (eta_next - eta_here) / CELL_WIDTH
    pushed = old_flux - GRAVITY * TIME_STEP * flow_depth * gradient
    friction = jnp.exp((-7.0 / 3.0) * jnp.log(flow_depth))
    return pushed / (1.0 + GRAVITY * TIME_STEP * MANNING_SQ * jnp.abs(old_flux) * friction)


def flood_kernel(row_count, col_count, *refs):
    closed_ref, tile_ref, depth_ref, side_ref, above_ref, below_ref = refs[:6]
    outs, kept, sems = refs[6:9], refs[9], refs[10]
    at = lax.broadcasted_iota(jnp.int32, (8, 1), 0)
    arrays = []
    for n in range(5):
        own = jnp.concatenate([depth_ref[...] if n == 0 else tile_ref[n], side_ref[n]], 1)
        first_row = 2 * n if n < 3 else 3 + n
        second_row = first_row + 1 if n < 3 else first_row
        halo = jnp.where(at == 0, below_ref[pl.ds(first_row, 1), :], 0.0)
        halo = jnp.where(at == 1, below_ref[pl.ds(second_row, 1), :], halo)
        halo = jnp.where(at == 6, above_ref[pl.ds(first_row, 1), :], halo)
        halo = jnp.where(at == 7, above_ref[pl.ds(second_row, 1), :], halo)
        arrays.append(jnp.concatenate([own, halo], 0))
    depth, bed, first, second, wet = arrays
    shape = depth.shape
    row_at = lax.broadcasted_iota(jnp.int32, shape, 0)
    col_at = lax.broadcasted_iota(jnp.int32, shape, 1)
    first_shut = (row_at == closed_ref[0]) | (row_at == closed_ref[1])
    second_shut = (col_at == closed_ref[2]) | (col_at == closed_ref[3])
    down = lambda x: pltpu.roll(x, shape[0] - 1, 0)
    up = lambda x: pltpu.roll(x, 1, 0)
    onward = lambda x: pltpu.roll(x, shape[1] - 1, 1)
    back = lambda x: pltpu.roll(x, 1, 1)
    bed_down = down(bed)
    bed_onward = onward(bed)
    copies = []

    def finish(n, value):
        kept[n] = value[:row_count, :col_count]
        copies.append(pltpu.make_async_copy(kept.at[n], outs[n], sems.at[n]))
        copies[-1].start()

    for step in range(2):
        eta = bed + depth
        first = jnp.where(first_shut, 0.0, face_flux(eta, down(eta), bed, bed_down, first))
        if step == 1:
            finish(1, first)
        second = jnp.where(second_shut, 0.0, face_flux(eta, onward(eta), bed, bed_onward, second))
        if step == 1:
            finish(2, second)
        depth = depth + wet * (up(first) - first + (back(second) - second))
    finish(0, depth)
    for copy in copies:
        copy.wait()


def exchanged(block, axis, step):
    return lax.ppermute(block, axis, [(i, i ^ (1 << step)) for i in range(lax.axis_size(axis))])


def swapped(first, last, axis, ring):
    count = lax.axis_size(axis)
    odd = lax.axis_index(axis) % 2 == 1
    inner = [(i, i ^ 1) for i in range(count)]
    outer = [] if ring else [(0, 0), (count - 1, count - 1)]
    for i in range(1, count if ring else count - 1, 2):
        outer += [(i, (i + 1) % count), ((i + 1) % count, i)]
    two = lax.ppermute(jnp.where(odd, last, first), axis, outer)
    one = lax.ppermute(jnp.where(odd, first, last), axis, inner)
    return jnp.where(odd, one, two), jnp.where(odd, two, one)


def local(
    river_lower,
    river_main,
    river_upper,
    river_rhs,
    weir_crest,
    weir_regime,
    weir_tile,
    weir_row,
    weir_col,
    bed_level,
    water_depth,
    flux_first,
    flux_second,
    wet_mask,
):
    sections, chains = weir_crest.shape
    row_count, col_count = water_depth.shape
    row_size = lax.axis_size("row")
    col_size = lax.axis_size("col")
    row_at = lax.axis_index("row")
    col_at = lax.axis_index("col")
    tiles = row_size * col_size
    weirs = sections * chains
    capacity = 2 * weirs // tiles
    lane_rows = chains // LANES

    def block_rows(array):
        split = array.reshape(sections, 2, 2, lane_rows, LANES)
        return split.transpose(0, 1, 3, 2, 4).reshape(-1, LANES)

    rhs_rows = river_rhs.reshape(sections, 2, lane_rows, LANES).transpose(0, 2, 1, 3).reshape(-1, LANES)
    rows = weirs // LANES
    high_count = tiles * capacity // LOW
    rows_each = capacity // LANES
    pitch = 3 * rows_each + 2
    river_block = pltpu.VMEM((sections * 4 * lane_rows, LANES), F32)
    blocks = sections // BLOCK
    steps = row_size.bit_length() - 1
    weir_shape = (sections, chains)
    whole = jax.ShapeDtypeStruct(weir_shape, jnp.int32)
    solved, packed, crest, regime, weir_rows, weir_cols = pl.pallas_call(
        functools.partial(solve_kernel, sections),
        out_shape=(
            jax.ShapeDtypeStruct((sections, 10, lane_rows, LANES), F32),
            jax.ShapeDtypeStruct((20, lane_rows, LANES), F32),
            jax.ShapeDtypeStruct(weir_shape, F32),
            whole,
            whole,
            whole,
        ),
        in_specs=[ANY] * 8,
        out_specs=(VMEM,) * 6,
        scratch_shapes=[
            river_block,
            river_block,
            river_block,
            pltpu.VMEM((sections * 2 * lane_rows, LANES), F32),
            pltpu.SemaphoreType.DMA((4, 4)),
            pltpu.SemaphoreType.DMA((4,)),
        ],
        compiler_params=WIDE,
        name="solve",
    )(
        block_rows(river_lower),
        block_rows(river_main),
        block_rows(river_upper),
        rhs_rows,
        weir_crest,
        weir_regime,
        weir_row,
        weir_col,
    )
    *places, whole_slots = pl.pallas_call(
        functools.partial(rank_kernel, tiles, capacity, blocks),
        out_shape=(
            jax.ShapeDtypeStruct((rows, LANES), jnp.int32),
            jax.ShapeDtypeStruct((blocks, tiles, LANES), F32),
            jax.ShapeDtypeStruct((1,), jnp.int32),
            jax.ShapeDtypeStruct((rows, LANES), jnp.int32),
        ),
        in_specs=[VMEM],
        out_specs=(VMEM, VMEM, SMEM, VMEM),
        compiler_params=PARAMS,
        cost_estimate=pl.CostEstimate(flops=2 * tiles * weirs * LOW, bytes_accessed=2**17, transcendentals=0),
        name="rank",
    )(weir_tile.reshape(rows, LANES))
    group, known = packed, ()
    for step in range(steps - 1):
        other = exchanged(group, "row", step)
        twenty = jax.ShapeDtypeStruct((20, lane_rows, LANES), F32)
        group, own_map, sent = pl.pallas_call(
            functools.partial(merge_kernel, step, step == 0),
            out_shape=(twenty, twenty, jax.ShapeDtypeStruct((6, lane_rows, LANES), F32)),
            in_specs=[SMEM] + [VMEM] * (2 + len(known)),
            out_specs=(VMEM, VMEM, VMEM),
            compiler_params=PARAMS,
            name="merge",
        )(row_at.reshape(1), group, other, *known)
        known = (own_map,)
    met = exchanged(sent, "row", steps - 1)
    cells = pl.pallas_call(
        functools.partial(cell_kernel, tiles, capacity, rows // 8, row_count),
        out_shape=jax.ShapeDtypeStruct((2 * high_count, LOW), F32),
        in_specs=[VMEM, VMEM, VMEM, ANY],
        out_specs=VMEM,
        compiler_params=PARAMS,
        cost_estimate=pl.CostEstimate(flops=4 * high_count * LOW * weirs, bytes_accessed=2**18, transcendentals=0),
        name="cells",
    )(whole_slots, weir_rows, weir_cols, sent)
    state_shape = jax.ShapeDtypeStruct((sections * lane_rows * 2, LANES), F32)
    state_rows, outgoing = pl.pallas_call(
        functools.partial(weir_kernel, sections, steps, tiles, capacity, row_count, col_count),
        out_shape=(state_shape, jax.ShapeDtypeStruct((tiles * pitch, LANES), F32)),
        in_specs=[SMEM] + [VMEM] * 5 + [VMEM, SMEM] + [VMEM] * 5,
        out_specs=(ANY, VMEM),
        scratch_shapes=[
            pltpu.VMEM(state_shape.shape, F32),
            pltpu.VMEM((rows, LANES), F32),
            pltpu.VMEM((4 * high_count, LOW), F32),
            pltpu.VMEM((4 * tiles, LANES), F32),
            pltpu.SemaphoreType.DMA((1,)),
        ],
        compiler_params=PARAMS,
        name="weirs",
    )(row_at.reshape(1), sent, met, own_map, solved, *places, cells, crest, regime, weir_rows, weir_cols)
    river_state = (
        state_rows.reshape(sections, lane_rows, 2, LANES).transpose(0, 2, 1, 3).reshape(sections, 2, chains)
    )
    messages = outgoing.reshape(tiles, pitch, 1, LANES)
    arrived = lax.all_to_all(messages, ("row", "col"), split_axis=0, concat_axis=0, tiled=True)
    tile_stack = jax.ShapeDtypeStruct((5, row_count, col_count), F32)
    side = jax.ShapeDtypeStruct((8, LANES), F32)
    tile, left, right = pl.pallas_call(
        functools.partial(stage_kernel, row_count, col_count),
        out_shape=(tile_stack, side, side),
        in_specs=[ANY] * 6,
        out_specs=(VMEM, VMEM, VMEM),
        scratch_shapes=[pltpu.VMEM((row_count, col_count), jnp.int32), pltpu.SemaphoreType.DMA((5,))],
        compiler_params=PARAMS,
        name="stage",
    )(water_depth, bed_level, flux_first, flux_second, wet_mask, outgoing)
    before, after = swapped(left, right, "col", False)
    tile_out = jax.ShapeDtypeStruct((row_count, col_count), F32)
    edge = jax.ShapeDtypeStruct((8, col_count + LANES), F32)
    flank = jax.ShapeDtypeStruct((5, row_count, LANES), F32)
    wetted, top, bottom, side = pl.pallas_call(
        functools.partial(apply_kernel, tiles, rows_each, row_count, col_count),
        out_shape=(tile_out, edge, edge, flank),
        in_specs=[VMEM] * 4,
        out_specs=(VMEM,) * 4,
        scratch_shapes=[pltpu.VMEM((4 * row_count * col_count // LOW, LOW), F32)],
        compiler_params=PARAMS,
        name="apply",
    )(arrived.reshape(tiles * pitch, LANES), tile, before, after)
    above, below = swapped(top, bottom, "row", True)
    closed = jnp.stack(
        [
            jnp.where(row_at == 0, row_count + 7, -1),
            jnp.where(row_at == row_size - 1, row_count - 1, -1),
            jnp.where(col_at == 0, col_count + LANES - 1, -1),
            jnp.where(col_at == col_size - 1, col_count - 1, -1),
        ]
    ).astype(jnp.int32)
    depth_out, first_out, second_out = pl.pallas_call(
        functools.partial(flood_kernel, row_count, col_count),
        out_shape=(tile_out, tile_out, tile_out),
        in_specs=[SMEM] + [VMEM] * 5,
        out_specs=(ANY, ANY, ANY),
        scratch_shapes=[pltpu.VMEM((3, row_count, col_count), F32), pltpu.SemaphoreType.DMA((3,))],
        compiler_params=PARAMS,
        name="flood",
    )(closed, tile, wetted, side, above, below)
    return (river_state, depth_out, first_out, second_out)


def solution(mesh):
    in_specs = (
        P("row", None, None, "col"),
        P("row", None, None, "col"),
        P("row", None, None, "col"),
        P("row", None, "col"),
        P("row", "col"),
        P("row", "col"),
        P("row", "col", None, None, None),
        P("row", "col"),
        P("row", "col"),
        P("row", "col"),
        P("row", "col"),
        P("row", "col"),
        P("row", "col"),
        P("row", "col"),
    )
    out_specs = (P("row", None, "col"), P("row", "col"), P("row", "col"), P("row", "col"))
    return jax.shard_map(local, mesh=mesh, in_specs=in_specs, out_specs=out_specs, check_vma=False)
```

```python
import functools

import jax
import jax.numpy as jnp
from jax import lax
from jax.experimental import pallas as pl
from jax.experimental.pallas import tpu as pltpu
from jax.sharding import PartitionSpec as P

GRAVITY = 9.81
TIME_STEP = 1.0
CELL_WIDTH = 10.0
MANNING_SQ = 0.0009
DEPTH_FLOOR = 0.05
WEIR_GAIN = 0.5
FREE_COEF = 0.5
SUB_COEF = 0.4
SUB_OFFSET = 0.25
GATE_COEF = 0.2

F32 = jnp.float32
BF16 = jnp.bfloat16
LANES = 128
LOW = 256
BLOCK = 2
VMEM = pl.BlockSpec(memory_space=pltpu.VMEM)
SMEM = pl.BlockSpec(memory_space=pltpu.SMEM)
ANY = pl.BlockSpec(memory_space=pl.ANY)
HBM = pl.BlockSpec(memory_space=pltpu.HBM)
WIDE = pltpu.CompilerParams(vmem_limit_bytes=60 * 2**20)
PARAMS = pltpu.CompilerParams(vmem_limit_bytes=40 * 2**20)


def start_copies(sources, targets, sems):
    copies = [pltpu.make_async_copy(s, t, sems.at[n]) for n, (s, t) in enumerate(zip(sources, targets))]
    for copy in copies:
        copy.start()
    return copies


def mat_mat(a, b):
    return [[a[i][0] * b[0][j] + a[i][1] * b[1][j] for j in range(2)] for i in range(2)]


def mat_vec(a, v):
    return [a[i][0] * v[0] + a[i][1] * v[1] for i in range(2)]


def mat_sub(a, b):
    return [[a[i][j] - b[i][j] for j in range(2)] for i in range(2)]


def mat_neg(a):
    return [[-a[i][j] for j in range(2)] for i in range(2)]


def mat_inv(m):
    scale = 1.0 / (m[0][0] * m[1][1] - m[0][1] * m[1][0])
    return [[m[1][1] * scale, -m[0][1] * scale], [-m[1][0] * scale, m[0][0] * scale]]


def rank_kernel(tiles, capacity, blocks, tile_ref, slot_ref, base_ref, flag_ref, whole_ref):
    table = lax.broadcasted_iota(jnp.int32, (tiles, LANES), 0)
    first_slot = table.astype(F32) * capacity
    row_at = lax.broadcasted_iota(jnp.int32, (LANES, 2 * LANES), 0)
    col_at = lax.broadcasted_iota(jnp.int32, (LANES, 2 * LANES), 1)
    earlier = jnp.where(row_at < col_at, 1.0, 0.0).astype(BF16)

    def body(b, carry):
        rank, most = carry
        base = jnp.floor(rank * (1.0 / LOW))
        base_ref[b] = base
        offset = first_slot + (rank - base * LOW)
        start = offset
        for n in range(BLOCK):
            g = b * BLOCK + n
            ids = tile_ref[pl.ds((g // 8) * 64 + g % 8, 8, stride=8), :]
            hits = [ids[r : r + 1, :] == table for r in range(8)]
            hot = jnp.concatenate([jnp.where(h, 1.0, 0.0).astype(BF16) for h in hits], 0)
            counts = jnp.dot(hot, earlier, preferred_element_type=F32)
            rows, bases = [], []
            for r in range(8):
                part = counts[r * tiles : (r + 1) * tiles]
                place = jnp.where(hits[r], part[:, :LANES] + offset, 0.0)
                rows.append(jnp.sum(place, axis=0, keepdims=True))
                bases.append(jnp.sum(jnp.where(hits[r], base * LOW, 0.0), axis=0, keepdims=True))
                offset = offset + part[:, LANES:]
            slots = jnp.concatenate(rows, 0)
            at = pl.ds(pl.multiple_of(g * 8, 8), 8)
            slot_ref[at, :] = slots.astype(jnp.int32)
            whole_ref[at, :] = (slots + jnp.concatenate(bases, 0)).astype(jnp.int32)
        last = jnp.floor((offset - first_slot - 1.0) * (1.0 / LOW))
        return rank + (offset - start), jnp.maximum(most, last)

    nothing = jnp.zeros((tiles, LANES), F32)
    most = lax.fori_loop(0, blocks, body, (nothing, nothing), unroll=8)[1]
    flag_ref[0] = jnp.max(most).astype(jnp.int32)


def solve_kernel(sections, *refs):
    inputs, later = refs[:4], refs[4:8]
    solved_ref, packed_ref = refs[8:10]
    fetched = refs[10:14]
    lower_ref, main_ref, upper_ref, rhs_ref, sems, later_sems = refs[14:]
    pieces = []
    for n in range(4):
        parts = [[r.at[pl.ds(n * r.shape[0] // 4, r.shape[0] // 4)] for r in group] for group in (inputs, refs[14:18])]
        pieces.append(start_copies(*parts, sems.at[n]))
    copies = start_copies(later, fetched, later_sems)

    def block(ref, k):
        return [[ref[pl.ds(k * 32 + i * 16 + j, 8, stride=2), :] for j in range(2)] for i in range(2)]

    couples = []
    for k in range(sections):
        if k % (sections // 4) == 0:
            for copy in pieces[k // (sections // 4)]:
                copy.wait()
        lower = block(lower_ref, k)
        main = block(main_ref, k)
        upper = block(upper_ref, k)
        right = [rhs_ref[pl.ds(k * 16 + j, 8, stride=2), :] for j in range(2)]
        if k == 0:
            inverse = mat_inv(main)
            left = mat_neg(mat_mat(inverse, lower))
            value = mat_vec(inverse, right)
        else:
            inverse = mat_inv(mat_sub(main, mat_mat(lower, couples[-1])))
            left = mat_neg(mat_mat(inverse, mat_mat(lower, left)))
            moved = mat_vec(lower, value)
            value = mat_vec(inverse, [right[i] - moved[i] for i in range(2)])
        couples.append(mat_mat(inverse, upper))
        for i in range(2):
            solved_ref[k, i] = value[i]
            for j in range(2):
                solved_ref[k, 2 + 2 * i + j] = left[i][j]
    spike = mat_neg(couples[-1])
    tail = (value, left, spike)
    for i in range(2):
        for j in range(2):
            solved_ref[sections - 1, 6 + 2 * i + j] = spike[i][j]
    for k in range(sections - 2, -1, -1):
        couple = couples[k]
        after = mat_vec(couple, value)
        value = [solved_ref[k, i] - after[i] for i in range(2)]
        after = mat_mat(couple, left)
        left = [[solved_ref[k, 2 + 2 * i + j] - after[i][j] for j in range(2)] for i in range(2)]
        spike = mat_neg(mat_mat(couple, spike))
        for i in range(2):
            solved_ref[k, i] = value[i]
            for j in range(2):
                solved_ref[k, 2 + 2 * i + j] = left[i][j]
                solved_ref[k, 6 + 2 * i + j] = spike[i][j]
    for i in range(2):
        packed_ref[i] = value[i]
        packed_ref[2 + i] = tail[0][i]
        for j in range(2):
            packed_ref[4 + 2 * i + j] = left[i][j]
            packed_ref[8 + 2 * i + j] = tail[1][i][j]
            packed_ref[12 + 2 * i + j] = spike[i][j]
            packed_ref[16 + 2 * i + j] = tail[2][i][j]
    for copy in copies:
        copy.wait()


def load_pair(ref, n):
    return [ref[n], ref[n + 1]]


def load_square(ref, n):
    return [load_pair(ref, n), load_pair(ref, n + 2)]


def store_all(ref, values):
    flat = []
    for value in values:
        flat += [*value[0], *value[1]] if isinstance(value[0], list) else value
    for n, item in enumerate(flat):
        ref[n] = item


def pick(flag, one, other):
    if isinstance(one, list):
        return [pick(flag, a, b) for a, b in zip(one, other)]
    return jnp.where(flag, one, other)


def add(a, b):
    if isinstance(a, list):
        return [add(x, y) for x, y in zip(a, b)]
    return a + b


def meet(head_y, head_left, tail_y, tail_right):
    inner = mat_mat(head_left, tail_right)
    inverse = mat_inv([[1.0 - inner[0][0], -inner[0][1]], [-inner[1][0], 1.0 - inner[1][1]]])
    return inverse, mat_vec(inverse, add(head_y, mat_vec(head_left, tail_y)))


def merge_kernel(step, first, last, position_ref, own_ref, other_ref, *refs):
    known_ref = None if first else refs[0]
    out_ref, map_ref = refs[-2:]
    position = position_ref[0]
    late = ((position >> step) & 1) == 1

    def group(ref):
        return [load_pair(ref, 0), load_pair(ref, 2)] + [load_square(ref, n) for n in (4, 8, 12, 16)]

    own, other = group(own_ref), group(other_ref)
    head_y, tail_y, head_left, tail_left, head_right, tail_right = pick(late, other, own)
    next_head_y, next_tail_y, next_head_left, next_tail_left, next_head_right, next_tail_right = pick(
        late, own, other
    )
    inverse, head = meet(next_head_y, next_head_left, tail_y, tail_right)
    head_before = mat_mat(inverse, mat_mat(next_head_left, tail_left))
    head_after = mat_mat(inverse, next_head_right)
    tail = add(tail_y, mat_vec(tail_right, head))
    tail_before = add(tail_left, mat_mat(tail_right, head_before))
    tail_after = mat_mat(tail_right, head_after)
    joined = [
        add(head_y, mat_vec(head_right, head)),
        add(next_tail_y, mat_vec(next_tail_left, tail)),
        add(head_left, mat_mat(head_right, head_before)),
        mat_mat(next_tail_left, tail_before),
        mat_mat(head_right, head_after),
        add(next_tail_right, mat_mat(next_tail_left, tail_after)),
    ]
    zero = jnp.zeros(tail[0].shape, F32)
    one = zero + 1.0
    unit, none, nothing = [[one, zero], [zero, one]], [[zero, zero], [zero, zero]], [zero, zero]
    if first:
        maps = [
            [pick(late, tail_before, unit), pick(late, tail_after, none), pick(late, tail, nothing)],
            [pick(late, none, head_before), pick(late, unit, head_after), pick(late, nothing, head)],
        ]
    else:
        maps = []
        for n in range(2):
            by_before = load_square(known_ref, 10 * n)
            by_after = load_square(known_ref, 10 * n + 4)
            value = load_pair(known_ref, 10 * n + 8)
            maps.append(
                [
                    pick(late, mat_mat(by_before, tail_before), add(by_before, mat_mat(by_after, head_before))),
                    pick(late, add(by_after, mat_mat(by_before, tail_after)), mat_mat(by_after, head_after)),
                    pick(late, add(value, mat_vec(by_before, tail)), add(value, mat_vec(by_after, head))),
                ]
            )
    store_all(map_ref, maps[0] + maps[1])
    if last:
        later = ((position >> (step + 1)) & 1) == 1
        store_all(out_ref, [pick(later, joined[0], joined[1]), pick(later, joined[2], joined[5])])
    else:
        store_all(out_ref, joined)


def rows16(row):
    return jnp.broadcast_to(row, (16, LANES)).astype(BF16)


def table16(count):
    shape = (count // 16, 16, LANES)
    at = lax.broadcasted_iota(jnp.int32, shape, 0) * 16 + lax.broadcasted_iota(jnp.int32, shape, 1)
    return at.astype(F32).astype(BF16)


def halves(value):
    high = value.astype(BF16).astype(F32)
    return high, value - high


def one_hots(high, low, values, high_table, low_table):
    one = jnp.ones((), BF16)
    zero = jnp.zeros((), BF16)
    left, right = [], []
    for r in range(high.shape[0]):
        hit = high_table == rows16(high[r : r + 1])[None]
        left.append(
            jnp.concatenate(
                [jnp.where(hit, rows16(v[r : r + 1])[None], zero).reshape(-1, LANES) for v in values], 0
            )
        )
        hit = low_table == rows16(low[r : r + 1])[None]
        right.append(jnp.where(hit, one, zero).reshape(-1, LANES))
    return jnp.concatenate(left, 1), jnp.concatenate(right, 1)


def product(left, right):
    return lax.dot_general(left, right, (((1,), (1,)), ((), ())), preferred_element_type=F32)


def group_at(g):
    over = pl.multiple_of((g // 8) * 8, 8)
    along = pl.multiple_of((g % 8) * LANES, LANES)
    return (pl.ds(over, 8), pl.ds(along, LANES))


def fill_slots(tiles, capacity, start, stop, most, slot_ref, base_ref, flag_ref, values, total_ref, side=None):
    windows = capacity // LOW
    taken = min(most, windows)
    window_table = table16(taken * tiles)
    low_table = table16(LOW)
    if side is not None:
        side_code, side_ref = side
        tile_table = table16(tiles)
        side_table = table16(LANES)
        side_ref[...] = jnp.zeros_like(side_ref)

    def block_values(b):
        groups = [values(b * BLOCK + n) for n in range(BLOCK)]
        return [jnp.concatenate([g[v] for g in groups], 0) for v in range(len(groups[0]))]

    def add_block(b, first, with_side):
        rows = pl.ds(pl.multiple_of(b * (8 * BLOCK), 8 * BLOCK), 8 * BLOCK)
        slot = slot_ref[rows, :]
        value = block_values(b)
        tile = slot // capacity
        window = slot % capacity // LOW - first
        code = jnp.where((window >= 0) & (window < taken), window * tiles + tile, -1)
        left, right = one_hots(code.astype(F32), (slot % LOW).astype(F32), value, window_table, low_table)
        found = product(left, right)
        base = base_ref[b] + first
        base = jnp.concatenate([base, base], 1)
        for v in range(len(value)):
            parts = [found[(v * taken + i) * tiles : (v * taken + i + 1) * tiles] for i in range(taken)]
            for q in range(windows):
                put = jnp.where(base == q, parts[0], 0.0)
                for i in range(1, taken):
                    put = jnp.where(base == q - i, parts[i], put)
                total_ref[pl.ds((v * windows + q) * tiles, tiles), :] += put
        if with_side:
            code = jnp.concatenate([side_code(b * BLOCK + n) for n in range(BLOCK)], 0)
            left, right = one_hots(tile.astype(F32), code.astype(F32), value, tile_table, side_table)
            side_ref[...] += product(left, right)

    def body(b, carry):
        add_block(b, 0, side is not None)
        return carry

    lax.fori_loop(start, stop, body, 0, unroll=4)
    for first in range(taken, windows, taken):

        @pl.when(flag_ref[0] >= first)
        def _(first=first):
            def rest(b, carry):
                add_block(b, first, False)
                return carry

            lax.fori_loop(start, stop, rest, 0)


def store_slots(tiles, capacity, total_ref, part, scale, out_ref, pitch, row):
    windows = capacity // LOW
    for q in range(windows):
        first = total_ref[pl.ds((part * windows + q) * tiles, tiles), :]
        value = first * scale + total_ref[pl.ds(((part + 1) * windows + q) * tiles, tiles), :]
        for j in range(LOW // LANES):
            at = pl.ds(row + j * windows + q, tiles, stride=pitch)
            out_ref[at, :] = value[:, j * LANES : (j + 1) * LANES]


def cell_kernel(tiles, capacity, groups, row_count, *refs):
    slot_ref, row_ref, col_ref, _, out_ref = refs
    high_table = table16(tiles * capacity // LOW)
    low_table = table16(LOW)
    out_ref[...] = jnp.zeros_like(out_ref)

    def body(g, carry):
        slot = slot_ref[pl.ds(pl.multiple_of(g * 8, 8), 8), :]
        col = col_ref[group_at(g)]
        high = (col // LOW) * row_count + row_ref[group_at(g)]
        left, right = one_hots(
            (slot % capacity // LOW * tiles + slot // capacity).astype(F32),
            (slot % LOW).astype(F32),
            [high.astype(F32), (col % LOW).astype(F32)],
            high_table,
            low_table,
        )
        out_ref[...] += product(left, right)
        return carry

    lax.fori_loop(0, groups, body, 0, unroll=16)


def weir_kernel(sections, steps, tiles, capacity, row_count, col_count, *refs):
    position_ref, own_ref, other_ref, map_ref = refs[:4]
    solved_ref, slot_ref, base_ref, flag_ref, cells_ref = refs[4:9]
    crest_ref, regime_ref, row_ref, col_ref = refs[9:13]
    state_out, out_ref, state_ref, phase_ref, total_ref, side_ref, sems = refs[13:]
    late = ((position_ref[0] >> (steps - 1)) & 1) == 1
    own = [load_pair(own_ref, 0), load_square(own_ref, 2)]
    other = [load_pair(other_ref, 0), load_square(other_ref, 2)]
    tail_y, tail_right = pick(late, other, own)
    head_y, head_left = pick(late, own, other)
    head = meet(head_y, head_left, tail_y, tail_right)[1]
    tail = add(tail_y, mat_vec(tail_right, head))
    zero = jnp.zeros(tail[0].shape, F32)
    outer_before = pick(late, tail, [zero, zero])
    outer_after = pick(late, [zero, zero], head)
    before, after = (
        add(
            load_pair(map_ref, n + 8),
            add(
                mat_vec(load_square(map_ref, n), outer_before),
                mat_vec(load_square(map_ref, n + 4), outer_after),
            ),
        )
        for n in (0, 10)
    )
    for k in range(sections):
        for i in range(2):
            state = solved_ref[k, i]
            for j in range(2):
                state = state + solved_ref[k, 2 + 2 * i + j] * before[j]
                state = state + solved_ref[k, 6 + 2 * i + j] * after[j]
            state_ref[pl.ds(k * 16 + i, 8, stride=2), :] = state
            if i == 0:
                phase_ref[pl.ds((k // 8) * 64 + k % 8, 8, stride=8), :] = state

    state_copy = pltpu.make_async_copy(state_ref, state_out, sems.at[0])
    state_copy.start()

    def values(g):
        phase = phase_ref[pl.ds(pl.multiple_of(g * 8, 8), 8), :]
        regime = regime_ref[group_at(g)]
        head = jnp.maximum(phase - crest_ref[group_at(g)], 0.0)
        free = jnp.where(regime == 0, FREE_COEF * head * jnp.sqrt(head), 0.0)
        sub = jnp.where(
            regime == 1,
            SUB_COEF * jnp.sqrt(head + SUB_OFFSET),
            jnp.where(regime == 2, GATE_COEF, 0.0),
        )
        return [*halves(WEIR_GAIN * (free + sub * phase)), *halves(WEIR_GAIN * sub)]

    def side_code(g):
        col = col_ref[group_at(g)]
        place = jnp.where(col < 2, col, jnp.where(col >= col_count - 2, col - (col_count - 4), -1))
        return jnp.where(place >= 0, place * row_count + row_ref[group_at(g)], -1)

    total_ref[...] = jnp.zeros_like(total_ref)
    side = (side_code, side_ref)
    fill_slots(tiles, capacity, 0, sections // BLOCK, 2, slot_ref, base_ref, flag_ref, values, total_ref, side)
    rows_each = capacity // LANES
    pitch = 3 * rows_each + 2
    at = lax.broadcasted_iota(jnp.int32, (tiles, LANES), 1)
    first_cols = at < 2 * row_count
    for v in range(2):
        store_slots(tiles, capacity, total_ref, 2 * v, 1.0, out_ref, pitch, v * rows_each)
        sums = side_ref[pl.ds(2 * v * tiles, tiles), :] + side_ref[pl.ds((2 * v + 1) * tiles, tiles), :]
        beside = jnp.where(first_cols, pltpu.roll(sums, tiles - 1, 0), pltpu.roll(sums, 1, 0))
        out_ref[pl.ds(3 * rows_each + v, tiles, stride=pitch), :] = beside
    store_slots(tiles, capacity, cells_ref, 0, float(LOW), out_ref, pitch, 2 * rows_each)
    state_copy.wait()


def side_lanes(n):
    at = lax.broadcasted_iota(jnp.int32, (8, LANES), 1)
    return (at == 2 * n) | (at == 2 * n + 1)


def stage_kernel(row_count, col_count, *refs):
    tile_ref, left_ref, right_ref, wet_ref, sems = refs[6:]
    for copy in start_copies(refs[:5], [tile_ref.at[n] for n in range(4)] + [wet_ref], sems):
        copy.wait()
    tile_ref[4] = wet_ref[...].astype(F32) * (TIME_STEP / CELL_WIDTH)
    left = jnp.zeros(left_ref.shape, F32)
    right = left
    for t in range(row_count // 8):
        for n in range(5):
            at = 5 * t + n
            first = tile_ref[n, pl.ds(8 * t, 8), pl.ds(0, LANES)]
            last = tile_ref[n, pl.ds(8 * t, 8), pl.ds(col_count - LANES, LANES)]
            left = jnp.where(side_lanes(at), pltpu.roll(first, 2 * at, 1), left)
            right = jnp.where(side_lanes(at), pltpu.roll(last, 2 * at + 2, 1), right)
    left_ref[...] = left
    right_ref[...] = right


def unpacked(strip, n, rows, lane):
    parts = [pltpu.roll(strip, (lane - 2 * (5 * t + n)) % LANES, 1) for t in range(rows // 8)]
    return jnp.concatenate(parts, 0)


def apply_kernel(sources, rows_each, row_count, col_count, *refs):
    in_ref, tile_ref, before_ref, after_ref = refs[:4]
    depth_ref, top_ref, bottom_ref, side_ref, total_ref = refs[4:]
    pitch = 3 * rows_each + 2
    high_count = row_count * col_count // LOW
    high_table = table16(high_count)
    low_table = table16(LOW)
    total_ref[...] = jnp.zeros_like(total_ref)
    step = 8 // rows_each if rows_each < 8 else 1

    def body(g, carry):
        def part(v):
            return jnp.concatenate(
                [in_ref[pl.ds((g * step + n) * pitch + v * rows_each, rows_each), :] for n in range(step)], 0
            )

        cell = part(2).astype(jnp.int32)
        left, right = one_hots(
            (cell // LOW).astype(F32),
            (cell % LOW).astype(F32),
            [*halves(part(0)), *halves(part(1))],
            high_table,
            low_table,
        )
        total_ref[...] += product(left, right)
        return carry

    lax.fori_loop(0, sources // step, body, 0, unroll=32)
    for n in range(col_count // LOW):
        def summed(v):
            start = 2 * v * high_count + n * row_count
            return total_ref[pl.ds(start, row_count), :] + total_ref[pl.ds(start + high_count, row_count), :]

        cols = pl.ds(n * LOW, LOW)
        depth = tile_ref[0, :, cols]
        surface = tile_ref[1, :, cols] + depth
        depth_ref[:, cols] = jnp.maximum(depth + (summed(0) - summed(1) * surface), 0.0)
    row_at = lax.broadcasted_iota(jnp.int32, (row_count, LANES), 0)
    col_at = lax.broadcasted_iota(jnp.int32, (row_count, LANES), 1)

    def columns(v):
        sums = jnp.sum(in_ref[pl.ds(3 * rows_each + v, sources, stride=pitch), :], axis=0, keepdims=True)
        result = jnp.zeros((row_count, LANES), F32)
        for place, lane in enumerate((0, 1, LANES - 2, LANES - 1)):
            wanted = col_at == place * row_count + row_at
            column = jnp.sum(jnp.where(wanted, sums, 0.0), axis=1, keepdims=True)
            result = jnp.where(col_at == lane, column, result)
        return result

    before, after = before_ref[...], after_ref[...]
    for n in range(5):
        right = unpacked(after, n, row_count, 0)
        left = unpacked(before, n, row_count, LANES - 2)
        side_ref[n] = jnp.where(col_at < LANES // 2, right, left)
    depth = side_ref[0]
    surface = side_ref[1] + depth
    side_ref[0] = jnp.maximum(depth + (columns(0) - columns(1) * surface), 0.0)
    inner, outer = pl.ds(0, col_count), pl.ds(col_count, LANES)
    for out, near, rows in ((top_ref, 0, (0, 1)), (bottom_ref, row_count - 1, (row_count - 2, row_count - 1))):
        for n in range(5):
            for j in range(2 if n < 3 else 1):
                row = pl.ds(rows[j] if n < 3 else near, 1)
                at = pl.ds(2 * n + j if n < 3 else 3 + n, 1)
                out[at, inner] = depth_ref[row, :] if n == 0 else tile_ref[n, row, :]
                out[at, outer] = side_ref[n, row, :]


def face_flux(eta_here, eta_next, bed_here, bed_next, old_flux):
    flow_depth = jnp.maximum(
        jnp.maximum(eta_here, eta_next) - jnp.maximum(bed_here, bed_next), DEPTH_FLOOR
    )
    gradient = (eta_next - eta_here) / CELL_WIDTH
    pushed = old_flux - GRAVITY * TIME_STEP * flow_depth * gradient
    friction = jnp.exp((-7.0 / 3.0) * jnp.log(flow_depth))
    return pushed / (1.0 + GRAVITY * TIME_STEP * MANNING_SQ * jnp.abs(old_flux) * friction)


def flood_kernel(row_count, col_count, *refs):
    closed_ref, tile_ref, depth_ref, side_ref, above_ref, below_ref = refs[:6]
    outs, kept, sems = refs[6:9], refs[9], refs[10]
    at = lax.broadcasted_iota(jnp.int32, (8, 1), 0)
    arrays = []
    for n in range(5):
        own = jnp.concatenate([depth_ref[...] if n == 0 else tile_ref[n], side_ref[n]], 1)
        first_row = 2 * n if n < 3 else 3 + n
        second_row = first_row + 1 if n < 3 else first_row
        halo = jnp.where(at == 0, below_ref[pl.ds(first_row, 1), :], 0.0)
        halo = jnp.where(at == 1, below_ref[pl.ds(second_row, 1), :], halo)
        halo = jnp.where(at == 6, above_ref[pl.ds(first_row, 1), :], halo)
        halo = jnp.where(at == 7, above_ref[pl.ds(second_row, 1), :], halo)
        arrays.append(jnp.concatenate([own, halo], 0))
    depth, bed, first, second, wet = arrays
    shape = depth.shape
    row_at = lax.broadcasted_iota(jnp.int32, shape, 0)
    col_at = lax.broadcasted_iota(jnp.int32, shape, 1)
    first_shut = (row_at == closed_ref[0]) | (row_at == closed_ref[1])
    second_shut = (col_at == closed_ref[2]) | (col_at == closed_ref[3])
    down = lambda x: pltpu.roll(x, shape[0] - 1, 0)
    up = lambda x: pltpu.roll(x, 1, 0)
    onward = lambda x: pltpu.roll(x, shape[1] - 1, 1)
    back = lambda x: pltpu.roll(x, 1, 1)
    bed_down = down(bed)
    bed_onward = onward(bed)
    copies = []

    def finish(n, value):
        kept[n] = value[:row_count, :col_count]
        copies.append(pltpu.make_async_copy(kept.at[n], outs[n], sems.at[n]))
        copies[-1].start()

    for step in range(2):
        eta = bed + depth
        first = jnp.where(first_shut, 0.0, face_flux(eta, down(eta), bed, bed_down, first))
        if step == 1:
            finish(1, first)
        second = jnp.where(second_shut, 0.0, face_flux(eta, onward(eta), bed, bed_onward, second))
        if step == 1:
            finish(2, second)
        depth = depth + wet * (up(first) - first + (back(second) - second))
    finish(0, depth)
    for copy in copies:
        copy.wait()


def exchanged(block, axis, step):
    return lax.ppermute(block, axis, [(i, i ^ (1 << step)) for i in range(lax.axis_size(axis))])


def swapped(first, last, axis, ring):
    count = lax.axis_size(axis)
    odd = lax.axis_index(axis) % 2 == 1
    inner = [(i, i ^ 1) for i in range(count)]
    outer = [] if ring else [(0, 0), (count - 1, count - 1)]
    for i in range(1, count if ring else count - 1, 2):
        outer += [(i, (i + 1) % count), ((i + 1) % count, i)]
    two = lax.ppermute(jnp.where(odd, last, first), axis, outer)
    one = lax.ppermute(jnp.where(odd, first, last), axis, inner)
    return jnp.where(odd, one, two), jnp.where(odd, two, one)


def local(
    river_lower,
    river_main,
    river_upper,
    river_rhs,
    weir_crest,
    weir_regime,
    weir_tile,
    weir_row,
    weir_col,
    bed_level,
    water_depth,
    flux_first,
    flux_second,
    wet_mask,
):
    sections, chains = weir_crest.shape
    row_count, col_count = water_depth.shape
    row_size = lax.axis_size("row")
    col_size = lax.axis_size("col")
    row_at = lax.axis_index("row")
    col_at = lax.axis_index("col")
    tiles = row_size * col_size
    weirs = sections * chains
    capacity = 2 * weirs // tiles
    lane_rows = chains // LANES

    def block_rows(array):
        split = array.reshape(sections, 2, 2, lane_rows, LANES)
        return split.transpose(0, 1, 3, 2, 4).reshape(-1, LANES)

    rhs_rows = river_rhs.reshape(sections, 2, lane_rows, LANES).transpose(0, 2, 1, 3).reshape(-1, LANES)
    rows = weirs // LANES
    high_count = tiles * capacity // LOW
    rows_each = capacity // LANES
    pitch = 3 * rows_each + 2
    river_block = pltpu.VMEM((sections * 4 * lane_rows, LANES), F32)
    blocks = sections // BLOCK
    steps = row_size.bit_length() - 1
    weir_shape = (sections, chains)
    solved, packed, crest, regime, weir_rows, weir_cols = pl.pallas_call(
        functools.partial(solve_kernel, sections),
        out_shape=(
            pltpu.VMEM((sections, 10, lane_rows, LANES), F32),
            pltpu.VMEM((20, lane_rows, LANES), F32),
            pltpu.VMEM(weir_shape, F32),
            pltpu.VMEM(weir_shape, jnp.int32),
            pltpu.VMEM(weir_shape, jnp.int32),
            pltpu.VMEM(weir_shape, jnp.int32),
        ),
        in_specs=[ANY] * 8,
        out_specs=(VMEM,) * 6,
        scratch_shapes=[
            river_block,
            river_block,
            river_block,
            pltpu.VMEM((sections * 2 * lane_rows, LANES), F32),
            pltpu.SemaphoreType.DMA((4, 4)),
            pltpu.SemaphoreType.DMA((4,)),
        ],
        compiler_params=WIDE,
        name="solve",
    )(
        block_rows(river_lower),
        block_rows(river_main),
        block_rows(river_upper),
        rhs_rows,
        weir_crest,
        weir_regime,
        weir_row,
        weir_col,
    )
    *places, whole_slots = pl.pallas_call(
        functools.partial(rank_kernel, tiles, capacity, blocks),
        out_shape=(
            jax.ShapeDtypeStruct((rows, LANES), jnp.int32),
            jax.ShapeDtypeStruct((blocks, tiles, LANES), F32),
            jax.ShapeDtypeStruct((1,), jnp.int32),
            jax.ShapeDtypeStruct((rows, LANES), jnp.int32),
        ),
        in_specs=[VMEM],
        out_specs=(VMEM, VMEM, SMEM, VMEM),
        compiler_params=PARAMS,
        cost_estimate=pl.CostEstimate(flops=2 * tiles * weirs * LOW, bytes_accessed=2**17, transcendentals=0),
        name="rank",
    )(weir_tile.reshape(rows, LANES))
    group, known = packed, ()
    for step in range(steps - 1):
        other = exchanged(group, "row", step)
        last = step == steps - 2
        twenty = jax.ShapeDtypeStruct((20, lane_rows, LANES), F32)
        group, own_map = pl.pallas_call(
            functools.partial(merge_kernel, step, step == 0, last),
            out_shape=(jax.ShapeDtypeStruct((6, lane_rows, LANES), F32) if last else twenty, twenty),
            in_specs=[SMEM] + [VMEM] * (2 + len(known)),
            out_specs=(VMEM, VMEM),
            compiler_params=PARAMS,
            name="merge",
        )(row_at.reshape(1), group, other, *known)
        known = (own_map,)
    sent = group
    met = exchanged(sent, "row", steps - 1)
    cells = pl.pallas_call(
        functools.partial(cell_kernel, tiles, capacity, rows // 8, row_count),
        out_shape=jax.ShapeDtypeStruct((2 * high_count, LOW), F32),
        in_specs=[VMEM, VMEM, VMEM, ANY],
        out_specs=VMEM,
        compiler_params=PARAMS,
        cost_estimate=pl.CostEstimate(flops=4 * high_count * LOW * weirs, bytes_accessed=2**18, transcendentals=0),
        name="cells",
    )(whole_slots, weir_rows, weir_cols, sent)
    state_shape = jax.ShapeDtypeStruct((sections * lane_rows * 2, LANES), F32)
    state_rows, outgoing = pl.pallas_call(
        functools.partial(weir_kernel, sections, steps, tiles, capacity, row_count, col_count),
        out_shape=(state_shape, jax.ShapeDtypeStruct((tiles * pitch, LANES), F32)),
        in_specs=[SMEM] + [VMEM] * 5 + [VMEM, SMEM] + [VMEM] * 5,
        out_specs=(ANY, VMEM),
        scratch_shapes=[
            pltpu.VMEM(state_shape.shape, F32),
            pltpu.VMEM((rows, LANES), F32),
            pltpu.VMEM((4 * high_count, LOW), F32),
            pltpu.VMEM((4 * tiles, LANES), F32),
            pltpu.SemaphoreType.DMA((1,)),
        ],
        compiler_params=PARAMS,
        name="weirs",
    )(row_at.reshape(1), sent, met, own_map, solved, *places, cells, crest, regime, weir_rows, weir_cols)
    river_state = (
        state_rows.reshape(sections, lane_rows, 2, LANES).transpose(0, 2, 1, 3).reshape(sections, 2, chains)
    )
    messages = outgoing.reshape(tiles, pitch, 1, LANES)
    arrived = lax.all_to_all(messages, ("row", "col"), split_axis=0, concat_axis=0, tiled=True)
    tile_stack = jax.ShapeDtypeStruct((5, row_count, col_count), F32)
    side = jax.ShapeDtypeStruct((8, LANES), F32)
    tile, left, right = pl.pallas_call(
        functools.partial(stage_kernel, row_count, col_count),
        out_shape=(tile_stack, side, side),
        in_specs=[ANY] * 6,
        out_specs=(VMEM, VMEM, VMEM),
        scratch_shapes=[pltpu.VMEM((row_count, col_count), jnp.int32), pltpu.SemaphoreType.DMA((5,))],
        compiler_params=PARAMS,
        name="stage",
    )(water_depth, bed_level, flux_first, flux_second, wet_mask, state_rows)
    before, after = swapped(left, right, "col", False)
    tile_out = jax.ShapeDtypeStruct((row_count, col_count), F32)
    edge = jax.ShapeDtypeStruct((8, col_count + LANES), F32)
    flank = jax.ShapeDtypeStruct((5, row_count, LANES), F32)
    wetted, top, bottom, side = pl.pallas_call(
        functools.partial(apply_kernel, tiles, rows_each, row_count, col_count),
        out_shape=(tile_out, edge, edge, flank),
        in_specs=[VMEM] * 4,
        out_specs=(VMEM,) * 4,
        scratch_shapes=[pltpu.VMEM((4 * row_count * col_count // LOW, LOW), F32)],
        compiler_params=PARAMS,
        name="apply",
    )(arrived.reshape(tiles * pitch, LANES), tile, before, after)
    above, below = swapped(top, bottom, "row", True)
    closed = jnp.stack(
        [
            jnp.where(row_at == 0, row_count + 7, -1),
            jnp.where(row_at == row_size - 1, row_count - 1, -1),
            jnp.where(col_at == 0, col_count + LANES - 1, -1),
            jnp.where(col_at == col_size - 1, col_count - 1, -1),
        ]
    ).astype(jnp.int32)
    depth_out, first_out, second_out = pl.pallas_call(
        functools.partial(flood_kernel, row_count, col_count),
        out_shape=(tile_out, tile_out, tile_out),
        in_specs=[SMEM] + [VMEM] * 5,
        out_specs=(ANY, ANY, ANY),
        scratch_shapes=[pltpu.VMEM((3, row_count, col_count), F32), pltpu.SemaphoreType.DMA((3,))],
        compiler_params=PARAMS,
        name="flood",
    )(closed, tile, wetted, side, above, below)
    return (river_state, depth_out, first_out, second_out)


def solution(mesh):
    in_specs = (
        P("row", None, None, "col"),
        P("row", None, None, "col"),
        P("row", None, None, "col"),
        P("row", None, "col"),
        P("row", "col"),
        P("row", "col"),
        P("row", "col", None, None, None),
        P("row", "col"),
        P("row", "col"),
        P("row", "col"),
        P("row", "col"),
        P("row", "col"),
        P("row", "col"),
        P("row", "col"),
    )
    out_specs = (P("row", None, "col"), P("row", "col"), P("row", "col"), P("row", "col"))
    return jax.shard_map(local, mesh=mesh, in_specs=in_specs, out_specs=out_specs, check_vma=False)
```

```python
import functools

import jax
import jax.numpy as jnp
from jax import lax
from jax.experimental import pallas as pl
from jax.experimental.pallas import tpu as pltpu
from jax.sharding import PartitionSpec as P

GRAVITY = 9.81
TIME_STEP = 1.0
CELL_WIDTH = 10.0
MANNING_SQ = 0.0009
DEPTH_FLOOR = 0.05
WEIR_GAIN = 0.5
FREE_COEF = 0.5
SUB_COEF = 0.4
SUB_OFFSET = 0.25
GATE_COEF = 0.2

F32 = jnp.float32
BF16 = jnp.bfloat16
LANES = 128
LOW = 256
BLOCK = 2
VMEM = pl.BlockSpec(memory_space=pltpu.VMEM)
SMEM = pl.BlockSpec(memory_space=pltpu.SMEM)
ANY = pl.BlockSpec(memory_space=pl.ANY)
HBM = pl.BlockSpec(memory_space=pltpu.HBM)
WIDE = pltpu.CompilerParams(vmem_limit_bytes=60 * 2**20)
PARAMS = pltpu.CompilerParams(vmem_limit_bytes=40 * 2**20)


def start_copies(sources, targets, sems):
    copies = [pltpu.make_async_copy(s, t, sems.at[n]) for n, (s, t) in enumerate(zip(sources, targets))]
    for copy in copies:
        copy.start()
    return copies


def mat_mat(a, b):
    return [[a[i][0] * b[0][j] + a[i][1] * b[1][j] for j in range(2)] for i in range(2)]


def mat_vec(a, v):
    return [a[i][0] * v[0] + a[i][1] * v[1] for i in range(2)]


def mat_sub(a, b):
    return [[a[i][j] - b[i][j] for j in range(2)] for i in range(2)]


def mat_neg(a):
    return [[-a[i][j] for j in range(2)] for i in range(2)]


def mat_inv(m):
    scale = 1.0 / (m[0][0] * m[1][1] - m[0][1] * m[1][0])
    return [[m[1][1] * scale, -m[0][1] * scale], [-m[1][0] * scale, m[0][0] * scale]]


def rank_kernel(tiles, capacity, blocks, tile_ref, slot_ref, base_ref, flag_ref):
    table = lax.broadcasted_iota(jnp.int32, (tiles, LANES), 0)
    first_slot = table.astype(F32) * capacity
    row_at = lax.broadcasted_iota(jnp.int32, (LANES, 2 * LANES), 0)
    col_at = lax.broadcasted_iota(jnp.int32, (LANES, 2 * LANES), 1)
    earlier = jnp.where(row_at < col_at, 1.0, 0.0).astype(BF16)

    def body(b, carry):
        offset, most = carry
        base = jnp.floor((offset - first_slot) * (1.0 / LOW))
        base_ref[b] = base
        for n in range(BLOCK):
            g = b * BLOCK + n
            ids = tile_ref[pl.ds((g // 8) * 64 + g % 8, 8, stride=8), :]
            hits = [ids[r : r + 1, :] == table for r in range(8)]
            hot = jnp.concatenate([jnp.where(h, 1.0, 0.0).astype(BF16) for h in hits], 0)
            counts = jnp.dot(hot, earlier, preferred_element_type=F32)
            rows = []
            for r in range(8):
                part = counts[r * tiles : (r + 1) * tiles]
                place = jnp.where(hits[r], part[:, :LANES] + offset, 0.0)
                rows.append(jnp.sum(place, axis=0, keepdims=True))
                offset = offset + part[:, LANES:]
            slot_ref[pl.ds(pl.multiple_of(g * 8, 8), 8), :] = jnp.concatenate(rows, 0).astype(jnp.int32)
        last = jnp.floor((offset - first_slot - 1.0) * (1.0 / LOW)) - base
        return offset, jnp.maximum(most, last)

    most = lax.fori_loop(0, blocks, body, (first_slot, jnp.zeros((tiles, LANES), F32)), unroll=8)[1]
    flag_ref[0] = jnp.max(most).astype(jnp.int32)


def solve_kernel(sections, *refs):
    inputs, later = refs[:4], refs[4:8]
    solved_ref, packed_ref = refs[8:10]
    fetched = refs[10:14]
    lower_ref, main_ref, upper_ref, rhs_ref, sems, later_sems = refs[14:]
    pieces = []
    for n in range(4):
        parts = [[r.at[pl.ds(n * r.shape[0] // 4, r.shape[0] // 4)] for r in group] for group in (inputs, refs[14:18])]
        pieces.append(start_copies(*parts, sems.at[n]))
    copies = start_copies(later, fetched, later_sems)

    def block(ref, k):
        return [[ref[pl.ds(k * 32 + i * 16 + j, 8, stride=2), :] for j in range(2)] for i in range(2)]

    couples = []
    for k in range(sections):
        if k % (sections // 4) == 0:
            for copy in pieces[k // (sections // 4)]:
                copy.wait()
        lower = block(lower_ref, k)
        main = block(main_ref, k)
        upper = block(upper_ref, k)
        right = [rhs_ref[pl.ds(k * 16 + j, 8, stride=2), :] for j in range(2)]
        if k == 0:
            inverse = mat_inv(main)
            left = mat_neg(mat_mat(inverse, lower))
            value = mat_vec(inverse, right)
        else:
            inverse = mat_inv(mat_sub(main, mat_mat(lower, couples[-1])))
            left = mat_neg(mat_mat(inverse, mat_mat(lower, left)))
            moved = mat_vec(lower, value)
            value = mat_vec(inverse, [right[i] - moved[i] for i in range(2)])
        couples.append(mat_mat(inverse, upper))
        for i in range(2):
            solved_ref[k, i] = value[i]
            for j in range(2):
                solved_ref[k, 2 + 2 * i + j] = left[i][j]
    spike = mat_neg(couples[-1])
    tail = (value, left, spike)
    for i in range(2):
        for j in range(2):
            solved_ref[sections - 1, 6 + 2 * i + j] = spike[i][j]
    for k in range(sections - 2, -1, -1):
        couple = couples[k]
        after = mat_vec(couple, value)
        value = [solved_ref[k, i] - after[i] for i in range(2)]
        after = mat_mat(couple, left)
        left = [[solved_ref[k, 2 + 2 * i + j] - after[i][j] for j in range(2)] for i in range(2)]
        spike = mat_neg(mat_mat(couple, spike))
        for i in range(2):
            solved_ref[k, i] = value[i]
            for j in range(2):
                solved_ref[k, 2 + 2 * i + j] = left[i][j]
                solved_ref[k, 6 + 2 * i + j] = spike[i][j]
    for i in range(2):
        packed_ref[i] = value[i]
        packed_ref[2 + i] = tail[0][i]
        for j in range(2):
            packed_ref[4 + 2 * i + j] = left[i][j]
            packed_ref[8 + 2 * i + j] = tail[1][i][j]
            packed_ref[12 + 2 * i + j] = spike[i][j]
            packed_ref[16 + 2 * i + j] = tail[2][i][j]
    for copy in copies:
        copy.wait()


def load_pair(ref, n):
    return [ref[n], ref[n + 1]]


def load_square(ref, n):
    return [load_pair(ref, n), load_pair(ref, n + 2)]


def store_all(ref, values):
    flat = []
    for value in values:
        flat += [*value[0], *value[1]] if isinstance(value[0], list) else value
    for n, item in enumerate(flat):
        ref[n] = item


def pick(flag, one, other):
    if isinstance(one, list):
        return [pick(flag, a, b) for a, b in zip(one, other)]
    return jnp.where(flag, one, other)


def add(a, b):
    if isinstance(a, list):
        return [add(x, y) for x, y in zip(a, b)]
    return a + b


def meet(head_y, head_left, tail_y, tail_right):
    inner = mat_mat(head_left, tail_right)
    inverse = mat_inv([[1.0 - inner[0][0], -inner[0][1]], [-inner[1][0], 1.0 - inner[1][1]]])
    return inverse, mat_vec(inverse, add(head_y, mat_vec(head_left, tail_y)))


def merge_kernel(step, first, last, position_ref, own_ref, other_ref, *refs):
    known_ref = None if first else refs[0]
    out_ref, map_ref = refs[-2:]
    position = position_ref[0]
    late = ((position >> step) & 1) == 1

    def group(ref):
        return [load_pair(ref, 0), load_pair(ref, 2)] + [load_square(ref, n) for n in (4, 8, 12, 16)]

    own, other = group(own_ref), group(other_ref)
    head_y, tail_y, head_left, tail_left, head_right, tail_right = pick(late, other, own)
    next_head_y, next_tail_y, next_head_left, next_tail_left, next_head_right, next_tail_right = pick(
        late, own, other
    )
    inverse, head = meet(next_head_y, next_head_left, tail_y, tail_right)
    head_before = mat_mat(inverse, mat_mat(next_head_left, tail_left))
    head_after = mat_mat(inverse, next_head_right)
    tail = add(tail_y, mat_vec(tail_right, head))
    tail_before = add(tail_left, mat_mat(tail_right, head_before))
    tail_after = mat_mat(tail_right, head_after)
    joined = [
        add(head_y, mat_vec(head_right, head)),
        add(next_tail_y, mat_vec(next_tail_left, tail)),
        add(head_left, mat_mat(head_right, head_before)),
        mat_mat(next_tail_left, tail_before),
        mat_mat(head_right, head_after),
        add(next_tail_right, mat_mat(next_tail_left, tail_after)),
    ]
    zero = jnp.zeros(tail[0].shape, F32)
    one = zero + 1.0
    unit, none, nothing = [[one, zero], [zero, one]], [[zero, zero], [zero, zero]], [zero, zero]
    if first:
        maps = [
            [pick(late, tail_before, unit), pick(late, tail_after, none), pick(late, tail, nothing)],
            [pick(late, none, head_before), pick(late, unit, head_after), pick(late, nothing, head)],
        ]
    else:
        maps = []
        for n in range(2):
            by_before = load_square(known_ref, 10 * n)
            by_after = load_square(known_ref, 10 * n + 4)
            value = load_pair(known_ref, 10 * n + 8)
            maps.append(
                [
                    pick(late, mat_mat(by_before, tail_before), add(by_before, mat_mat(by_after, head_before))),
                    pick(late, add(by_after, mat_mat(by_before, tail_after)), mat_mat(by_after, head_after)),
                    pick(late, add(value, mat_vec(by_before, tail)), add(value, mat_vec(by_after, head))),
                ]
            )
    store_all(map_ref, maps[0] + maps[1])
    if last:
        later = ((position >> (step + 1)) & 1) == 1
        store_all(out_ref, [pick(later, joined[0], joined[1]), pick(later, joined[2], joined[5])])
    else:
        store_all(out_ref, joined)


def rows16(row):
    return jnp.broadcast_to(row, (16, LANES)).astype(BF16)


def table16(count):
    shape = (count // 16, 16, LANES)
    at = lax.broadcasted_iota(jnp.int32, shape, 0) * 16 + lax.broadcasted_iota(jnp.int32, shape, 1)
    return at.astype(F32).astype(BF16)


def halves(value):
    high = value.astype(BF16).astype(F32)
    return high, value - high


def one_hots(high, low, values, high_table, low_table):
    one = jnp.ones((), BF16)
    zero = jnp.zeros((), BF16)
    left, right = [], []
    for r in range(high.shape[0]):
        hit = high_table == rows16(high[r : r + 1])[None]
        left.append(
            jnp.concatenate(
                [jnp.where(hit, rows16(v[r : r + 1])[None], zero).reshape(-1, LANES) for v in values], 0
            )
        )
        hit = low_table == rows16(low[r : r + 1])[None]
        right.append(jnp.where(hit, one, zero).reshape(-1, LANES))
    return jnp.concatenate(left, 1), jnp.concatenate(right, 1)


def product(left, right):
    return lax.dot_general(left, right, (((1,), (1,)), ((), ())), preferred_element_type=F32)


def group_at(g):
    over = pl.multiple_of((g // 8) * 8, 8)
    along = pl.multiple_of((g % 8) * LANES, LANES)
    return (pl.ds(over, 8), pl.ds(along, LANES))


def fill_slots(tiles, capacity, blocks, slot_ref, base_ref, flag_ref, values, total_ref, side_code, side_ref):
    windows = capacity // LOW
    taken = min(2, windows)
    low_table = table16(LOW)
    side_table = table16(LANES)
    first_window = lax.broadcasted_iota(jnp.int32, (tiles, LANES), 0).astype(F32) * windows
    one = jnp.ones((), BF16)
    zero = jnp.zeros((), BF16)
    total_ref[...] = jnp.zeros_like(total_ref)
    side_ref[...] = jnp.zeros_like(side_ref)

    def add_block(b, first):
        rows = pl.ds(pl.multiple_of(b * (8 * BLOCK), 8 * BLOCK), 8 * BLOCK)
        slot = slot_ref[rows, :]
        window = (slot // LOW).astype(F32)
        low = (slot % LOW).astype(F32)
        place = jnp.concatenate([side_code(b * BLOCK + n) for n in range(BLOCK)], 0).astype(F32)
        groups = [values(b * BLOCK + n) for n in range(BLOCK)]
        value = [jnp.concatenate([g[v] for g in groups], 0) for v in range(len(groups[0]))]
        base = base_ref[b] + first
        covered = [jnp.where(base + i < windows, first_window + (base + i), -1.0) for i in range(taken)]
        window_table = jnp.concatenate(covered, 0).astype(BF16).reshape(taken * tiles // 16, 16, LANES)
        left, right, side_left, side_right = [], [], [], []
        for r in range(8 * BLOCK):
            hit = window_table == rows16(window[r : r + 1])[None]
            parts = [jnp.where(hit, rows16(v[r : r + 1])[None], zero).reshape(-1, LANES) for v in value]
            left.append(jnp.concatenate(parts, 0))
            if taken == 2:
                parts = [p[:tiles] + p[tiles:] for p in parts]
            side_left.append(jnp.concatenate(parts, 0))
            hit = low_table == rows16(low[r : r + 1])[None]
            right.append(jnp.where(hit, one, zero).reshape(-1, LANES))
            hit = side_table == rows16(place[r : r + 1])[None]
            side_right.append(jnp.where(hit, one, zero).reshape(-1, LANES))
        found = product(jnp.concatenate(left, 1), jnp.concatenate(right, 1))
        base = jnp.concatenate([base, base], 1)
        for v in range(len(value) // 2):
            parts = []
            for i in range(taken):
                high, rest = (((2 * v + n) * taken + i) * tiles for n in range(2))
                parts.append(found[high : high + tiles] + found[rest : rest + tiles])
            for q in range(windows):
                put = jnp.where(base == q, parts[0], 0.0)
                for i in range(1, taken):
                    put = jnp.where(base == q - i, parts[i], put)
                total_ref[pl.ds((v * windows + q) * tiles, tiles), :] += put
        side_ref[...] += product(jnp.concatenate(side_left, 1), jnp.concatenate(side_right, 1))

    def body(b, carry):
        add_block(b, 0)
        return carry

    lax.fori_loop(0, blocks, body, 0, unroll=4)
    for first in range(taken, windows, taken):

        @pl.when(flag_ref[0] >= first)
        def _(first=first):
            def rest(b, carry):
                add_block(b, first)
                return carry

            lax.fori_loop(0, blocks, rest, 0)


def store_slots(tiles, capacity, window_of, out_ref, pitch, row):
    windows = capacity // LOW
    for q in range(windows):
        value = window_of(q)
        for j in range(LOW // LANES):
            at = pl.ds(row + j * windows + q, tiles, stride=pitch)
            out_ref[at, :] = value[:, j * LANES : (j + 1) * LANES]


def cell_kernel(tiles, capacity, groups, row_count, *refs):
    slot_ref, row_ref, col_ref, _, out_ref = refs
    high_table = table16(tiles * capacity // LOW)
    low_table = table16(LOW)
    out_ref[...] = jnp.zeros_like(out_ref)

    def body(g, carry):
        slot = slot_ref[pl.ds(pl.multiple_of(g * 8, 8), 8), :]
        col = col_ref[group_at(g)]
        high = (col // LOW) * row_count + row_ref[group_at(g)]
        left, right = one_hots(
            (slot % capacity // LOW * tiles + slot // capacity).astype(F32),
            (slot % LOW).astype(F32),
            [high.astype(F32), (col % LOW).astype(F32)],
            high_table,
            low_table,
        )
        out_ref[...] += product(left, right)
        return carry

    lax.fori_loop(0, groups, body, 0, unroll=16)


def weir_kernel(sections, steps, tiles, capacity, row_count, col_count, *refs):
    position_ref, own_ref, other_ref, map_ref = refs[:4]
    solved_ref, slot_ref, base_ref, flag_ref, cells_ref = refs[4:9]
    crest_ref, regime_ref, row_ref, col_ref = refs[9:13]
    state_out, out_ref, state_ref, phase_ref, total_ref, side_ref, sems = refs[13:]
    late = ((position_ref[0] >> (steps - 1)) & 1) == 1
    own = [load_pair(own_ref, 0), load_square(own_ref, 2)]
    other = [load_pair(other_ref, 0), load_square(other_ref, 2)]
    tail_y, tail_right = pick(late, other, own)
    head_y, head_left = pick(late, own, other)
    head = meet(head_y, head_left, tail_y, tail_right)[1]
    tail = add(tail_y, mat_vec(tail_right, head))
    zero = jnp.zeros(tail[0].shape, F32)
    outer_before = pick(late, tail, [zero, zero])
    outer_after = pick(late, [zero, zero], head)
    before, after = (
        add(
            load_pair(map_ref, n + 8),
            add(
                mat_vec(load_square(map_ref, n), outer_before),
                mat_vec(load_square(map_ref, n + 4), outer_after),
            ),
        )
        for n in (0, 10)
    )
    for k in range(sections):
        for i in range(2):
            state = solved_ref[k, i]
            for j in range(2):
                state = state + solved_ref[k, 2 + 2 * i + j] * before[j]
                state = state + solved_ref[k, 6 + 2 * i + j] * after[j]
            state_ref[pl.ds(k * 16 + i, 8, stride=2), :] = state
            if i == 0:
                phase_ref[pl.ds((k // 8) * 64 + k % 8, 8, stride=8), :] = state

    state_copy = pltpu.make_async_copy(state_ref, state_out, sems.at[0])
    state_copy.start()

    def values(g):
        phase = phase_ref[pl.ds(pl.multiple_of(g * 8, 8), 8), :]
        regime = regime_ref[group_at(g)]
        head = jnp.maximum(phase - crest_ref[group_at(g)], 0.0)
        free = jnp.where(regime == 0, FREE_COEF * head * jnp.sqrt(head), 0.0)
        sub = jnp.where(
            regime == 1,
            SUB_COEF * jnp.sqrt(head + SUB_OFFSET),
            jnp.where(regime == 2, GATE_COEF, 0.0),
        )
        return [*halves(WEIR_GAIN * (free + sub * phase)), *halves(WEIR_GAIN * sub)]

    def side_code(g):
        col = col_ref[group_at(g)]
        place = jnp.where(col < 2, col, jnp.where(col >= col_count - 2, col - (col_count - 4), -1))
        return jnp.where(place >= 0, place * row_count + row_ref[group_at(g)], -1)

    blocks = sections // BLOCK
    fill_slots(tiles, capacity, blocks, slot_ref, base_ref, flag_ref, values, total_ref, side_code, side_ref)
    windows = capacity // LOW
    rows_each = capacity // LANES
    pitch = 3 * rows_each + 2
    at = lax.broadcasted_iota(jnp.int32, (tiles, LANES), 1)
    first_cols = at < 2 * row_count
    for v in range(2):
        window_of = lambda q: total_ref[pl.ds((v * windows + q) * tiles, tiles), :]
        store_slots(tiles, capacity, window_of, out_ref, pitch, v * rows_each)
        sums = side_ref[pl.ds(2 * v * tiles, tiles), :] + side_ref[pl.ds((2 * v + 1) * tiles, tiles), :]
        beside = jnp.where(first_cols, pltpu.roll(sums, tiles - 1, 0), pltpu.roll(sums, 1, 0))
        out_ref[pl.ds(3 * rows_each + v, tiles, stride=pitch), :] = beside
    cell_part = lambda n, q: cells_ref[pl.ds((n * windows + q) * tiles, tiles), :]
    window_of = lambda q: cell_part(0, q) * float(LOW) + cell_part(1, q)
    store_slots(tiles, capacity, window_of, out_ref, pitch, 2 * rows_each)
    state_copy.wait()


def side_lanes(n):
    at = lax.broadcasted_iota(jnp.int32, (8, LANES), 1)
    return (at == 2 * n) | (at == 2 * n + 1)


def stage_kernel(row_count, col_count, *refs):
    tile_ref, left_ref, right_ref, wet_ref, sems = refs[6:]
    for copy in start_copies(refs[:5], [tile_ref.at[n] for n in range(4)] + [wet_ref], sems):
        copy.wait()
    tile_ref[4] = wet_ref[...].astype(F32) * (TIME_STEP / CELL_WIDTH)
    left = jnp.zeros(left_ref.shape, F32)
    right = left
    for t in range(row_count // 8):
        for n in range(5):
            at = 5 * t + n
            first = tile_ref[n, pl.ds(8 * t, 8), pl.ds(0, LANES)]
            last = tile_ref[n, pl.ds(8 * t, 8), pl.ds(col_count - LANES, LANES)]
            left = jnp.where(side_lanes(at), pltpu.roll(first, 2 * at, 1), left)
            right = jnp.where(side_lanes(at), pltpu.roll(last, 2 * at + 2, 1), right)
    left_ref[...] = left
    right_ref[...] = right


def unpacked(strip, n, rows, lane):
    parts = [pltpu.roll(strip, (lane - 2 * (5 * t + n)) % LANES, 1) for t in range(rows // 8)]
    return jnp.concatenate(parts, 0)


def apply_kernel(sources, rows_each, row_count, col_count, *refs):
    in_ref, tile_ref, before_ref, after_ref = refs[:4]
    depth_ref, top_ref, bottom_ref, side_ref, total_ref = refs[4:]
    pitch = 3 * rows_each + 2
    high_count = row_count * col_count // LOW
    high_table = table16(high_count)
    low_table = table16(LOW)
    total_ref[...] = jnp.zeros_like(total_ref)
    step = 8 // rows_each if rows_each < 8 else 1

    def body(g, carry):
        def part(v):
            return jnp.concatenate(
                [in_ref[pl.ds((g * step + n) * pitch + v * rows_each, rows_each), :] for n in range(step)], 0
            )

        cell = part(2).astype(jnp.int32)
        left, right = one_hots(
            (cell // LOW).astype(F32),
            (cell % LOW).astype(F32),
            [*halves(part(0)), *halves(part(1))],
            high_table,
            low_table,
        )
        total_ref[...] += product(left, right)
        return carry

    lax.fori_loop(0, sources // step, body, 0, unroll=32)
    for n in range(col_count // LOW):
        def summed(v):
            start = 2 * v * high_count + n * row_count
            return total_ref[pl.ds(start, row_count), :] + total_ref[pl.ds(start + high_count, row_count), :]

        cols = pl.ds(n * LOW, LOW)
        depth = tile_ref[0, :, cols]
        surface = tile_ref[1, :, cols] + depth
        depth_ref[:, cols] = jnp.maximum(depth + (summed(0) - summed(1) * surface), 0.0)
    row_at = lax.broadcasted_iota(jnp.int32, (row_count, LANES), 0)
    col_at = lax.broadcasted_iota(jnp.int32, (row_count, LANES), 1)

    def columns(v):
        sums = jnp.sum(in_ref[pl.ds(3 * rows_each + v, sources, stride=pitch), :], axis=0, keepdims=True)
        result = jnp.zeros((row_count, LANES), F32)
        for place, lane in enumerate((0, 1, LANES - 2, LANES - 1)):
            wanted = col_at == place * row_count + row_at
            column = jnp.sum(jnp.where(wanted, sums, 0.0), axis=1, keepdims=True)
            result = jnp.where(col_at == lane, column, result)
        return result

    before, after = before_ref[...], after_ref[...]
    for n in range(5):
        right = unpacked(after, n, row_count, 0)
        left = unpacked(before, n, row_count, LANES - 2)
        side_ref[n] = jnp.where(col_at < LANES // 2, right, left)
    depth = side_ref[0]
    surface = side_ref[1] + depth
    side_ref[0] = jnp.maximum(depth + (columns(0) - columns(1) * surface), 0.0)
    inner, outer = pl.ds(0, col_count), pl.ds(col_count, LANES)
    for out, near, rows in ((top_ref, 0, (0, 1)), (bottom_ref, row_count - 1, (row_count - 2, row_count - 1))):
        for n in range(5):
            for j in range(2 if n < 3 else 1):
                row = pl.ds(rows[j] if n < 3 else near, 1)
                at = pl.ds(2 * n + j if n < 3 else 3 + n, 1)
                out[at, inner] = depth_ref[row, :] if n == 0 else tile_ref[n, row, :]
                out[at, outer] = side_ref[n, row, :]


def face_flux(eta_here, eta_next, bed_here, bed_next, old_flux):
    flow_depth = jnp.maximum(
        jnp.maximum(eta_here, eta_next) - jnp.maximum(bed_here, bed_next), DEPTH_FLOOR
    )
    gradient = (eta_next - eta_here) / CELL_WIDTH
    pushed = old_flux - GRAVITY * TIME_STEP * flow_depth * gradient
    friction = jnp.exp((-7.0 / 3.0) * jnp.log(flow_depth))
    return pushed / (1.0 + GRAVITY * TIME_STEP * MANNING_SQ * jnp.abs(old_flux) * friction)


def flood_kernel(row_count, col_count, *refs):
    closed_ref, tile_ref, depth_ref, side_ref, above_ref, below_ref = refs[:6]
    outs, kept, sems = refs[6:9], refs[9], refs[10]
    at = lax.broadcasted_iota(jnp.int32, (8, 1), 0)
    arrays = []
    for n in range(5):
        own = jnp.concatenate([depth_ref[...] if n == 0 else tile_ref[n], side_ref[n]], 1)
        first_row = 2 * n if n < 3 else 3 + n
        second_row = first_row + 1 if n < 3 else first_row
        halo = jnp.where(at == 0, below_ref[pl.ds(first_row, 1), :], 0.0)
        halo = jnp.where(at == 1, below_ref[pl.ds(second_row, 1), :], halo)
        halo = jnp.where(at == 6, above_ref[pl.ds(first_row, 1), :], halo)
        halo = jnp.where(at == 7, above_ref[pl.ds(second_row, 1), :], halo)
        arrays.append(jnp.concatenate([own, halo], 0))
    depth, bed, first, second, wet = arrays
    shape = depth.shape
    row_at = lax.broadcasted_iota(jnp.int32, shape, 0)
    col_at = lax.broadcasted_iota(jnp.int32, shape, 1)
    first_shut = (row_at == closed_ref[0]) | (row_at == closed_ref[1])
    second_shut = (col_at == closed_ref[2]) | (col_at == closed_ref[3])
    down = lambda x: pltpu.roll(x, shape[0] - 1, 0)
    up = lambda x: pltpu.roll(x, 1, 0)
    onward = lambda x: pltpu.roll(x, shape[1] - 1, 1)
    back = lambda x: pltpu.roll(x, 1, 1)
    bed_down = down(bed)
    bed_onward = onward(bed)
    copies = []

    def finish(n, value):
        kept[n] = value[:row_count, :col_count]
        copies.append(pltpu.make_async_copy(kept.at[n], outs[n], sems.at[n]))
        copies[-1].start()

    for step in range(2):
        eta = bed + depth
        first = jnp.where(first_shut, 0.0, face_flux(eta, down(eta), bed, bed_down, first))
        if step == 1:
            finish(1, first)
        second = jnp.where(second_shut, 0.0, face_flux(eta, onward(eta), bed, bed_onward, second))
        if step == 1:
            finish(2, second)
        depth = depth + wet * (up(first) - first + (back(second) - second))
    finish(0, depth)
    for copy in copies:
        copy.wait()


def exchanged(block, axis, step):
    return lax.ppermute(block, axis, [(i, i ^ (1 << step)) for i in range(lax.axis_size(axis))])


def swapped(first, last, axis, ring):
    count = lax.axis_size(axis)
    odd = lax.axis_index(axis) % 2 == 1
    inner = [(i, i ^ 1) for i in range(count)]
    outer = [] if ring else [(0, 0), (count - 1, count - 1)]
    for i in range(1, count if ring else count - 1, 2):
        outer += [(i, (i + 1) % count), ((i + 1) % count, i)]
    two = lax.ppermute(jnp.where(odd, last, first), axis, outer)
    one = lax.ppermute(jnp.where(odd, first, last), axis, inner)
    return jnp.where(odd, one, two), jnp.where(odd, two, one)


def local(
    river_lower,
    river_main,
    river_upper,
    river_rhs,
    weir_crest,
    weir_regime,
    weir_tile,
    weir_row,
    weir_col,
    bed_level,
    water_depth,
    flux_first,
    flux_second,
    wet_mask,
):
    sections, chains = weir_crest.shape
    row_count, col_count = water_depth.shape
    row_size = lax.axis_size("row")
    col_size = lax.axis_size("col")
    row_at = lax.axis_index("row")
    col_at = lax.axis_index("col")
    tiles = row_size * col_size
    weirs = sections * chains
    capacity = 2 * weirs // tiles
    lane_rows = chains // LANES

    def block_rows(array):
        split = array.reshape(sections, 2, 2, lane_rows, LANES)
        return split.transpose(0, 1, 3, 2, 4).reshape(-1, LANES)

    rhs_rows = river_rhs.reshape(sections, 2, lane_rows, LANES).transpose(0, 2, 1, 3).reshape(-1, LANES)
    rows = weirs // LANES
    high_count = tiles * capacity // LOW
    rows_each = capacity // LANES
    pitch = 3 * rows_each + 2
    river_block = pltpu.VMEM((sections * 4 * lane_rows, LANES), F32)
    blocks = sections // BLOCK
    steps = row_size.bit_length() - 1
    weir_shape = (sections, chains)
    solved, packed, crest, regime, weir_rows, weir_cols = pl.pallas_call(
        functools.partial(solve_kernel, sections),
        out_shape=(
            pltpu.VMEM((sections, 10, lane_rows, LANES), F32),
            pltpu.VMEM((20, lane_rows, LANES), F32),
            pltpu.VMEM(weir_shape, F32),
            pltpu.VMEM(weir_shape, jnp.int32),
            pltpu.VMEM(weir_shape, jnp.int32),
            pltpu.VMEM(weir_shape, jnp.int32),
        ),
        in_specs=[ANY] * 8,
        out_specs=(VMEM,) * 6,
        scratch_shapes=[
            river_block,
            river_block,
            river_block,
            pltpu.VMEM((sections * 2 * lane_rows, LANES), F32),
            pltpu.SemaphoreType.DMA((4, 4)),
            pltpu.SemaphoreType.DMA((4,)),
        ],
        compiler_params=WIDE,
        name="solve",
    )(
        block_rows(river_lower),
        block_rows(river_main),
        block_rows(river_upper),
        rhs_rows,
        weir_crest,
        weir_regime,
        weir_row,
        weir_col,
    )
    places = pl.pallas_call(
        functools.partial(rank_kernel, tiles, capacity, blocks),
        out_shape=(
            jax.ShapeDtypeStruct((rows, LANES), jnp.int32),
            jax.ShapeDtypeStruct((blocks, tiles, LANES), F32),
            jax.ShapeDtypeStruct((1,), jnp.int32),
        ),
        in_specs=[VMEM],
        out_specs=(VMEM, VMEM, SMEM),
        compiler_params=PARAMS,
        cost_estimate=pl.CostEstimate(flops=2 * tiles * weirs * LOW, bytes_accessed=2**17, transcendentals=0),
        name="rank",
    )(weir_tile.reshape(rows, LANES))
    group, known = packed, ()
    for step in range(steps - 1):
        other = exchanged(group, "row", step)
        last = step == steps - 2
        twenty = jax.ShapeDtypeStruct((20, lane_rows, LANES), F32)
        group, own_map = pl.pallas_call(
            functools.partial(merge_kernel, step, step == 0, last),
            out_shape=(jax.ShapeDtypeStruct((6, lane_rows, LANES), F32) if last else twenty, twenty),
            in_specs=[SMEM] + [VMEM] * (2 + len(known)),
            out_specs=(VMEM, VMEM),
            compiler_params=PARAMS,
            name="merge",
        )(row_at.reshape(1), group, other, *known)
        known = (own_map,)
    sent = group
    met = exchanged(sent, "row", steps - 1)
    cells = pl.pallas_call(
        functools.partial(cell_kernel, tiles, capacity, rows // 8, row_count),
        out_shape=jax.ShapeDtypeStruct((2 * high_count, LOW), F32),
        in_specs=[VMEM, VMEM, VMEM, ANY],
        out_specs=VMEM,
        compiler_params=PARAMS,
        cost_estimate=pl.CostEstimate(flops=4 * high_count * LOW * weirs, bytes_accessed=2**18, transcendentals=0),
        name="cells",
    )(places[0], weir_rows, weir_cols, sent)
    state_shape = jax.ShapeDtypeStruct((sections * lane_rows * 2, LANES), F32)
    state_rows, outgoing = pl.pallas_call(
        functools.partial(weir_kernel, sections, steps, tiles, capacity, row_count, col_count),
        out_shape=(state_shape, jax.ShapeDtypeStruct((tiles * pitch, LANES), F32)),
        in_specs=[SMEM] + [VMEM] * 5 + [VMEM, SMEM] + [VMEM] * 5,
        out_specs=(ANY, VMEM),
        scratch_shapes=[
            pltpu.VMEM(state_shape.shape, F32),
            pltpu.VMEM((rows, LANES), F32),
            pltpu.VMEM((2 * high_count, LOW), F32),
            pltpu.VMEM((4 * tiles, LANES), F32),
            pltpu.SemaphoreType.DMA((1,)),
        ],
        compiler_params=PARAMS,
        name="weirs",
    )(row_at.reshape(1), sent, met, own_map, solved, *places, cells, crest, regime, weir_rows, weir_cols)
    river_state = (
        state_rows.reshape(sections, lane_rows, 2, LANES).transpose(0, 2, 1, 3).reshape(sections, 2, chains)
    )
    messages = outgoing.reshape(tiles, pitch, 1, LANES)
    arrived = lax.all_to_all(messages, ("row", "col"), split_axis=0, concat_axis=0, tiled=True)
    tile_stack = jax.ShapeDtypeStruct((5, row_count, col_count), F32)
    side = jax.ShapeDtypeStruct((8, LANES), F32)
    tile, left, right = pl.pallas_call(
        functools.partial(stage_kernel, row_count, col_count),
        out_shape=(tile_stack, side, side),
        in_specs=[ANY] * 6,
        out_specs=(VMEM, VMEM, VMEM),
        scratch_shapes=[pltpu.VMEM((row_count, col_count), jnp.int32), pltpu.SemaphoreType.DMA((5,))],
        compiler_params=PARAMS,
        name="stage",
    )(water_depth, bed_level, flux_first, flux_second, wet_mask, state_rows)
    before, after = swapped(left, right, "col", False)
    tile_out = jax.ShapeDtypeStruct((row_count, col_count), F32)
    edge = jax.ShapeDtypeStruct((8, col_count + LANES), F32)
    flank = jax.ShapeDtypeStruct((5, row_count, LANES), F32)
    wetted, top, bottom, side = pl.pallas_call(
        functools.partial(apply_kernel, tiles, rows_each, row_count, col_count),
        out_shape=(tile_out, edge, edge, flank),
        in_specs=[VMEM] * 4,
        out_specs=(VMEM,) * 4,
        scratch_shapes=[pltpu.VMEM((4 * row_count * col_count // LOW, LOW), F32)],
        compiler_params=PARAMS,
        name="apply",
    )(arrived.reshape(tiles * pitch, LANES), tile, before, after)
    above, below = swapped(top, bottom, "row", True)
    closed = jnp.stack(
        [
            jnp.where(row_at == 0, row_count + 7, -1),
            jnp.where(row_at == row_size - 1, row_count - 1, -1),
            jnp.where(col_at == 0, col_count + LANES - 1, -1),
            jnp.where(col_at == col_size - 1, col_count - 1, -1),
        ]
    ).astype(jnp.int32)
    depth_out, first_out, second_out = pl.pallas_call(
        functools.partial(flood_kernel, row_count, col_count),
        out_shape=(tile_out, tile_out, tile_out),
        in_specs=[SMEM] + [VMEM] * 5,
        out_specs=(ANY, ANY, ANY),
        scratch_shapes=[pltpu.VMEM((3, row_count, col_count), F32), pltpu.SemaphoreType.DMA((3,))],
        compiler_params=PARAMS,
        name="flood",
    )(closed, tile, wetted, side, above, below)
    return (river_state, depth_out, first_out, second_out)


def solution(mesh):
    in_specs = (
        P("row", None, None, "col"),
        P("row", None, None, "col"),
        P("row", None, None, "col"),
        P("row", None, "col"),
        P("row", "col"),
        P("row", "col"),
        P("row", "col", None, None, None),
        P("row", "col"),
        P("row", "col"),
        P("row", "col"),
        P("row", "col"),
        P("row", "col"),
        P("row", "col"),
        P("row", "col"),
    )
    out_specs = (P("row", None, "col"), P("row", "col"), P("row", "col"), P("row", "col"))
    return jax.shard_map(local, mesh=mesh, in_specs=in_specs, out_specs=out_specs, check_vma=False)
```

```python
import functools

import jax
import jax.numpy as jnp
from jax import lax
from jax.experimental import pallas as pl
from jax.experimental.pallas import tpu as pltpu
from jax.sharding import PartitionSpec as P

GRAVITY = 9.81
TIME_STEP = 1.0
CELL_WIDTH = 10.0
MANNING_SQ = 0.0009
DEPTH_FLOOR = 0.05
WEIR_GAIN = 0.5
FREE_COEF = 0.5
SUB_COEF = 0.4
SUB_OFFSET = 0.25
GATE_COEF = 0.2

F32 = jnp.float32
BF16 = jnp.bfloat16
LANES = 128
LOW = 256
BLOCK = 2
VMEM = pl.BlockSpec(memory_space=pltpu.VMEM)
SMEM = pl.BlockSpec(memory_space=pltpu.SMEM)
ANY = pl.BlockSpec(memory_space=pl.ANY)
HBM = pl.BlockSpec(memory_space=pltpu.HBM)
WIDE = pltpu.CompilerParams(vmem_limit_bytes=60 * 2**20)
PARAMS = pltpu.CompilerParams(vmem_limit_bytes=40 * 2**20)


def start_copies(sources, targets, sems):
    copies = [pltpu.make_async_copy(s, t, sems.at[n]) for n, (s, t) in enumerate(zip(sources, targets))]
    for copy in copies:
        copy.start()
    return copies


def mat_mat(a, b):
    return [[a[i][0] * b[0][j] + a[i][1] * b[1][j] for j in range(2)] for i in range(2)]


def mat_vec(a, v):
    return [a[i][0] * v[0] + a[i][1] * v[1] for i in range(2)]


def mat_sub(a, b):
    return [[a[i][j] - b[i][j] for j in range(2)] for i in range(2)]


def mat_neg(a):
    return [[-a[i][j] for j in range(2)] for i in range(2)]


def mat_inv(m):
    scale = 1.0 / (m[0][0] * m[1][1] - m[0][1] * m[1][0])
    return [[m[1][1] * scale, -m[0][1] * scale], [-m[1][0] * scale, m[0][0] * scale]]


def rank_kernel(tiles, capacity, blocks, tile_ref, slot_ref, base_ref, flag_ref):
    table = lax.broadcasted_iota(jnp.int32, (tiles, LANES), 0)
    first_slot = table.astype(F32) * capacity
    row_at = lax.broadcasted_iota(jnp.int32, (LANES, 2 * LANES), 0)
    col_at = lax.broadcasted_iota(jnp.int32, (LANES, 2 * LANES), 1)
    earlier = jnp.where(row_at < col_at, 1.0, 0.0).astype(BF16)

    def body(b, carry):
        offset, most = carry
        base = jnp.floor((offset - first_slot) * (1.0 / LOW))
        base_ref[b] = base
        for n in range(BLOCK):
            g = b * BLOCK + n
            ids = tile_ref[pl.ds((g // 8) * 64 + g % 8, 8, stride=8), :]
            hits = [ids[r : r + 1, :] == table for r in range(8)]
            hot = jnp.concatenate([jnp.where(h, 1.0, 0.0).astype(BF16) for h in hits], 0)
            counts = jnp.dot(hot, earlier, preferred_element_type=F32)
            rows = []
            for r in range(8):
                part = counts[r * tiles : (r + 1) * tiles]
                place = jnp.where(hits[r], part[:, :LANES] + offset, 0.0)
                rows.append(jnp.sum(place, axis=0, keepdims=True))
                offset = offset + part[:, LANES:]
            slot_ref[pl.ds(pl.multiple_of(g * 8, 8), 8), :] = jnp.concatenate(rows, 0).astype(jnp.int32)
        last = jnp.floor((offset - first_slot - 1.0) * (1.0 / LOW)) - base
        return offset, jnp.maximum(most, last)

    most = lax.fori_loop(0, blocks, body, (first_slot, jnp.zeros((tiles, LANES), F32)), unroll=8)[1]
    flag_ref[0] = jnp.max(most).astype(jnp.int32)


def solve_kernel(sections, *refs):
    inputs = refs[:4]
    solved_ref, packed_ref = refs[4:6]
    lower_ref, main_ref, upper_ref, rhs_ref, sems = refs[6:]
    pieces = []
    for n in range(4):
        parts = [[r.at[pl.ds(n * r.shape[0] // 4, r.shape[0] // 4)] for r in group] for group in (inputs, refs[6:10])]
        pieces.append(start_copies(*parts, sems.at[n]))

    def block(ref, k):
        return [[ref[pl.ds(k * 32 + i * 16 + j, 8, stride=2), :] for j in range(2)] for i in range(2)]

    couples = []
    for k in range(sections):
        if k % (sections // 4) == 0:
            for copy in pieces[k // (sections // 4)]:
                copy.wait()
        lower = block(lower_ref, k)
        main = block(main_ref, k)
        upper = block(upper_ref, k)
        right = [rhs_ref[pl.ds(k * 16 + j, 8, stride=2), :] for j in range(2)]
        if k == 0:
            inverse = mat_inv(main)
            left = mat_neg(mat_mat(inverse, lower))
            value = mat_vec(inverse, right)
        else:
            inverse = mat_inv(mat_sub(main, mat_mat(lower, couples[-1])))
            left = mat_neg(mat_mat(inverse, mat_mat(lower, left)))
            moved = mat_vec(lower, value)
            value = mat_vec(inverse, [right[i] - moved[i] for i in range(2)])
        couples.append(mat_mat(inverse, upper))
        for i in range(2):
            solved_ref[k, i] = value[i]
            for j in range(2):
                solved_ref[k, 2 + 2 * i + j] = left[i][j]
    spike = mat_neg(couples[-1])
    tail = (value, left, spike)
    for i in range(2):
        for j in range(2):
            solved_ref[sections - 1, 6 + 2 * i + j] = spike[i][j]
    for k in range(sections - 2, -1, -1):
        couple = couples[k]
        after = mat_vec(couple, value)
        value = [solved_ref[k, i] - after[i] for i in range(2)]
        after = mat_mat(couple, left)
        left = [[solved_ref[k, 2 + 2 * i + j] - after[i][j] for j in range(2)] for i in range(2)]
        spike = mat_neg(mat_mat(couple, spike))
        for i in range(2):
            solved_ref[k, i] = value[i]
            for j in range(2):
                solved_ref[k, 2 + 2 * i + j] = left[i][j]
                solved_ref[k, 6 + 2 * i + j] = spike[i][j]
    for i in range(2):
        packed_ref[i] = value[i]
        packed_ref[2 + i] = tail[0][i]
        for j in range(2):
            packed_ref[4 + 2 * i + j] = left[i][j]
            packed_ref[8 + 2 * i + j] = tail[1][i][j]
            packed_ref[12 + 2 * i + j] = spike[i][j]
            packed_ref[16 + 2 * i + j] = tail[2][i][j]


def load_pair(ref, n):
    return [ref[n], ref[n + 1]]


def load_square(ref, n):
    return [load_pair(ref, n), load_pair(ref, n + 2)]


def store_all(ref, values):
    flat = []
    for value in values:
        flat += [*value[0], *value[1]] if isinstance(value[0], list) else value
    for n, item in enumerate(flat):
        ref[n] = item


def pick(flag, one, other):
    if isinstance(one, list):
        return [pick(flag, a, b) for a, b in zip(one, other)]
    return jnp.where(flag, one, other)


def add(a, b):
    if isinstance(a, list):
        return [add(x, y) for x, y in zip(a, b)]
    return a + b


def meet(head_y, head_left, tail_y, tail_right):
    inner = mat_mat(head_left, tail_right)
    inverse = mat_inv([[1.0 - inner[0][0], -inner[0][1]], [-inner[1][0], 1.0 - inner[1][1]]])
    return inverse, mat_vec(inverse, add(head_y, mat_vec(head_left, tail_y)))


def merge_kernel(step, first, last, position_ref, own_ref, other_ref, *refs):
    known_ref = None if first else refs[0]
    out_ref, map_ref = refs[-2:]
    position = position_ref[0]
    late = ((position >> step) & 1) == 1

    def group(ref):
        return [load_pair(ref, 0), load_pair(ref, 2)] + [load_square(ref, n) for n in (4, 8, 12, 16)]

    own, other = group(own_ref), group(other_ref)
    head_y, tail_y, head_left, tail_left, head_right, tail_right = pick(late, other, own)
    next_head_y, next_tail_y, next_head_left, next_tail_left, next_head_right, next_tail_right = pick(
        late, own, other
    )
    inverse, head = meet(next_head_y, next_head_left, tail_y, tail_right)
    head_before = mat_mat(inverse, mat_mat(next_head_left, tail_left))
    head_after = mat_mat(inverse, next_head_right)
    tail = add(tail_y, mat_vec(tail_right, head))
    tail_before = add(tail_left, mat_mat(tail_right, head_before))
    tail_after = mat_mat(tail_right, head_after)
    joined = [
        add(head_y, mat_vec(head_right, head)),
        add(next_tail_y, mat_vec(next_tail_left, tail)),
        add(head_left, mat_mat(head_right, head_before)),
        mat_mat(next_tail_left, tail_before),
        mat_mat(head_right, head_after),
        add(next_tail_right, mat_mat(next_tail_left, tail_after)),
    ]
    zero = jnp.zeros(tail[0].shape, F32)
    one = zero + 1.0
    unit, none, nothing = [[one, zero], [zero, one]], [[zero, zero], [zero, zero]], [zero, zero]
    if first:
        maps = [
            [pick(late, tail_before, unit), pick(late, tail_after, none), pick(late, tail, nothing)],
            [pick(late, none, head_before), pick(late, unit, head_after), pick(late, nothing, head)],
        ]
    else:
        maps = []
        for n in range(2):
            by_before = load_square(known_ref, 10 * n)
            by_after = load_square(known_ref, 10 * n + 4)
            value = load_pair(known_ref, 10 * n + 8)
            maps.append(
                [
                    pick(late, mat_mat(by_before, tail_before), add(by_before, mat_mat(by_after, head_before))),
                    pick(late, add(by_after, mat_mat(by_before, tail_after)), mat_mat(by_after, head_after)),
                    pick(late, add(value, mat_vec(by_before, tail)), add(value, mat_vec(by_after, head))),
                ]
            )
    store_all(map_ref, maps[0] + maps[1])
    if last:
        later = ((position >> (step + 1)) & 1) == 1
        store_all(out_ref, [pick(later, joined[0], joined[1]), pick(later, joined[2], joined[5])])
    else:
        store_all(out_ref, joined)


def rows16(row):
    return jnp.broadcast_to(row, (16, LANES)).astype(BF16)


def table16(count):
    shape = (count // 16, 16, LANES)
    at = lax.broadcasted_iota(jnp.int32, shape, 0) * 16 + lax.broadcasted_iota(jnp.int32, shape, 1)
    return at.astype(F32).astype(BF16)


def halves(value):
    high = value.astype(BF16).astype(F32)
    return high, value - high


def one_hots(high, low, values, high_table, low_table):
    one = jnp.ones((), BF16)
    zero = jnp.zeros((), BF16)
    left, right = [], []
    for r in range(high.shape[0]):
        hit = high_table == rows16(high[r : r + 1])[None]
        left.append(
            jnp.concatenate(
                [jnp.where(hit, rows16(v[r : r + 1])[None], zero).reshape(-1, LANES) for v in values], 0
            )
        )
        hit = low_table == rows16(low[r : r + 1])[None]
        right.append(jnp.where(hit, one, zero).reshape(-1, LANES))
    return jnp.concatenate(left, 1), jnp.concatenate(right, 1)


def product(left, right):
    return lax.dot_general(left, right, (((1,), (1,)), ((), ())), preferred_element_type=F32)


def group_at(g):
    over = pl.multiple_of((g // 8) * 8, 8)
    along = pl.multiple_of((g % 8) * LANES, LANES)
    return (pl.ds(over, 8), pl.ds(along, LANES))


def fill_slots(tiles, capacity, blocks, slot_ref, base_ref, flag_ref, values, total_ref, side_code, side_ref):
    windows = capacity // LOW
    taken = min(2, windows)
    low_table = table16(LOW)
    side_table = table16(LANES)
    first_window = lax.broadcasted_iota(jnp.int32, (tiles, LANES), 0).astype(F32) * windows
    one = jnp.ones((), BF16)
    zero = jnp.zeros((), BF16)
    total_ref[...] = jnp.zeros_like(total_ref)
    side_ref[...] = jnp.zeros_like(side_ref)

    def add_block(b, first):
        rows = pl.ds(pl.multiple_of(b * (8 * BLOCK), 8 * BLOCK), 8 * BLOCK)
        slot = slot_ref[rows, :]
        window = (slot // LOW).astype(F32)
        low = (slot % LOW).astype(F32)
        place = jnp.concatenate([side_code(b * BLOCK + n) for n in range(BLOCK)], 0).astype(F32)
        groups = [values(b * BLOCK + n) for n in range(BLOCK)]
        value = [jnp.concatenate([g[v] for g in groups], 0) for v in range(len(groups[0]))]
        base = base_ref[b] + first
        covered = [jnp.where(base + i < windows, first_window + (base + i), -1.0) for i in range(taken)]
        window_table = jnp.concatenate(covered, 0).astype(BF16).reshape(taken * tiles // 16, 16, LANES)
        left, right, side_left, side_right = [], [], [], []
        for r in range(8 * BLOCK):
            hit = window_table == rows16(window[r : r + 1])[None]
            parts = [jnp.where(hit, rows16(v[r : r + 1])[None], zero).reshape(-1, LANES) for v in value]
            left.append(jnp.concatenate(parts, 0))
            if taken == 2:
                parts = [p[:tiles] + p[tiles:] for p in parts]
            side_left.append(jnp.concatenate(parts, 0))
            hit = low_table == rows16(low[r : r + 1])[None]
            right.append(jnp.where(hit, one, zero).reshape(-1, LANES))
            hit = side_table == rows16(place[r : r + 1])[None]
            side_right.append(jnp.where(hit, one, zero).reshape(-1, LANES))
        found = product(jnp.concatenate(left, 1), jnp.concatenate(right, 1))
        base = jnp.concatenate([base, base], 1)
        for v in range(len(value) // 2):
            parts = []
            for i in range(taken):
                high, rest = (((2 * v + n) * taken + i) * tiles for n in range(2))
                parts.append(found[high : high + tiles] + found[rest : rest + tiles])
            for q in range(windows):
                put = jnp.where(base == q, parts[0], 0.0)
                for i in range(1, taken):
                    put = jnp.where(base == q - i, parts[i], put)
                total_ref[pl.ds((v * windows + q) * tiles, tiles), :] += put
        side_ref[...] += product(jnp.concatenate(side_left, 1), jnp.concatenate(side_right, 1))

    def body(b, carry):
        add_block(b, 0)
        return carry

    lax.fori_loop(0, blocks, body, 0, unroll=4)
    for first in range(taken, windows, taken):

        @pl.when(flag_ref[0] >= first)
        def _(first=first):
            def rest(b, carry):
                add_block(b, first)
                return carry

            lax.fori_loop(0, blocks, rest, 0)


def store_slots(capacity, first, count, window_of, out_ref, pitch, row):
    windows = capacity // LOW
    for q in range(windows):
        value = window_of(q)
        for j in range(LOW // LANES):
            at = pl.ds(first * pitch + row + j * windows + q, count, stride=pitch)
            out_ref[at, :] = value[:, j * LANES : (j + 1) * LANES]


def cell_kernel(tiles, capacity, groups, row_count, *refs):
    slot_ref, row_ref, col_ref, _, out_ref = refs
    high_table = table16(tiles * capacity // LOW)
    low_table = table16(LOW)
    out_ref[...] = jnp.zeros_like(out_ref)

    def body(g, carry):
        slot = slot_ref[pl.ds(pl.multiple_of(g * 8, 8), 8), :]
        col = col_ref[group_at(g)]
        high = (col // LOW) * row_count + row_ref[group_at(g)]
        left, right = one_hots(
            (slot % capacity // LOW * tiles + slot // capacity).astype(F32),
            (slot % LOW).astype(F32),
            [high.astype(F32), (col % LOW).astype(F32)],
            high_table,
            low_table,
        )
        out_ref[...] += product(left, right)
        return carry

    lax.fori_loop(0, groups, body, 0, unroll=16)


def weir_kernel(sections, steps, tiles, capacity, row_count, col_count, *refs):
    position_ref, own_ref, other_ref, map_ref = refs[:4]
    solved_ref, slot_ref, base_ref, flag_ref, cells_ref = refs[4:9]
    crest_ref, regime_ref, row_ref, col_ref = refs[9:13]
    state_out, out_ref, state_ref, phase_ref, total_ref, side_ref, message_ref, sems = refs[13:]
    late = ((position_ref[0] >> (steps - 1)) & 1) == 1
    own = [load_pair(own_ref, 0), load_square(own_ref, 2)]
    other = [load_pair(other_ref, 0), load_square(other_ref, 2)]
    tail_y, tail_right = pick(late, other, own)
    head_y, head_left = pick(late, own, other)
    head = meet(head_y, head_left, tail_y, tail_right)[1]
    tail = add(tail_y, mat_vec(tail_right, head))
    zero = jnp.zeros(tail[0].shape, F32)
    outer_before = pick(late, tail, [zero, zero])
    outer_after = pick(late, [zero, zero], head)
    before, after = (
        add(
            load_pair(map_ref, n + 8),
            add(
                mat_vec(load_square(map_ref, n), outer_before),
                mat_vec(load_square(map_ref, n + 4), outer_after),
            ),
        )
        for n in (0, 10)
    )
    for k in range(sections):
        for i in range(2):
            state = solved_ref[k, i]
            for j in range(2):
                state = state + solved_ref[k, 2 + 2 * i + j] * before[j]
                state = state + solved_ref[k, 6 + 2 * i + j] * after[j]
            state_ref[pl.ds(k * 16 + i, 8, stride=2), :] = state
            if i == 0:
                phase_ref[pl.ds((k // 8) * 64 + k % 8, 8, stride=8), :] = state

    state_copy = pltpu.make_async_copy(state_ref, state_out, sems.at[0])
    state_copy.start()

    def values(g):
        phase = phase_ref[pl.ds(pl.multiple_of(g * 8, 8), 8), :]
        regime = regime_ref[group_at(g)]
        head = jnp.maximum(phase - crest_ref[group_at(g)], 0.0)
        free = jnp.where(regime == 0, FREE_COEF * head * jnp.sqrt(head), 0.0)
        sub = jnp.where(
            regime == 1,
            SUB_COEF * jnp.sqrt(head + SUB_OFFSET),
            jnp.where(regime == 2, GATE_COEF, 0.0),
        )
        return [*halves(WEIR_GAIN * (free + sub * phase)), *halves(WEIR_GAIN * sub)]

    def side_code(g):
        col = col_ref[group_at(g)]
        place = jnp.where(col < 2, col, jnp.where(col >= col_count - 2, col - (col_count - 4), -1))
        return jnp.where(place >= 0, place * row_count + row_ref[group_at(g)], -1)

    blocks = sections // BLOCK
    fill_slots(tiles, capacity, blocks, slot_ref, base_ref, flag_ref, values, total_ref, side_code, side_ref)
    windows = capacity // LOW
    rows_each = capacity // LANES
    pitch = 3 * rows_each + 2
    at = lax.broadcasted_iota(jnp.int32, (tiles, LANES), 1)
    first_cols = at < 2 * row_count
    beside = []
    for v in range(2):
        sums = side_ref[pl.ds(2 * v * tiles, tiles), :] + side_ref[pl.ds((2 * v + 1) * tiles, tiles), :]
        beside.append(jnp.where(first_cols, pltpu.roll(sums, tiles - 1, 0), pltpu.roll(sums, 1, 0)))
    count = tiles // 4
    copies = []
    for first in range(0, tiles, count):
        for v in range(2):
            window_of = lambda q: total_ref[pl.ds((v * windows + q) * tiles + first, count), :]
            store_slots(capacity, first, count, window_of, message_ref, pitch, v * rows_each)
            at = pl.ds(first * pitch + 3 * rows_each + v, count, stride=pitch)
            message_ref[at, :] = beside[v][first : first + count]
        cell_part = lambda n, q: cells_ref[pl.ds((n * windows + q) * tiles + first, count), :]
        window_of = lambda q: cell_part(0, q) * float(LOW) + cell_part(1, q)
        store_slots(capacity, first, count, window_of, message_ref, pitch, 2 * rows_each)
        rows = pl.ds(first * pitch, count * pitch)
        copies.append(pltpu.make_async_copy(message_ref.at[rows], out_ref.at[rows], sems.at[1 + len(copies)]))
        copies[-1].start()
    for copy in copies:
        copy.wait()
    state_copy.wait()


def side_lanes(n):
    at = lax.broadcasted_iota(jnp.int32, (8, LANES), 1)
    return (at == 2 * n) | (at == 2 * n + 1)


def stage_kernel(row_count, col_count, *refs):
    tile_ref, left_ref, right_ref, wet_ref, sems = refs[6:]
    for copy in start_copies(refs[:5], [tile_ref.at[n] for n in range(4)] + [wet_ref], sems):
        copy.wait()
    tile_ref[4] = wet_ref[...].astype(F32) * (TIME_STEP / CELL_WIDTH)
    left = jnp.zeros(left_ref.shape, F32)
    right = left
    for t in range(row_count // 8):
        for n in range(5):
            at = 5 * t + n
            first = tile_ref[n, pl.ds(8 * t, 8), pl.ds(0, LANES)]
            last = tile_ref[n, pl.ds(8 * t, 8), pl.ds(col_count - LANES, LANES)]
            left = jnp.where(side_lanes(at), pltpu.roll(first, 2 * at, 1), left)
            right = jnp.where(side_lanes(at), pltpu.roll(last, 2 * at + 2, 1), right)
    left_ref[...] = left
    right_ref[...] = right


def unpacked(strip, n, rows, lane):
    parts = [pltpu.roll(strip, (lane - 2 * (5 * t + n)) % LANES, 1) for t in range(rows // 8)]
    return jnp.concatenate(parts, 0)


def apply_kernel(sources, rows_each, row_count, col_count, *refs):
    in_ref, tile_ref, before_ref, after_ref = refs[:4]
    depth_ref, top_ref, bottom_ref, side_ref, total_ref = refs[4:]
    pitch = 3 * rows_each + 2
    high_count = row_count * col_count // LOW
    high_table = table16(high_count)
    low_table = table16(LOW)
    total_ref[...] = jnp.zeros_like(total_ref)
    step = 8 // rows_each if rows_each < 8 else 1

    def body(g, carry):
        def part(v):
            return jnp.concatenate(
                [in_ref[pl.ds((g * step + n) * pitch + v * rows_each, rows_each), :] for n in range(step)], 0
            )

        cell = part(2).astype(jnp.int32)
        left, right = one_hots(
            (cell // LOW).astype(F32),
            (cell % LOW).astype(F32),
            [*halves(part(0)), *halves(part(1))],
            high_table,
            low_table,
        )
        total_ref[...] += product(left, right)
        return carry

    lax.fori_loop(0, sources // step, body, 0, unroll=32)
    for n in range(col_count // LOW):
        def summed(v):
            start = 2 * v * high_count + n * row_count
            return total_ref[pl.ds(start, row_count), :] + total_ref[pl.ds(start + high_count, row_count), :]

        cols = pl.ds(n * LOW, LOW)
        depth = tile_ref[0, :, cols]
        surface = tile_ref[1, :, cols] + depth
        depth_ref[:, cols] = jnp.maximum(depth + (summed(0) - summed(1) * surface), 0.0)
    row_at = lax.broadcasted_iota(jnp.int32, (row_count, LANES), 0)
    col_at = lax.broadcasted_iota(jnp.int32, (row_count, LANES), 1)

    def columns(v):
        sums = jnp.sum(in_ref[pl.ds(3 * rows_each + v, sources, stride=pitch), :], axis=0, keepdims=True)
        result = jnp.zeros((row_count, LANES), F32)
        for place, lane in enumerate((0, 1, LANES - 2, LANES - 1)):
            wanted = col_at == place * row_count + row_at
            column = jnp.sum(jnp.where(wanted, sums, 0.0), axis=1, keepdims=True)
            result = jnp.where(col_at == lane, column, result)
        return result

    before, after = before_ref[...], after_ref[...]
    for n in range(5):
        right = unpacked(after, n, row_count, 0)
        left = unpacked(before, n, row_count, LANES - 2)
        side_ref[n] = jnp.where(col_at < LANES // 2, right, left)
    depth = side_ref[0]
    surface = side_ref[1] + depth
    side_ref[0] = jnp.maximum(depth + (columns(0) - columns(1) * surface), 0.0)
    inner, outer = pl.ds(0, col_count), pl.ds(col_count, LANES)
    for out, near, rows in ((top_ref, 0, (0, 1)), (bottom_ref, row_count - 1, (row_count - 2, row_count - 1))):
        for n in range(5):
            for j in range(2 if n < 3 else 1):
                row = pl.ds(rows[j] if n < 3 else near, 1)
                at = pl.ds(2 * n + j if n < 3 else 3 + n, 1)
                out[at, inner] = depth_ref[row, :] if n == 0 else tile_ref[n, row, :]
                out[at, outer] = side_ref[n, row, :]


def face_flux(eta_here, eta_next, bed_here, bed_next, old_flux):
    flow_depth = jnp.maximum(
        jnp.maximum(eta_here, eta_next) - jnp.maximum(bed_here, bed_next), DEPTH_FLOOR
    )
    gradient = (eta_next - eta_here) / CELL_WIDTH
    pushed = old_flux - GRAVITY * TIME_STEP * flow_depth * gradient
    friction = jnp.exp((-7.0 / 3.0) * jnp.log(flow_depth))
    return pushed / (1.0 + GRAVITY * TIME_STEP * MANNING_SQ * jnp.abs(old_flux) * friction)


def flood_kernel(row_count, col_count, *refs):
    closed_ref, tile_ref, depth_ref, side_ref, above_ref, below_ref = refs[:6]
    outs, kept, sems = refs[6:9], refs[9], refs[10]
    at = lax.broadcasted_iota(jnp.int32, (8, 1), 0)
    arrays = []
    for n in range(5):
        own = jnp.concatenate([depth_ref[...] if n == 0 else tile_ref[n], side_ref[n]], 1)
        first_row = 2 * n if n < 3 else 3 + n
        second_row = first_row + 1 if n < 3 else first_row
        halo = jnp.where(at == 0, below_ref[pl.ds(first_row, 1), :], 0.0)
        halo = jnp.where(at == 1, below_ref[pl.ds(second_row, 1), :], halo)
        halo = jnp.where(at == 6, above_ref[pl.ds(first_row, 1), :], halo)
        halo = jnp.where(at == 7, above_ref[pl.ds(second_row, 1), :], halo)
        arrays.append(jnp.concatenate([own, halo], 0))
    depth, bed, first, second, wet = arrays
    shape = depth.shape
    row_at = lax.broadcasted_iota(jnp.int32, shape, 0)
    col_at = lax.broadcasted_iota(jnp.int32, shape, 1)
    first_shut = (row_at == closed_ref[0]) | (row_at == closed_ref[1])
    second_shut = (col_at == closed_ref[2]) | (col_at == closed_ref[3])
    down = lambda x: pltpu.roll(x, shape[0] - 1, 0)
    up = lambda x: pltpu.roll(x, 1, 0)
    onward = lambda x: pltpu.roll(x, shape[1] - 1, 1)
    back = lambda x: pltpu.roll(x, 1, 1)
    bed_down = down(bed)
    bed_onward = onward(bed)
    copies = []

    def finish(n, value):
        kept[n] = value[:row_count, :col_count]
        copies.append(pltpu.make_async_copy(kept.at[n], outs[n], sems.at[n]))
        copies[-1].start()

    for step in range(2):
        eta = bed + depth
        first = jnp.where(first_shut, 0.0, face_flux(eta, down(eta), bed, bed_down, first))
        if step == 1:
            finish(1, first)
        second = jnp.where(second_shut, 0.0, face_flux(eta, onward(eta), bed, bed_onward, second))
        if step == 1:
            finish(2, second)
        depth = depth + wet * (up(first) - first + (back(second) - second))
    finish(0, depth)
    for copy in copies:
        copy.wait()


def exchanged(block, axis, step):
    return lax.ppermute(block, axis, [(i, i ^ (1 << step)) for i in range(lax.axis_size(axis))])


def swapped(first, last, axis, ring):
    count = lax.axis_size(axis)
    odd = lax.axis_index(axis) % 2 == 1
    inner = [(i, i ^ 1) for i in range(count)]
    outer = [] if ring else [(0, 0), (count - 1, count - 1)]
    for i in range(1, count if ring else count - 1, 2):
        outer += [(i, (i + 1) % count), ((i + 1) % count, i)]
    two = lax.ppermute(jnp.where(odd, last, first), axis, outer)
    one = lax.ppermute(jnp.where(odd, first, last), axis, inner)
    return jnp.where(odd, one, two), jnp.where(odd, two, one)


def local(
    river_lower,
    river_main,
    river_upper,
    river_rhs,
    weir_crest,
    weir_regime,
    weir_tile,
    weir_row,
    weir_col,
    bed_level,
    water_depth,
    flux_first,
    flux_second,
    wet_mask,
):
    sections, chains = weir_crest.shape
    row_count, col_count = water_depth.shape
    row_size = lax.axis_size("row")
    col_size = lax.axis_size("col")
    row_at = lax.axis_index("row")
    col_at = lax.axis_index("col")
    tiles = row_size * col_size
    weirs = sections * chains
    capacity = 2 * weirs // tiles
    lane_rows = chains // LANES

    def block_rows(array):
        split = array.reshape(sections, 2, 2, lane_rows, LANES)
        return split.transpose(0, 1, 3, 2, 4).reshape(-1, LANES)

    rhs_rows = river_rhs.reshape(sections, 2, lane_rows, LANES).transpose(0, 2, 1, 3).reshape(-1, LANES)
    rows = weirs // LANES
    high_count = tiles * capacity // LOW
    rows_each = capacity // LANES
    pitch = 3 * rows_each + 2
    river_block = pltpu.VMEM((sections * 4 * lane_rows, LANES), F32)
    blocks = sections // BLOCK
    steps = row_size.bit_length() - 1
    solved, packed = pl.pallas_call(
        functools.partial(solve_kernel, sections),
        out_shape=(
            pltpu.VMEM((sections, 10, lane_rows, LANES), F32),
            pltpu.VMEM((20, lane_rows, LANES), F32),
        ),
        in_specs=[ANY] * 4,
        out_specs=(VMEM,) * 2,
        scratch_shapes=[
            river_block,
            river_block,
            river_block,
            pltpu.VMEM((sections * 2 * lane_rows, LANES), F32),
            pltpu.SemaphoreType.DMA((4, 4)),
        ],
        compiler_params=WIDE,
        name="solve",
    )(
        block_rows(river_lower),
        block_rows(river_main),
        block_rows(river_upper),
        rhs_rows,
    )
    places = pl.pallas_call(
        functools.partial(rank_kernel, tiles, capacity, blocks),
        out_shape=(
            jax.ShapeDtypeStruct((rows, LANES), jnp.int32),
            jax.ShapeDtypeStruct((blocks, tiles, LANES), F32),
            jax.ShapeDtypeStruct((1,), jnp.int32),
        ),
        in_specs=[VMEM],
        out_specs=(VMEM, VMEM, SMEM),
        compiler_params=PARAMS,
        cost_estimate=pl.CostEstimate(flops=2 * tiles * weirs * LOW, bytes_accessed=2**17, transcendentals=0),
        name="rank",
    )(weir_tile.reshape(rows, LANES))
    group, known = packed, ()
    for step in range(steps - 1):
        other = exchanged(group, "row", step)
        last = step == steps - 2
        twenty = jax.ShapeDtypeStruct((20, lane_rows, LANES), F32)
        group, own_map = pl.pallas_call(
            functools.partial(merge_kernel, step, step == 0, last),
            out_shape=(jax.ShapeDtypeStruct((6, lane_rows, LANES), F32) if last else twenty, twenty),
            in_specs=[SMEM] + [VMEM] * (2 + len(known)),
            out_specs=(VMEM, VMEM),
            compiler_params=PARAMS,
            name="merge",
        )(row_at.reshape(1), group, other, *known)
        known = (own_map,)
    sent = group
    met = exchanged(sent, "row", steps - 1)
    cells = pl.pallas_call(
        functools.partial(cell_kernel, tiles, capacity, rows // 8, row_count),
        out_shape=jax.ShapeDtypeStruct((2 * high_count, LOW), F32),
        in_specs=[VMEM, VMEM, VMEM, ANY],
        out_specs=VMEM,
        compiler_params=PARAMS,
        cost_estimate=pl.CostEstimate(flops=4 * high_count * LOW * weirs, bytes_accessed=2**18, transcendentals=0),
        name="cells",
    )(places[0], weir_row, weir_col, sent)
    state_shape = jax.ShapeDtypeStruct((sections * lane_rows * 2, LANES), F32)
    state_rows, outgoing = pl.pallas_call(
        functools.partial(weir_kernel, sections, steps, tiles, capacity, row_count, col_count),
        out_shape=(state_shape, jax.ShapeDtypeStruct((tiles * pitch, LANES), F32)),
        in_specs=[SMEM] + [VMEM] * 5 + [VMEM, SMEM] + [VMEM] * 5,
        out_specs=(ANY, ANY),
        scratch_shapes=[
            pltpu.VMEM(state_shape.shape, F32),
            pltpu.VMEM((rows, LANES), F32),
            pltpu.VMEM((2 * high_count, LOW), F32),
            pltpu.VMEM((4 * tiles, LANES), F32),
            pltpu.VMEM((tiles * pitch, LANES), F32),
            pltpu.SemaphoreType.DMA((5,)),
        ],
        compiler_params=PARAMS,
        name="weirs",
    )(row_at.reshape(1), sent, met, own_map, solved, *places, cells, weir_crest, weir_regime, weir_row, weir_col)
    river_state = (
        state_rows.reshape(sections, lane_rows, 2, LANES).transpose(0, 2, 1, 3).reshape(sections, 2, chains)
    )
    messages = outgoing.reshape(tiles, pitch, 1, LANES)
    arrived = lax.all_to_all(messages, ("row", "col"), split_axis=0, concat_axis=0, tiled=True)
    tile_stack = jax.ShapeDtypeStruct((5, row_count, col_count), F32)
    side = jax.ShapeDtypeStruct((8, LANES), F32)
    tile, left, right = pl.pallas_call(
        functools.partial(stage_kernel, row_count, col_count),
        out_shape=(tile_stack, side, side),
        in_specs=[ANY] * 6,
        out_specs=(VMEM, VMEM, VMEM),
        scratch_shapes=[pltpu.VMEM((row_count, col_count), jnp.int32), pltpu.SemaphoreType.DMA((5,))],
        compiler_params=PARAMS,
        name="stage",
    )(water_depth, bed_level, flux_first, flux_second, wet_mask, state_rows)
    before, after = swapped(left, right, "col", False)
    tile_out = jax.ShapeDtypeStruct((row_count, col_count), F32)
    edge = jax.ShapeDtypeStruct((8, col_count + LANES), F32)
    flank = jax.ShapeDtypeStruct((5, row_count, LANES), F32)
    wetted, top, bottom, side = pl.pallas_call(
        functools.partial(apply_kernel, tiles, rows_each, row_count, col_count),
        out_shape=(tile_out, edge, edge, flank),
        in_specs=[VMEM] * 4,
        out_specs=(VMEM,) * 4,
        scratch_shapes=[pltpu.VMEM((4 * row_count * col_count // LOW, LOW), F32)],
        compiler_params=PARAMS,
        name="apply",
    )(arrived.reshape(tiles * pitch, LANES), tile, before, after)
    above, below = swapped(top, bottom, "row", True)
    closed = jnp.stack(
        [
            jnp.where(row_at == 0, row_count + 7, -1),
            jnp.where(row_at == row_size - 1, row_count - 1, -1),
            jnp.where(col_at == 0, col_count + LANES - 1, -1),
            jnp.where(col_at == col_size - 1, col_count - 1, -1),
        ]
    ).astype(jnp.int32)
    depth_out, first_out, second_out = pl.pallas_call(
        functools.partial(flood_kernel, row_count, col_count),
        out_shape=(tile_out, tile_out, tile_out),
        in_specs=[SMEM] + [VMEM] * 5,
        out_specs=(ANY, ANY, ANY),
        scratch_shapes=[pltpu.VMEM((3, row_count, col_count), F32), pltpu.SemaphoreType.DMA((3,))],
        compiler_params=PARAMS,
        name="flood",
    )(closed, tile, wetted, side, above, below)
    return (river_state, depth_out, first_out, second_out)


def solution(mesh):
    in_specs = (
        P("row", None, None, "col"),
        P("row", None, None, "col"),
        P("row", None, None, "col"),
        P("row", None, "col"),
        P("row", "col"),
        P("row", "col"),
        P("row", "col", None, None, None),
        P("row", "col"),
        P("row", "col"),
        P("row", "col"),
        P("row", "col"),
        P("row", "col"),
        P("row", "col"),
        P("row", "col"),
    )
    out_specs = (P("row", None, "col"), P("row", "col"), P("row", "col"), P("row", "col"))
    return jax.shard_map(local, mesh=mesh, in_specs=in_specs, out_specs=out_specs, check_vma=False)
```
